128 devices in a mesh: cat: 32 (over y, z, core), tp: 4 (over x).
Axes of the slice: x: 4, y: 4, z: 4, core: 2. Of those that a mesh axis runs over, the one named last changes fastest.
Arguments:
- query_emb: bfloat16 [32768, 512], P('cat', 'tp'), may hold values from -100 to 100
- positive_emb: bfloat16 [32768, 512], P('cat', 'tp'), may hold values from -6 to 6
- item_hidden: bfloat16 [65536, 1024], P('cat', 'tp'), may hold values from -6 to 6
- item_weight: bfloat16 [1024, 512], P('tp'), may hold values from -0.1875 to 0.1875
- neg_blocks: int32 [128, 64], P('cat'), may hold values from 0 to 255, all different within a row
- block_home: int32 [256], replicated, may hold values from 0 to 255, each once
- sample_counts: int32 [65536], replicated, may hold values from 1 to 4096
Outputs:
- query_loss: float32 [32768], P('cat')
- query_grad: bfloat16 [32768, 512], P('cat', 'tp')
The draws below stay inside these ranges and needn't reach their ends.
Inputs may be any that keep to these rules, and one draw needn't show every extreme that they name: `neg_blocks`: each row names 64 different catalog blocks. `block_home`: each storage position once.
All inputs are finite; a program needn't handle non-finite values.
Results may differ from the reference program's by a relative error of at most 0.012.
Values may be sent and summed in bfloat16 or wider, within the bound.
No kernel may reach another device: no remote copies, remote signals or barrier semaphores. Data moves between devices by JAX's collectives and lax.ppermute only.
A program may use at most 192 MiB of HBM per device.

```python
import math
import jax
import jax.numpy as jnp
from jax import lax

E = 512
HID = 1024
BLK = 256
NNEG = 64
QBLOCKS = 128
QUERIES = 32768
NB = 256
ITEMS = 65536


def draw_query_emb(key, part):
    key = jax.random.fold_in(key, 11)
    key_base, key_scale = jax.random.split(key, 2)
    base_vals = jnp.clip(jax.random.normal(key_base, (QUERIES, E), jnp.float32), -4.0, 4.0)
    row_scale = jnp.exp(jax.random.uniform(key_scale, (QUERIES, 1), jnp.float32, -0.7, 1.1))
    return jnp.clip(base_vals * row_scale, -100.0, 100.0).astype(jnp.bfloat16)


def with_ends(entries, own_key, smallest, largest):
    index_at = [jax.random.randint(jax.random.fold_in(own_key, axis), (), 0, length) for axis, length in enumerate(entries.shape)]
    main_axis = entries.shape.index(max(entries.shape))
    beside = index_at[:main_axis] + [(index_at[main_axis] + 1) % entries.shape[main_axis]] + index_at[main_axis + 1:]
    return entries.at[tuple(index_at)].set(smallest).at[tuple(beside)].set(largest)


def steps_of(own_key, dims, cuts, least, top_value):
    loudness = 1.0
    for axis_at, parts in cuts:
        heights = jax.random.uniform(jax.random.fold_in(jax.random.fold_in(own_key, 6), axis_at), (parts,), jnp.float32, least / len(cuts), top_value / len(cuts))
        loudness = loudness * jnp.repeat(jnp.exp(heights), dims[axis_at] // parts).reshape((-1,) + (1,) * (len(dims) - 1 - axis_at))
    return loudness


def distinct(own_key, rows, count, top, lift):
    ranking = jax.random.permutation(jax.random.fold_in(own_key, 1), count)
    boost = ranking
    for power in range(3):
        boost = boost * boost // count
    boost = boost * lift // count
    tickets = jax.random.randint(jax.random.fold_in(own_key, 2), (rows, count), 0, 4096) + boost
    sure = jax.random.permutation(jax.random.fold_in(own_key, 3), rows)[jnp.arange(count) % rows]
    tickets = jnp.where(jnp.arange(rows)[:, None] == sure[None, :], 1 << 14, tickets)
    priority = tickets * count + jnp.arange(count)
    return lax.top_k(priority.astype(jnp.int32), top)[1].astype(jnp.int32)


def bell_draw(key, dims, width, bound, cuts=(), dtype=jnp.bfloat16):
    level = steps_of(key, dims, cuts, -0.22, 0.18) if cuts else 1.0
    entries = jax.random.normal(key, dims, jnp.float32) * width * level
    return jnp.minimum(jnp.maximum(entries, -bound), bound).astype(dtype)


def setup_inputs(seed: int = 0) -> dict:
    splits = jax.random.split(jax.random.key(seed), 8)
    return {
        "query_emb": draw_query_emb(jax.random.fold_in(splits[7], 71), 0),
        "positive_emb": bell_draw(splits[1], (QUERIES, E), 1.0, 6.0, ((0, 32), (1, 4))),
        "item_hidden": bell_draw(splits[2], (ITEMS, HID), 1.0, 6.0, ((0, 32), (1, 4))),
        "item_weight": bell_draw(splits[3], (HID, E), HID ** -0.5, 0.1875, ((0, 4),)),
        "neg_blocks": distinct(splits[4], QBLOCKS, NB, NNEG, 4096),
        "block_home": jax.random.permutation(splits[5], NB).astype(jnp.int32),
        "sample_counts": with_ends(jax.random.randint(splits[6], (ITEMS,), 1, 4097), jax.random.fold_in(splits[6], 1), 1, 4096).astype(jnp.int32),
    }


def reference(query_emb, positive_emb, item_hidden, item_weight, neg_blocks, block_home, sample_counts):
    score_scale = 2.0 / math.sqrt(E)
    item_vec = jnp.dot(item_hidden, item_weight, preferred_element_type=jnp.float32).astype(jnp.bfloat16)
    log_q = jnp.log(sample_counts.astype(jnp.float32))
    vec_blocks = item_vec.reshape(NB, BLK, E)
    logq_blocks = log_q.reshape(NB, BLK)
    home_ids = block_home[neg_blocks].astype(jnp.int32)
    query_blocks = query_emb.reshape(QBLOCKS, BLK, E)
    positive_blocks = positive_emb.reshape(QBLOCKS, BLK, E)

    def one_block(inputs):
        query_block, positive_block, block_ids = inputs
        picked = vec_blocks[block_ids].reshape(NNEG * BLK, E)
        picked_q = logq_blocks[block_ids].reshape(NNEG * BLK)
        scores = score_scale * jnp.dot(query_block, picked.T, preferred_element_type=jnp.float32) - picked_q[None, :]
        pos_score = score_scale * lax.optimization_barrier(jnp.sum(query_block.astype(jnp.float32) * positive_block.astype(jnp.float32), axis=1))
        run_max = jnp.maximum(lax.optimization_barrier(jnp.max(scores, axis=1)), pos_score)
        run_sum = lax.optimization_barrier(jnp.sum(jnp.exp(scores - run_max[:, None]), axis=1)) + jnp.exp(pos_score - run_max)
        log_total = run_max + jnp.log(run_sum)
        weights = jnp.exp(scores - log_total[:, None]).astype(jnp.bfloat16)
        weighted = jnp.dot(weights, picked, preferred_element_type=jnp.float32)
        pos_weight = jnp.exp(pos_score - log_total)
        query_grad = score_scale * (weighted + (pos_weight - 1.0)[:, None] * positive_block.astype(jnp.float32))
        return (log_total - pos_score, query_grad.astype(jnp.bfloat16))
    query_loss, query_grad = lax.map(one_block, (query_blocks, positive_blocks, home_ids))
    return (query_loss.reshape(QUERIES), query_grad.reshape(QUERIES, E))
```

```python
import functools
import math

import jax
import jax.numpy as jnp
from jax import lax
from jax.experimental import pallas as pl
from jax.experimental.pallas import tpu as pltpu
from jax.sharding import PartitionSpec as P

BLK = 256
TP = 4
NY = 4
NZ = 4
E = 512
LOG2E = math.log2(math.e)
LN2 = math.log(2.0)
SCALE = 2.0 / math.sqrt(E)
LOW = -1e30
ROWS = BLK // TP // 2
NBD = 8
PICKS = 64
COLS = PICKS * ROWS
TILE = 512


def cat_perm(dy, dz, dc):
    def at(y, z, c):
        return ((y % NY) * NZ + z % NZ) * 2 + c % 2

    return [
        (at(y, z, c), at(y + dy, z + dz, c + dc))
        for y in range(NY)
        for z in range(NZ)
        for c in range(2)
    ]


def send(value, dy=0, dz=0, dc=0):
    return lax.ppermute(value, "cat", cat_perm(dy, dz, dc))


def send_x(value, d):
    return lax.ppermute(value, "tp", [(i, (i + d) % TP) for i in range(TP)])


def tower_kernel(core_ref, *refs):
    hidden = refs[0:4]
    weight = refs[4:8]
    keep_ref, give_ref, scratch = refs[8:]
    acc = jnp.dot(hidden[0][...], weight[0][...], preferred_element_type=jnp.float32)
    for d in range(1, 4):
        acc += jnp.dot(hidden[d][...], weight[d][...], preferred_element_type=jnp.float32)
    scratch[...] = acc.astype(jnp.bfloat16).reshape(scratch.shape)
    core = core_ref[0]
    keep_ref[...] = scratch[:, core]
    give_ref[...] = scratch[:, 1 - core]


def tower(core, hidden, weight):
    half = jax.ShapeDtypeStruct((NBD, ROWS, E), jnp.bfloat16)
    return pl.pallas_call(
        tower_kernel,
        out_shape=(half, half),
        in_specs=[pl.BlockSpec(memory_space=pltpu.SMEM)]
        + [pl.BlockSpec(memory_space=pltpu.VMEM)] * 8,
        out_specs=(pl.BlockSpec(memory_space=pltpu.VMEM),) * 2,
        scratch_shapes=[pltpu.VMEM((NBD, 2, ROWS, E), jnp.bfloat16)],
        compiler_params=pltpu.CompilerParams(vmem_limit_bytes=40 << 20),
        cost_estimate=pl.CostEstimate(
            flops=2 * 512 * 1024 * 512, bytes_accessed=3 << 20, transcendentals=0
        ),
        name="tower",
    )(core, *hidden, *weight)


PLACES = ((0, 32), (32, 32), (64, 16), (80, 16), (96, 32))
PLACES = PLACES + tuple((start + 128, size) for start, size in PLACES)


def one_block(q_ref, lq_ref, row_ref, table, picked, scores, first):
    for j in range(PICKS):
        picked[pl.ds(j * ROWS, ROWS), :] = table[row_ref[first + j]]
    query = jnp.concatenate([q_ref[s] for s in range(TP)], axis=1)
    top = jnp.full((BLK, 128), LOW, jnp.float32)
    for n in range(COLS // TILE):
        cols = pl.ds(n * TILE, TILE)
        part = lax.dot_general(
            query,
            picked[cols, :],
            (((1,), (1,)), ((), ())),
            preferred_element_type=jnp.float32,
        )
        part = part * (SCALE * LOG2E) - lq_ref[0, :, cols]
        scores[:, cols] = part
        for g in range(TILE // 128):
            top = jnp.maximum(top, part[:, g * 128 : (g + 1) * 128])
    top = jnp.max(top, axis=1, keepdims=True)
    total = jnp.zeros((BLK, 128), jnp.float32)
    acc = jnp.zeros((BLK, E), jnp.float32)
    for n in range(COLS // TILE):
        cols = pl.ds(n * TILE, TILE)
        weight = jnp.exp2(scores[:, cols] - top)
        for g in range(TILE // 128):
            total += weight[:, g * 128 : (g + 1) * 128]
        acc += jnp.dot(
            weight.astype(jnp.bfloat16), picked[cols, :], preferred_element_type=jnp.float32
        )
    return top, jnp.sum(total, axis=1, keepdims=True), acc


def rows_of(top, total):
    lane = lax.broadcasted_iota(jnp.int32, (BLK, 128), 1)
    both = jnp.where(lane == 0, top, jnp.where(lane == 1, total, 0.0))
    return jnp.transpose(both)[:8]


def fill(pieces, table, sems):
    copies = [
        pltpu.make_async_copy(piece, table.at[pl.ds(start, size)], sems.at[n])
        for n, (piece, (start, size)) in enumerate(zip(pieces, PLACES))
    ]
    for copy in copies:
        copy.start()
    for copy in copies:
        copy.wait()


def first_kernel(row_ref, q_ref, lq_ref, *refs):
    pieces = refs[:10]
    out_ref, stat_ref, table, picked, scores, sems = refs[10:]
    step = pl.program_id(0)

    @pl.when(step == 0)
    def _():
        fill(pieces, table, sems)

    top, total, acc = one_block(q_ref, lq_ref, row_ref, table, picked, scores, step * PICKS)
    out_ref[...] = acc.astype(jnp.bfloat16)
    stat_ref[0] = rows_of(top, total)


def second_kernel(row_ref, q_ref, lq_ref, *refs):
    pieces = refs[:10]
    other_ref, other_stat_ref, pos_ref = refs[10:13]
    out_ref, stat_ref, table, picked, scores, sems = refs[13:]
    step = pl.program_id(0)

    @pl.when(step == 0)
    def _():
        fill(pieces, table, sems)

    top, total, acc = one_block(q_ref, lq_ref, row_ref, table, picked, scores, step * PICKS)
    theirs = jnp.transpose(jnp.concatenate([other_stat_ref[0]] * 16, axis=0))
    their_top, their_total = theirs[:, 0:1], theirs[:, 1:2]
    joint = jnp.maximum(top, their_top)
    mine_by, theirs_by = jnp.exp2(top - joint), jnp.exp2(their_top - joint)
    acc = acc * mine_by + other_ref[...].astype(jnp.float32) * theirs_by
    for s in range(TP):
        out_ref[s] = acc[:, s * 128 : (s + 1) * 128].astype(jnp.bfloat16)
    stat = rows_of(joint, total * mine_by + their_total * theirs_by)
    row = lax.broadcasted_iota(jnp.int32, (8, BLK), 0)
    stat_ref[0] = jnp.where(row == 2, pos_ref[0], stat)


def attend(body, rows, query, lq, pieces, extra, out_shape, out_spec, name):
    blocks = lq.shape[0]
    stat_spec = pl.BlockSpec((1, 8, BLK), lambda i, r: (i, 0, 0))
    extra_specs = []
    if extra:
        extra_specs = [
            pl.BlockSpec((BLK, E), lambda i, r: (i, 0)),
            stat_spec,
            pl.BlockSpec((1, 1, BLK), lambda i, r: (i, 0, 0)),
        ]
    return pl.pallas_call(
        body,
        grid_spec=pltpu.PrefetchScalarGridSpec(
            num_scalar_prefetch=1,
            grid=(blocks,),
            in_specs=[
                pl.BlockSpec((TP, BLK, 128), lambda i, r: (0, i, 0)),
                pl.BlockSpec((1, 1, COLS), lambda i, r: (i, 0, 0)),
            ]
            + [pl.BlockSpec(memory_space=pl.ANY)] * 10
            + extra_specs,
            out_specs=(out_spec, stat_spec),
            scratch_shapes=[
                pltpu.VMEM((256, ROWS, E), jnp.bfloat16),
                pltpu.VMEM((COLS, E), jnp.bfloat16),
                pltpu.VMEM((BLK, COLS), jnp.float32),
                pltpu.SemaphoreType.DMA((10,)),
            ],
        ),
        out_shape=(out_shape, jax.ShapeDtypeStruct((blocks, 8, BLK), jnp.float32)),
        compiler_params=pltpu.CompilerParams(
            dimension_semantics=("arbitrary",), vmem_limit_bytes=48 << 20
        ),
        cost_estimate=pl.CostEstimate(
            flops=blocks * 4 * BLK * COLS * E,
            bytes_accessed=12 << 20,
            transcendentals=blocks * BLK * COLS,
        ),
        name=name,
    )(rows, query, lq, *pieces, *extra)


def last_kernel(*refs):
    parts, stats = refs[0:4], refs[4:8]
    positive_ref, loss_ref, grad_ref = refs[8:]
    stat = [ref[0] for ref in stats]
    pos = (stat[0][2:3] + stat[1][2:3] + stat[2][2:3] + stat[3][2:3]) * LOG2E
    joint = pos
    for one in stat:
        joint = jnp.maximum(joint, one[0:1])
    total = jnp.exp2(pos - joint)
    for one in stat:
        total += one[1:2] * jnp.exp2(one[0:1] - joint)
    log_total = joint + jnp.log(total) * LOG2E
    loss_ref[0] = (log_total - pos) * LN2
    factors = [jnp.exp2(one[0:1] - log_total) * SCALE for one in stat]
    factors.append((jnp.exp2(pos - log_total) - 1.0) * SCALE)
    row = lax.broadcasted_iota(jnp.int32, (128, BLK), 0)
    packed = jnp.zeros((128, BLK), jnp.float32)
    for n, factor in enumerate(factors):
        packed = jnp.where(row == n, factor, packed)
    by = jnp.transpose(packed)
    grad = by[:, 4:5] * positive_ref[...].astype(jnp.float32)
    for n in range(4):
        grad += by[:, n : n + 1] * parts[n][...].astype(jnp.float32)
    grad_ref[...] = grad.astype(jnp.bfloat16)


def last(parts, stats, positive):
    blocks = stats[0].shape[0]
    flat = pl.BlockSpec((BLK, 128), lambda i: (i, 0))
    stat_spec = pl.BlockSpec((1, 8, BLK), lambda i: (i, 0, 0))
    return pl.pallas_call(
        last_kernel,
        grid=(blocks,),
        in_specs=[flat] * 4 + [stat_spec] * 4 + [flat],
        out_specs=(pl.BlockSpec((1, 1, BLK), lambda i: (i, 0, 0)), flat),
        out_shape=(
            jax.ShapeDtypeStruct((blocks, 1, BLK), jnp.float32),
            jax.ShapeDtypeStruct((blocks * BLK, 128), jnp.bfloat16),
        ),
        compiler_params=pltpu.CompilerParams(vmem_limit_bytes=32 << 20),
        name="last",
    )(*parts, *stats, positive)


def spread(near, far):
    near_line = jnp.concatenate([near[None]] + [send(near, -d, 0)[None] for d in (1, 2, 3)])
    far_line = jnp.concatenate([far[None]] + [send(far, 0, -d)[None] for d in (1, 2, 3)])
    near_up, near_down = send(near_line, 0, 1), send(near_line, 0, -1)
    far_up, far_down = send(far_line, 1, 0), send(far_line, -1, 0)
    near_a, near_b = send(near_up[:2], 0, 1), send(near_down[2:], 0, -1)
    far_a, far_b = send(far_up[:2], 1, 0), send(far_down[2:], -1, 0)
    pieces = [near_line, near_down, near_a, near_b, near_up]
    pieces += [far_line, far_down, far_a, far_b, far_up]
    return [piece.reshape(-1, ROWS, E) for piece in pieces]


def local(query_emb, positive_emb, item_hidden, item_weight, neg_blocks, block_home, sample_counts):
    rank = lax.axis_index("tp")
    place = lax.axis_index("cat")
    core, my_z, my_y = place % 2, (place // 2) % NZ, place // (2 * NZ)
    qblocks = neg_blocks.shape[0]
    total_blocks = block_home.shape[0]

    hidden = item_hidden.reshape(NBD, TP, BLK // TP, -1)

    def piece(d):
        cut = lax.dynamic_index_in_dim(hidden, (rank + d) % TP, 1, keepdims=False)
        return cut.reshape(NBD * BLK // TP, -1)

    weights = [item_weight] + [send_x(item_weight, d) for d in (1, 2, 3)]
    hiddens = [piece(0)] + [send_x(piece(d), d) for d in (1, 2, 3)]
    keep, give = tower(core.reshape(1).astype(jnp.int32), hiddens, weights)
    pieces = spread(keep, send(give, 0, 0, 1))

    query = lax.all_gather(query_emb, "tp")
    other_query = send(query, 0, 0, 1)
    pos_part = SCALE * jnp.sum(
        query_emb.astype(jnp.float32) * positive_emb.astype(jnp.float32), axis=1
    ).reshape(qblocks, 1, BLK)

    picks = jnp.concatenate([send(neg_blocks, 0, 0, 1), neg_blocks])
    matches = picks[:, :, None] == jnp.arange(total_blocks, dtype=jnp.int32)[None, None, :]
    home = jnp.sum(jnp.where(matches, block_home[None, None, :], 0), axis=2)
    slot, owner = home % NBD, home // NBD
    dz = ((owner // 2) % NZ - my_z) % NZ
    dy = (owner // (2 * NZ) - my_y) % NY
    rows = jnp.where(
        owner % 2 == core, dz * 32 + dy * NBD + slot, 128 + dy * 32 + dz * NBD + slot
    ).astype(jnp.int32)
    log_table = (jnp.log(sample_counts.astype(jnp.float32)) * LOG2E).reshape(
        total_blocks, TP * 2, ROWS
    )
    my_log = lax.dynamic_index_in_dim(log_table, rank * 2 + core, 1, keepdims=False)
    lq = my_log[home].reshape(2 * qblocks, 1, COLS)

    theirs, their_stat = attend(
        first_kernel,
        rows[:qblocks].reshape(-1),
        other_query,
        lq[:qblocks],
        pieces,
        (),
        jax.ShapeDtypeStruct((qblocks * BLK, E), jnp.bfloat16),
        pl.BlockSpec((BLK, E), lambda i, r: (i, 0)),
        "attend_other",
    )
    from_other = send(theirs, 0, 0, 1)
    from_other_stat = send(their_stat, 0, 0, 1)
    mine, stat = attend(
        second_kernel,
        rows[qblocks:].reshape(-1),
        query,
        lq[qblocks:],
        pieces,
        (from_other, from_other_stat, pos_part),
        jax.ShapeDtypeStruct((TP, qblocks * BLK, 128), jnp.bfloat16),
        pl.BlockSpec((TP, BLK, 128), lambda i, r: (0, i, 0)),
        "attend_own",
    )

    def share(d):
        return lax.dynamic_index_in_dim(mine, (rank + d) % TP, 0, keepdims=False)

    stats = [stat] + [send_x(stat, d) for d in (1, 2, 3)]
    parts = [share(0)] + [send_x(share(d), d) for d in (1, 2, 3)]
    loss, grad = last(parts, stats, positive_emb)
    return loss.reshape(-1), grad


def solution(mesh):
    placed = (
        P("cat", "tp"),
        P("cat", "tp"),
        P("cat", "tp"),
        P("tp", None),
        P("cat", None),
        P(),
        P(),
    )
    return jax.shard_map(
        local, mesh=mesh, in_specs=placed, out_specs=(P("cat"), P("cat", "tp")), check_vma=False
    )
```

```python
import functools
import math

import jax
import jax.numpy as jnp
from jax import lax
from jax.experimental import pallas as pl
from jax.experimental.pallas import tpu as pltpu
from jax.sharding import PartitionSpec as P

BLK = 256
TP = 4
NY = 4
NZ = 4
E = 512
LOG2E = math.log2(math.e)
LN2 = math.log(2.0)
SCALE = 2.0 / math.sqrt(E)
LOW = -1e30
ROWS = BLK // TP // 2
NBD = 8
PICKS = 64
COLS = PICKS * ROWS
TILE = 512
HID = 1024
EXTRA = 32


def cat_perm(flip_y, flip_z, flip_c):
    def at(y, z, c):
        return (y * NZ + z) * 2 + c

    return [
        (at(y, z, c), at(y ^ flip_y, z ^ flip_z, c ^ flip_c))
        for y in range(NY)
        for z in range(NZ)
        for c in range(2)
    ]


def send(value, y=0, z=0, c=0):
    return lax.ppermute(value, "cat", cat_perm(y, z, c))


def send_x(value, d):
    return lax.ppermute(value, "tp", [(i, (i + d) % TP) for i in range(TP)])


def tower_kernel(core_ref, *refs):
    hidden = refs[0:4]
    mine, theirs = refs[4:8], refs[8]
    keep_ref, give_ref, scratch = refs[9:]
    core = core_ref[0]
    half = HID // TP // 2
    acc = jnp.zeros((NBD * 2 * ROWS, E), jnp.float32)
    for d in range(TP):
        low = jnp.where(core == 0, mine[d][...], theirs[d])
        high = jnp.where(core == 0, theirs[d], mine[d][...])
        acc += jnp.dot(hidden[d][:, :half], low, preferred_element_type=jnp.float32)
        acc += jnp.dot(hidden[d][:, half:], high, preferred_element_type=jnp.float32)
    scratch[...] = acc.astype(jnp.bfloat16).reshape(scratch.shape)
    keep_ref[...] = scratch[:, core]
    give_ref[...] = scratch[:, 1 - core]


def tower(core, hidden, mine, theirs):
    half = jax.ShapeDtypeStruct((NBD, ROWS, E), jnp.bfloat16)
    return pl.pallas_call(
        tower_kernel,
        out_shape=(half, half),
        in_specs=[pl.BlockSpec(memory_space=pltpu.SMEM)]
        + [pl.BlockSpec(memory_space=pltpu.VMEM)] * 9,
        out_specs=(pl.BlockSpec(memory_space=pltpu.VMEM),) * 2,
        scratch_shapes=[pltpu.VMEM((NBD, 2, ROWS, E), jnp.bfloat16)],
        compiler_params=pltpu.CompilerParams(vmem_limit_bytes=40 << 20),
        cost_estimate=pl.CostEstimate(
            flops=2 * 512 * 1024 * 512, bytes_accessed=3 << 20, transcendentals=0
        ),
        name="tower",
    )(core, *hidden, *mine, theirs)


PIECES = 16


def one_block(rank, q_ref, lq_ref, row_ref, table, picked, scores, first):
    for j in range(PICKS):
        picked[pl.ds(j * ROWS, ROWS), :] = table[row_ref[first + j]]
    query = jnp.concatenate(
        [q_ref[lax.rem(rank + TP - s, TP)] for s in range(TP)], axis=1
    )
    top = jnp.full((BLK, 128), LOW, jnp.float32)
    for n in range(COLS // TILE):
        cols = pl.ds(n * TILE, TILE)
        part = lax.dot_general(
            query,
            picked[cols, :],
            (((1,), (1,)), ((), ())),
            preferred_element_type=jnp.float32,
        )
        part = part * (SCALE * LOG2E) - lq_ref[0, :, cols]
        scores[:, cols] = part
        for g in range(TILE // 128):
            top = jnp.maximum(top, part[:, g * 128 : (g + 1) * 128])
    top = jnp.max(top, axis=1, keepdims=True)
    total = jnp.zeros((BLK, 128), jnp.float32)
    acc = jnp.zeros((BLK, E), jnp.float32)
    for n in range(COLS // TILE):
        cols = pl.ds(n * TILE, TILE)
        weight = jnp.exp2(scores[:, cols] - top)
        for g in range(TILE // 128):
            total += weight[:, g * 128 : (g + 1) * 128]
        acc += jnp.dot(
            weight.astype(jnp.bfloat16), picked[cols, :], preferred_element_type=jnp.float32
        )
    return top, jnp.sum(total, axis=1, keepdims=True), acc


def rows_of(top, total):
    lane = lax.broadcasted_iota(jnp.int32, (BLK, 128), 1)
    both = jnp.where(lane == 0, top, jnp.where(lane == 1, total, 0.0))
    return jnp.transpose(both)[:8]


def fill(pieces, table, sems):
    size = table.shape[0] // PIECES
    copies = [
        pltpu.make_async_copy(piece, table.at[pl.ds(n * size, size)], sems.at[n])
        for n, piece in enumerate(pieces)
    ]
    for copy in copies:
        copy.start()
    for copy in copies:
        copy.wait()


def first_kernel(row_ref, rank_ref, q_ref, lq_ref, *refs):
    pieces = refs[:PIECES]
    out_ref, stat_ref, table, picked, scores, sems = refs[PIECES:]
    step = pl.program_id(0)

    @pl.when(step == 0)
    def _():
        fill(pieces, table, sems)

    top, total, acc = one_block(rank_ref[0], q_ref, lq_ref, row_ref, table, picked, scores, step * PICKS)
    out_ref[...] = acc.astype(jnp.bfloat16)
    stat_ref[0] = rows_of(top, total)


def split_rows(row):
    out = []
    for _ in range(3):
        part = row.astype(jnp.bfloat16).astype(jnp.float32)
        out += [part[:, :128], part[:, 128:]]
        row = row - part
    return out


def joined_row(rows):
    halves = [rows[n : n + 1] + (rows[n + 2 : n + 3] + rows[n + 4 : n + 5]) for n in range(2)]
    return jnp.concatenate(halves, axis=1)


def second_kernel(row_ref, rank_ref, q_ref, lq_ref, *refs):
    pieces = refs[:PIECES]
    other_ref, other_stat_ref, pos_ref = refs[PIECES : PIECES + 3]
    outs = refs[PIECES + 3 : PIECES + 7]
    table, picked, scores, sems, quarters = refs[PIECES + 7 :]
    step = pl.program_id(0)

    @pl.when(step == 0)
    def _():
        fill(pieces, table, sems)

    top, total, acc = one_block(rank_ref[0], q_ref, lq_ref, row_ref, table, picked, scores, step * PICKS)
    theirs = jnp.transpose(jnp.concatenate([other_stat_ref[0]] * 16, axis=0))
    their_top, their_total = theirs[:, 0:1], theirs[:, 1:2]
    joint = jnp.maximum(top, their_top)
    mine_by, theirs_by = jnp.exp2(top - joint), jnp.exp2(their_top - joint)
    acc = acc * mine_by + other_ref[...].astype(jnp.float32) * theirs_by
    for s in range(TP):
        quarters[s] = acc[:, s * 128 : (s + 1) * 128].astype(jnp.bfloat16)
    stat = rows_of(joint, total * mine_by + their_total * theirs_by)
    rows = split_rows(stat[0:1]) + split_rows(stat[1:2]) + split_rows(pos_ref[0])
    rows.append(jnp.zeros((EXTRA - len(rows), 128), jnp.float32))
    tail = jnp.concatenate(rows, axis=0).astype(jnp.bfloat16)
    for d in range(TP):
        outs[d][0, :BLK] = quarters[lax.rem(rank_ref[0] + d, TP)]
        outs[d][0, BLK:] = tail


def attend(body, scalars, query, lq, pieces, extra, outs, out_specs, scratch, name):
    blocks = lq.shape[0]
    extra_specs = []
    if extra:
        extra_specs = [
            pl.BlockSpec((BLK, E), lambda i, *_: (i, 0)),
            pl.BlockSpec((1, 8, BLK), lambda i, *_: (i, 0, 0)),
            pl.BlockSpec((1, 1, BLK), lambda i, *_: (i, 0, 0)),
        ]
    return pl.pallas_call(
        body,
        grid_spec=pltpu.PrefetchScalarGridSpec(
            num_scalar_prefetch=len(scalars),
            grid=(blocks,),
            in_specs=[
                pl.BlockSpec((TP, BLK, 128), lambda i, *_: (0, i, 0)),
                pl.BlockSpec((1, 1, COLS), lambda i, *_: (i, 0, 0)),
            ]
            + [pl.BlockSpec(memory_space=pl.ANY)] * PIECES
            + extra_specs,
            out_specs=out_specs,
            scratch_shapes=[
                pltpu.VMEM((256, ROWS, E), jnp.bfloat16),
                pltpu.VMEM((COLS, E), jnp.bfloat16),
                pltpu.VMEM((BLK, COLS), jnp.float32),
                pltpu.SemaphoreType.DMA((PIECES,)),
            ]
            + scratch,
        ),
        out_shape=outs,
        compiler_params=pltpu.CompilerParams(
            dimension_semantics=("arbitrary",), vmem_limit_bytes=58 << 20
        ),
        cost_estimate=pl.CostEstimate(
            flops=blocks * 4 * BLK * COLS * E,
            bytes_accessed=12 << 20,
            transcendentals=blocks * BLK * COLS,
        ),
        name=name,
    )(*scalars, query, lq, *pieces, *extra)


def last_kernel(*refs):
    parts, positive_ref, loss_ref, grad_ref = refs[0:4], *refs[4:]
    tails = [ref[0, BLK:].astype(jnp.float32) for ref in parts]
    tops = [joined_row(tail[0:6]) for tail in tails]
    totals = [joined_row(tail[6:12]) for tail in tails]
    shares = [joined_row(tail[12:18]) for tail in tails]
    pos = (shares[0] + shares[1] + shares[2] + shares[3]) * LOG2E
    joint = pos
    for top in tops:
        joint = jnp.maximum(joint, top)
    total = jnp.exp2(pos - joint)
    for top, one in zip(tops, totals):
        total += one * jnp.exp2(top - joint)
    log_total = joint + jnp.log(total) * LOG2E
    loss_ref[0] = (log_total - pos) * LN2
    factors = [jnp.exp2(top - log_total) * SCALE for top in tops]
    factors.append((jnp.exp2(pos - log_total) - 1.0) * SCALE)
    row = lax.broadcasted_iota(jnp.int32, (128, BLK), 0)
    packed = jnp.zeros((128, BLK), jnp.float32)
    for n, factor in enumerate(factors):
        packed = jnp.where(row == n, factor, packed)
    by = jnp.transpose(packed)
    grad = by[:, 4:5] * positive_ref[...].astype(jnp.float32)
    for n in range(4):
        grad += by[:, n : n + 1] * parts[n][0, :BLK].astype(jnp.float32)
    grad_ref[...] = grad.astype(jnp.bfloat16)


def last(parts, positive):
    blocks = parts[0].shape[0]
    flat = pl.BlockSpec((BLK, 128), lambda i: (i, 0))
    return pl.pallas_call(
        last_kernel,
        grid=(blocks,),
        in_specs=[pl.BlockSpec((1, BLK + EXTRA, 128), lambda i: (i, 0, 0))] * 4 + [flat],
        out_specs=(pl.BlockSpec((1, 1, BLK), lambda i: (i, 0, 0)), flat),
        out_shape=(
            jax.ShapeDtypeStruct((blocks, 1, BLK), jnp.float32),
            jax.ShapeDtypeStruct((blocks * BLK, 128), jnp.bfloat16),
        ),
        compiler_params=pltpu.CompilerParams(vmem_limit_bytes=32 << 20),
        name="last",
    )(*parts, positive)


STREAMS = (
    (("y", 1), ("y", 3), ("z", 1), ("z", 3)),
    (("y", 3), ("y", 1), ("z", 3), ("z", 1)),
    (("z", 1), ("z", 3), ("y", 1), ("y", 3)),
    (("z", 3), ("z", 1), ("y", 3), ("y", 1)),
)


def spread(near, far):
    held = [near[: NBD // 2], near[NBD // 2 :], far[: NBD // 2], far[NBD // 2 :]]
    for step in range(2):
        got = [send(h, **{st[step][0]: st[step][1]}) for h, st in zip(held, STREAMS)]
        held = [jnp.concatenate([h, g]) for h, g in zip(held, got)]
    third = [send(h, **{st[2][0]: st[2][1]}) for h, st in zip(held, STREAMS)]
    fourth = [send(h, **{st[3][0]: st[3][1]}) for h, st in zip(held, STREAMS)]
    fifth = [send(h, **{st[3][0]: st[3][1]}) for h, st in zip(third, STREAMS)]
    pieces = []
    for four in zip(held, third, fourth, fifth):
        pieces += list(four)
    return pieces, held[0]


def place_of(flipped, first):
    return jnp.where(
        flipped == 0, 0, jnp.where(flipped == 2, 3, jnp.where(flipped == first, 1, 2))
    )


def local(query_emb, positive_emb, item_hidden, item_weight, neg_blocks, block_home, sample_counts):
    rank = lax.axis_index("tp")
    place = lax.axis_index("cat")
    core, my_z, my_y = place % 2, (place // 2) % NZ, place // (2 * NZ)
    qblocks = neg_blocks.shape[0]
    total_blocks = block_home.shape[0]

    hidden = item_hidden.reshape(NBD, TP, BLK // TP, -1)

    def piece(d):
        cut = lax.dynamic_index_in_dim(hidden, (rank + d) % TP, 1, keepdims=False)
        return cut.reshape(NBD * BLK // TP, -1)

    core_id = core.reshape(1).astype(jnp.int32)
    half = lax.dynamic_slice_in_dim(item_weight, core * (HID // TP // 2), HID // TP // 2, 0)
    mine_w = [half] + [send_x(half, d) for d in (1, 2, 3)]
    theirs_w = send(jnp.stack(mine_w), c=1)
    hiddens = [piece(0)] + [send_x(piece(d), d) for d in (1, 2, 3)]
    keep, give = tower(core_id, hiddens, mine_w, theirs_w)
    pieces, mark = spread(keep, send(give, c=1))

    late_query, _ = lax.optimization_barrier((query_emb, mark))
    rank_id = rank.reshape(1).astype(jnp.int32)
    query = jnp.stack([late_query] + [send_x(late_query, d) for d in (1, 2, 3)])
    other_query = send(query, c=1)
    pos_part = SCALE * jnp.sum(
        query_emb.astype(jnp.float32) * positive_emb.astype(jnp.float32), axis=1
    ).reshape(qblocks, 1, BLK)

    picks = jnp.concatenate([send(neg_blocks, c=1), neg_blocks])
    matches = picks[:, :, None] == jnp.arange(total_blocks, dtype=jnp.int32)[None, None, :]
    home = jnp.sum(jnp.where(matches, block_home[None, None, :], 0), axis=2)
    slot, owner = home % NBD, home // NBD
    flip_z = ((owner // 2) % NZ) ^ my_z
    flip_y = (owner // (2 * NZ)) ^ my_y
    late = slot // (NBD // 2)
    at_y = place_of(flip_y, jnp.where(late == 0, 1, 3))
    at_z = place_of(flip_z, jnp.where(late == 0, 1, 3))
    near = owner % 2 == core
    rows = jnp.where(near, at_z * 4 + at_y, 128 // 4 + at_y * 4 + at_z)
    rows = (rows * 4 + late * 64 + slot % 4).astype(jnp.int32)
    log_table = (jnp.log(sample_counts.astype(jnp.float32)) * LOG2E).reshape(
        total_blocks, TP * 2, ROWS
    )
    my_log = lax.dynamic_index_in_dim(log_table, rank * 2 + core, 1, keepdims=False)
    lq = my_log[home].reshape(2 * qblocks, 1, COLS)

    bf16 = jnp.bfloat16
    theirs, their_stat = attend(
        first_kernel,
        (rows[:qblocks].reshape(-1), rank_id),
        other_query,
        lq[:qblocks],
        pieces,
        (),
        (
            jax.ShapeDtypeStruct((qblocks * BLK, E), bf16),
            jax.ShapeDtypeStruct((qblocks, 8, BLK), jnp.float32),
        ),
        (
            pl.BlockSpec((BLK, E), lambda i, *_: (i, 0)),
            pl.BlockSpec((1, 8, BLK), lambda i, *_: (i, 0, 0)),
        ),
        [],
        "attend_other",
    )
    from_other = send(theirs, c=1)
    from_other_stat = send(their_stat, c=1)
    shares = attend(
        second_kernel,
        (rows[qblocks:].reshape(-1), rank_id),
        query,
        lq[qblocks:],
        pieces,
        (from_other, from_other_stat, pos_part),
        (jax.ShapeDtypeStruct((qblocks, BLK + EXTRA, 128), bf16),) * TP,
        (pl.BlockSpec((1, BLK + EXTRA, 128), lambda i, *_: (i, 0, 0)),) * TP,
        [pltpu.VMEM((TP, BLK, 128), bf16)],
        "attend_own",
    )
    parts = [shares[0]] + [send_x(shares[d], d) for d in (1, 2, 3)]
    loss, grad = last(parts, positive_emb)
    return loss.reshape(-1), grad


def solution(mesh):
    placed = (
        P("cat", "tp"),
        P("cat", "tp"),
        P("cat", "tp"),
        P("tp", None),
        P("cat", None),
        P(),
        P(),
    )
    return jax.shard_map(
        local, mesh=mesh, in_specs=placed, out_specs=(P("cat"), P("cat", "tp")), check_vma=False
    )
```

```python
import functools
import math

import jax
import jax.numpy as jnp
from jax import lax
from jax.experimental import pallas as pl
from jax.experimental.pallas import tpu as pltpu
from jax.sharding import PartitionSpec as P

BLK = 256
TP = 4
NY = 4
NZ = 4
E = 512
LOG2E = math.log2(math.e)
LN2 = math.log(2.0)
SCALE = 2.0 / math.sqrt(E)
LOW = -1e30
ROWS = BLK // TP // 2
NBD = 8
PICKS = 64
COLS = PICKS * ROWS
TILE = 512
HID = 1024
EXTRA = 32


def cat_perm(flip_y, flip_z, flip_c):
    def at(y, z, c):
        return (y * NZ + z) * 2 + c

    return [
        (at(y, z, c), at(y ^ flip_y, z ^ flip_z, c ^ flip_c))
        for y in range(NY)
        for z in range(NZ)
        for c in range(2)
    ]


def send(value, y=0, z=0, c=0):
    return lax.ppermute(value, "cat", cat_perm(y, z, c))


def send_x(value, d):
    return lax.ppermute(value, "tp", [(i, (i + d) % TP) for i in range(TP)])


def tower_kernel(core_ref, *refs):
    hidden = refs[0:4]
    mine, theirs = refs[4:8], refs[8]
    out_ref = refs[9]
    core = core_ref[0]
    half = HID // TP // 2
    acc = jnp.zeros((NBD * 2 * ROWS, E), jnp.float32)
    for d in range(TP):
        low = jnp.where(core == 0, mine[d][...], theirs[d])
        high = jnp.where(core == 0, theirs[d], mine[d][...])
        acc += jnp.dot(hidden[d][:, :half], low, preferred_element_type=jnp.float32)
        acc += jnp.dot(hidden[d][:, half:], high, preferred_element_type=jnp.float32)
    out_ref[...] = acc.astype(jnp.bfloat16).reshape(out_ref.shape)


def tower(core, hidden, mine, theirs):
    return pl.pallas_call(
        tower_kernel,
        out_shape=jax.ShapeDtypeStruct((2 * NBD, ROWS, E), jnp.bfloat16),
        in_specs=[pl.BlockSpec(memory_space=pltpu.SMEM)]
        + [pl.BlockSpec(memory_space=pltpu.VMEM)] * 9,
        out_specs=pl.BlockSpec(memory_space=pltpu.VMEM),
        compiler_params=pltpu.CompilerParams(vmem_limit_bytes=40 << 20),
        cost_estimate=pl.CostEstimate(
            flops=2 * 512 * 1024 * 512, bytes_accessed=3 << 20, transcendentals=0
        ),
        name="tower",
    )(core, *hidden, *mine, theirs)


PIECES = 8


def one_block(rank, q_ref, lq_ref, row_ref, table, picked, scores, first):
    for j in range(PICKS):
        picked[pl.ds(j * ROWS, ROWS), :] = table[row_ref[first + j]]
    query = jnp.concatenate(
        [q_ref[lax.rem(rank + TP - s, TP)] for s in range(TP)], axis=1
    )
    top = jnp.full((BLK, 128), LOW, jnp.float32)
    for n in range(COLS // TILE):
        cols = pl.ds(n * TILE, TILE)
        part = lax.dot_general(
            query,
            picked[cols, :],
            (((1,), (1,)), ((), ())),
            preferred_element_type=jnp.float32,
        )
        part = part * (SCALE * LOG2E) - lq_ref[0, :, cols]
        scores[:, cols] = part
        for g in range(TILE // 128):
            top = jnp.maximum(top, part[:, g * 128 : (g + 1) * 128])
    top = jnp.max(top, axis=1, keepdims=True)
    total = jnp.zeros((BLK, 128), jnp.float32)
    acc = jnp.zeros((BLK, E), jnp.float32)
    for n in range(COLS // TILE):
        cols = pl.ds(n * TILE, TILE)
        weight = jnp.exp2(scores[:, cols] - top)
        for g in range(TILE // 128):
            total += weight[:, g * 128 : (g + 1) * 128]
        acc += jnp.dot(
            weight.astype(jnp.bfloat16), picked[cols, :], preferred_element_type=jnp.float32
        )
    return top, jnp.sum(total, axis=1, keepdims=True), acc


def rows_of(top, total):
    lane = lax.broadcasted_iota(jnp.int32, (BLK, 128), 1)
    both = jnp.where(lane == 0, top, jnp.where(lane == 1, total, 0.0))
    return jnp.transpose(both)[:8]


def fill(pieces, table, sems):
    size = table.shape[0] // PIECES
    copies = [
        pltpu.make_async_copy(piece, table.at[pl.ds(n * size, size)], sems.at[n])
        for n, piece in enumerate(pieces)
    ]
    for copy in copies:
        copy.start()
    for copy in copies:
        copy.wait()


def first_kernel(row_ref, rank_ref, q_ref, lq_ref, *refs):
    pieces = refs[:PIECES]
    out_ref, stat_ref, table, picked, scores, sems = refs[PIECES:]
    step = pl.program_id(0)

    @pl.when(step == 0)
    def _():
        fill(pieces, table, sems)

    top, total, acc = one_block(rank_ref[0], q_ref, lq_ref, row_ref, table, picked, scores, step * PICKS)
    out_ref[...] = acc.astype(jnp.bfloat16)
    stat_ref[0] = rows_of(top, total)


def split_rows(row):
    out = []
    for _ in range(3):
        part = row.astype(jnp.bfloat16).astype(jnp.float32)
        out += [part[:, :128], part[:, 128:]]
        row = row - part
    return out


def joined_row(rows):
    halves = [rows[n : n + 1] + (rows[n + 2 : n + 3] + rows[n + 4 : n + 5]) for n in range(2)]
    return jnp.concatenate(halves, axis=1)


def second_kernel(row_ref, rank_ref, q_ref, lq_ref, *refs):
    pieces = refs[:PIECES]
    other_ref, other_stat_ref, pos_ref = refs[PIECES : PIECES + 3]
    outs = refs[PIECES + 3 : PIECES + 7]
    table, picked, scores, sems, quarters = refs[PIECES + 7 :]
    step = pl.program_id(0)

    @pl.when(step == 0)
    def _():
        fill(pieces, table, sems)

    top, total, acc = one_block(rank_ref[0], q_ref, lq_ref, row_ref, table, picked, scores, step * PICKS)
    theirs = jnp.transpose(jnp.concatenate([other_stat_ref[0]] * 16, axis=0))
    their_top, their_total = theirs[:, 0:1], theirs[:, 1:2]
    joint = jnp.maximum(top, their_top)
    mine_by, theirs_by = jnp.exp2(top - joint), jnp.exp2(their_top - joint)
    acc = acc * mine_by + other_ref[...].astype(jnp.float32) * theirs_by
    for s in range(TP):
        quarters[s] = acc[:, s * 128 : (s + 1) * 128].astype(jnp.bfloat16)
    stat = rows_of(joint, total * mine_by + their_total * theirs_by)
    rows = split_rows(stat[0:1]) + split_rows(stat[1:2]) + split_rows(pos_ref[0])
    rows.append(jnp.zeros((EXTRA - len(rows), 128), jnp.float32))
    tail = jnp.concatenate(rows, axis=0).astype(jnp.bfloat16)
    for d in range(TP):
        outs[d][0, :BLK] = quarters[lax.rem(rank_ref[0] + d, TP)]
        outs[d][0, BLK:] = tail


def attend(body, scalars, query, lq, pieces, extra, outs, out_specs, scratch, name):
    blocks = lq.shape[0]
    extra_specs = []
    if extra:
        extra_specs = [
            pl.BlockSpec((BLK, E), lambda i, *_: (i, 0)),
            pl.BlockSpec((1, 8, BLK), lambda i, *_: (i, 0, 0)),
            pl.BlockSpec((1, 1, BLK), lambda i, *_: (i, 0, 0)),
        ]
    return pl.pallas_call(
        body,
        grid_spec=pltpu.PrefetchScalarGridSpec(
            num_scalar_prefetch=len(scalars),
            grid=(blocks,),
            in_specs=[
                pl.BlockSpec((TP, BLK, 128), lambda i, *_: (0, i, 0)),
                pl.BlockSpec((1, 1, COLS), lambda i, *_: (i, 0, 0)),
            ]
            + [pl.BlockSpec(memory_space=pl.ANY)] * PIECES
            + extra_specs,
            out_specs=out_specs,
            scratch_shapes=[
                pltpu.VMEM((256, ROWS, E), jnp.bfloat16),
                pltpu.VMEM((COLS, E), jnp.bfloat16),
                pltpu.VMEM((BLK, COLS), jnp.float32),
                pltpu.SemaphoreType.DMA((PIECES,)),
            ]
            + scratch,
        ),
        out_shape=outs,
        compiler_params=pltpu.CompilerParams(
            dimension_semantics=("arbitrary",), vmem_limit_bytes=58 << 20
        ),
        cost_estimate=pl.CostEstimate(
            flops=blocks * 4 * BLK * COLS * E,
            bytes_accessed=12 << 20,
            transcendentals=blocks * BLK * COLS,
        ),
        name=name,
    )(*scalars, query, lq, *pieces, *extra)


def last_kernel(*refs):
    parts, positive_ref, loss_ref, grad_ref = refs[0:4], *refs[4:]
    tails = [ref[0, BLK:].astype(jnp.float32) for ref in parts]
    tops = [joined_row(tail[0:6]) for tail in tails]
    totals = [joined_row(tail[6:12]) for tail in tails]
    shares = [joined_row(tail[12:18]) for tail in tails]
    pos = (shares[0] + shares[1] + shares[2] + shares[3]) * LOG2E
    joint = pos
    for top in tops:
        joint = jnp.maximum(joint, top)
    total = jnp.exp2(pos - joint)
    for top, one in zip(tops, totals):
        total += one * jnp.exp2(top - joint)
    log_total = joint + jnp.log(total) * LOG2E
    loss_ref[0] = (log_total - pos) * LN2
    factors = [jnp.exp2(top - log_total) * SCALE for top in tops]
    factors.append((jnp.exp2(pos - log_total) - 1.0) * SCALE)
    row = lax.broadcasted_iota(jnp.int32, (128, BLK), 0)
    packed = jnp.zeros((128, BLK), jnp.float32)
    for n, factor in enumerate(factors):
        packed = jnp.where(row == n, factor, packed)
    by = jnp.transpose(packed)
    grad = by[:, 4:5] * positive_ref[...].astype(jnp.float32)
    for n in range(4):
        grad += by[:, n : n + 1] * parts[n][0, :BLK].astype(jnp.float32)
    grad_ref[...] = grad.astype(jnp.bfloat16)


def last(parts, positive):
    blocks = parts[0].shape[0]
    flat = pl.BlockSpec((BLK, 128), lambda i: (i, 0))
    return pl.pallas_call(
        last_kernel,
        grid=(blocks,),
        in_specs=[pl.BlockSpec((1, BLK + EXTRA, 128), lambda i: (i, 0, 0))] * 4 + [flat],
        out_specs=(pl.BlockSpec((1, 1, BLK), lambda i: (i, 0, 0)), flat),
        out_shape=(
            jax.ShapeDtypeStruct((blocks, 1, BLK), jnp.float32),
            jax.ShapeDtypeStruct((blocks * BLK, 128), jnp.bfloat16),
        ),
        compiler_params=pltpu.CompilerParams(vmem_limit_bytes=32 << 20),
        name="last",
    )(*parts, positive)


STREAMS = (
    (("y", 1), ("y", 3), ("z", 1), ("z", 3)),
    (("y", 3), ("y", 1), ("z", 3), ("z", 1)),
    (("z", 1), ("z", 3), ("y", 1), ("y", 3)),
    (("z", 3), ("z", 1), ("y", 3), ("y", 1)),
)


def together(*values):
    return list(lax.optimization_barrier(tuple(values)))


def spread(items, query):
    held = [items[n * 4 : n * 4 + 4] for n in range(4)]
    queries = [query]
    for step in range(4):
        got = [send(h, **{st[step][0]: st[step][1]}) for h, st in zip(held, STREAMS)]
        if step == 3:
            break
        got = together(*got, send_x(query, step + 1), query)
        queries.append(got[4])
        query = got[5]
        held = together(*[jnp.concatenate([h, g]) for h, g in zip(held, got)])
    return held, got, jnp.stack(queries)


def place_of(flipped, first):
    return jnp.where(
        flipped == 0, 0, jnp.where(flipped == 2, 3, jnp.where(flipped == first, 1, 2))
    )


def local(query_emb, positive_emb, item_hidden, item_weight, neg_blocks, block_home, sample_counts):
    rank = lax.axis_index("tp")
    place = lax.axis_index("cat")
    core, my_z, my_y = place % 2, (place // 2) % NZ, place // (2 * NZ)
    qblocks = neg_blocks.shape[0]
    total_blocks = block_home.shape[0]

    core_id = core.reshape(1).astype(jnp.int32)
    rank_id = rank.reshape(1).astype(jnp.int32)
    hidden = item_hidden.reshape(NBD, TP, 2, ROWS, -1)
    keep = lax.dynamic_index_in_dim(hidden, core, 2, keepdims=False)
    give = lax.dynamic_index_in_dim(hidden, 1 - core, 2, keepdims=False)
    half = lax.dynamic_slice_in_dim(item_weight, core * (HID // TP // 2), HID // TP // 2, 0)
    swapped = send(give, c=1)
    mine_w = [half] + [send_x(half, d) for d in (1, 2, 3)]
    both = jnp.concatenate([keep, swapped])

    def piece(d):
        cut = lax.dynamic_index_in_dim(both, (rank + d) % TP, 1, keepdims=False)
        return cut.reshape(2 * NBD * ROWS, -1)

    hiddens = [piece(0)] + [send_x(piece(d), d) for d in (1, 2, 3)]
    theirs_w = send(jnp.stack(mine_w), c=1)
    items, late_query = together(tower(core_id, hiddens, mine_w, theirs_w), query_emb)
    held, got, query = spread(items, late_query)
    pieces = []
    for pair in zip(held, got):
        pieces += list(pair)
    other_query = send(query, c=1)
    pos_part = SCALE * jnp.sum(
        query_emb.astype(jnp.float32) * positive_emb.astype(jnp.float32), axis=1
    ).reshape(qblocks, 1, BLK)

    picks = jnp.concatenate([send(neg_blocks, c=1), neg_blocks])
    matches = picks[:, :, None] == jnp.arange(total_blocks, dtype=jnp.int32)[None, None, :]
    home = jnp.sum(jnp.where(matches, block_home[None, None, :], 0), axis=2)
    slot, owner = home % NBD, home // NBD
    flip_z = ((owner // 2) % NZ) ^ my_z
    flip_y = (owner // (2 * NZ)) ^ my_y
    late = slot // (NBD // 2)
    at_y = place_of(flip_y, jnp.where(late == 0, 1, 3))
    at_z = place_of(flip_z, jnp.where(late == 0, 1, 3))
    near = owner % 2 == core
    rows = jnp.where(near, at_z * 4 + at_y, 128 // 4 + at_y * 4 + at_z)
    rows = (rows * 4 + late * 64 + slot % 4).astype(jnp.int32)
    log_table = (jnp.log(sample_counts.astype(jnp.float32)) * LOG2E).reshape(
        total_blocks, TP * 2, ROWS
    )
    my_log = lax.dynamic_index_in_dim(log_table, rank * 2 + core, 1, keepdims=False)
    lq = my_log[home].reshape(2 * qblocks, 1, COLS)

    bf16 = jnp.bfloat16
    theirs, their_stat = attend(
        first_kernel,
        (rows[:qblocks].reshape(-1), rank_id),
        other_query,
        lq[:qblocks],
        pieces,
        (),
        (
            jax.ShapeDtypeStruct((qblocks * BLK, E), bf16),
            jax.ShapeDtypeStruct((qblocks, 8, BLK), jnp.float32),
        ),
        (
            pl.BlockSpec((BLK, E), lambda i, *_: (i, 0)),
            pl.BlockSpec((1, 8, BLK), lambda i, *_: (i, 0, 0)),
        ),
        [],
        "attend_other",
    )
    from_other = send(theirs, c=1)
    from_other_stat = send(their_stat, c=1)
    shares = attend(
        second_kernel,
        (rows[qblocks:].reshape(-1), rank_id),
        query,
        lq[qblocks:],
        pieces,
        (from_other, from_other_stat, pos_part),
        (jax.ShapeDtypeStruct((qblocks, BLK + EXTRA, 128), bf16),) * TP,
        (pl.BlockSpec((1, BLK + EXTRA, 128), lambda i, *_: (i, 0, 0)),) * TP,
        [pltpu.VMEM((TP, BLK, 128), bf16)],
        "attend_own",
    )
    parts = [shares[0]] + [send_x(shares[d], d) for d in (1, 2, 3)]
    loss, grad = last(parts, positive_emb)
    return loss.reshape(-1), grad


def solution(mesh):
    placed = (
        P("cat", "tp"),
        P("cat", "tp"),
        P("cat", "tp"),
        P("tp", None),
        P("cat", None),
        P(),
        P(),
    )
    return jax.shard_map(
        local, mesh=mesh, in_specs=placed, out_specs=(P("cat"), P("cat", "tp")), check_vma=False
    )
```

```python
import functools
import math

import jax
import jax.numpy as jnp
from jax import lax
from jax.experimental import pallas as pl
from jax.experimental.pallas import tpu as pltpu
from jax.sharding import PartitionSpec as P

BLK = 256
TP = 4
NY = 4
NZ = 4
E = 512
LOG2E = math.log2(math.e)
LN2 = math.log(2.0)
SCALE = 2.0 / math.sqrt(E)
LOW = -1e30
ROWS = BLK // TP // 2
NBD = 8
PICKS = 64
COLS = PICKS * ROWS
TILE = 512
HID = 1024
EXTRA = 32


def cat_perm(flip_y, flip_z, flip_c):
    def at(y, z, c):
        return (y * NZ + z) * 2 + c

    return [
        (at(y, z, c), at(y ^ flip_y, z ^ flip_z, c ^ flip_c))
        for y in range(NY)
        for z in range(NZ)
        for c in range(2)
    ]


def send(value, y=0, z=0, c=0):
    return lax.ppermute(value, "cat", cat_perm(y, z, c))


def send_x(value, d):
    return lax.ppermute(value, "tp", [(i, (i + d) % TP) for i in range(TP)])


def tower_kernel(core_ref, *refs):
    hidden = refs[0:4]
    mine, theirs = refs[4:8], refs[8]
    out_ref = refs[9]
    core = core_ref[0]
    half = HID // TP // 2
    acc = jnp.zeros((NBD * 2 * ROWS, E), jnp.float32)
    for d in range(TP):
        low = jnp.where(core == 0, mine[d][...], theirs[d])
        high = jnp.where(core == 0, theirs[d], mine[d][...])
        acc += jnp.dot(hidden[d][:, :half], low, preferred_element_type=jnp.float32)
        acc += jnp.dot(hidden[d][:, half:], high, preferred_element_type=jnp.float32)
    out_ref[...] = acc.astype(jnp.bfloat16).reshape(out_ref.shape)


def tower(core, hidden, mine, theirs):
    return pl.pallas_call(
        tower_kernel,
        out_shape=jax.ShapeDtypeStruct((2 * NBD, ROWS, E), jnp.bfloat16),
        in_specs=[pl.BlockSpec(memory_space=pltpu.SMEM)]
        + [pl.BlockSpec(memory_space=pltpu.VMEM)] * 9,
        out_specs=pl.BlockSpec(memory_space=pltpu.VMEM),
        compiler_params=pltpu.CompilerParams(vmem_limit_bytes=40 << 20),
        cost_estimate=pl.CostEstimate(
            flops=2 * 512 * 1024 * 512, bytes_accessed=3 << 20, transcendentals=0
        ),
        name="tower",
    )(core, *hidden, *mine, theirs)


PIECES = 8


def one_block(rank, q_ref, lq_ref, row_ref, table, picked, scores, first):
    for j in range(PICKS):
        picked[pl.ds(j * ROWS, ROWS), :] = table[row_ref[first + j]]
    query = jnp.concatenate(
        [q_ref[lax.rem(rank + TP - s, TP)] for s in range(TP)], axis=1
    )
    top = jnp.full((BLK, 128), LOW, jnp.float32)
    for n in range(COLS // TILE):
        cols = pl.ds(n * TILE, TILE)
        part = lax.dot_general(
            query,
            picked[cols, :],
            (((1,), (1,)), ((), ())),
            preferred_element_type=jnp.float32,
        )
        part = part * (SCALE * LOG2E) - lq_ref[0, :, cols]
        scores[:, cols] = part
        for g in range(TILE // 128):
            top = jnp.maximum(top, part[:, g * 128 : (g + 1) * 128])
    top = jnp.max(top, axis=1, keepdims=True)
    total = jnp.zeros((BLK, 128), jnp.float32)
    acc = jnp.zeros((BLK, E), jnp.float32)
    for n in range(COLS // TILE):
        cols = pl.ds(n * TILE, TILE)
        weight = jnp.exp2(scores[:, cols] - top)
        for g in range(TILE // 128):
            total += weight[:, g * 128 : (g + 1) * 128]
        acc += jnp.dot(
            weight.astype(jnp.bfloat16), picked[cols, :], preferred_element_type=jnp.float32
        )
    return top, jnp.sum(total, axis=1, keepdims=True), acc


def rows_of(top, total):
    lane = lax.broadcasted_iota(jnp.int32, (BLK, 128), 1)
    both = jnp.where(lane == 0, top, jnp.where(lane == 1, total, 0.0))
    return jnp.transpose(both)[:8]


def fill(pieces, table, sems):
    size = table.shape[0] // PIECES
    copies = [
        pltpu.make_async_copy(piece, table.at[pl.ds(n * size, size)], sems.at[n])
        for n, piece in enumerate(pieces)
    ]
    for copy in copies:
        copy.start()
    for copy in copies:
        copy.wait()


def first_kernel(row_ref, rank_ref, q_ref, lq_ref, *refs):
    pieces = refs[:PIECES]
    out_ref, stat_ref, table, picked, scores, sems = refs[PIECES:]
    step = pl.program_id(0)

    @pl.when(step == 0)
    def _():
        fill(pieces, table, sems)

    top, total, acc = one_block(rank_ref[0], q_ref, lq_ref, row_ref, table, picked, scores, step * PICKS)
    out_ref[...] = acc.astype(jnp.bfloat16)
    stat_ref[0] = rows_of(top, total)


def split_rows(row):
    out = []
    for _ in range(3):
        part = row.astype(jnp.bfloat16).astype(jnp.float32)
        out += [part[:, :128], part[:, 128:]]
        row = row - part
    return out


def joined_row(rows):
    halves = [rows[n : n + 1] + (rows[n + 2 : n + 3] + rows[n + 4 : n + 5]) for n in range(2)]
    return jnp.concatenate(halves, axis=1)


def second_kernel(row_ref, rank_ref, q_ref, lq_ref, *refs):
    pieces = refs[:PIECES]
    other_ref, other_stat_ref, pos_ref = refs[PIECES : PIECES + 3]
    outs = refs[PIECES + 3 : PIECES + 7]
    table, picked, scores, sems, quarters = refs[PIECES + 7 :]
    step = pl.program_id(0)

    @pl.when(step == 0)
    def _():
        fill(pieces, table, sems)

    top, total, acc = one_block(rank_ref[0], q_ref, lq_ref, row_ref, table, picked, scores, step * PICKS)
    theirs = jnp.transpose(jnp.concatenate([other_stat_ref[0]] * 16, axis=0))
    their_top, their_total = theirs[:, 0:1], theirs[:, 1:2]
    joint = jnp.maximum(top, their_top)
    mine_by, theirs_by = jnp.exp2(top - joint), jnp.exp2(their_top - joint)
    acc = acc * mine_by + other_ref[...].astype(jnp.float32) * theirs_by
    for s in range(TP):
        quarters[s] = acc[:, s * 128 : (s + 1) * 128].astype(jnp.bfloat16)
    stat = rows_of(joint, total * mine_by + their_total * theirs_by)
    rows = split_rows(stat[0:1]) + split_rows(stat[1:2]) + split_rows(pos_ref[0])
    rows.append(jnp.zeros((EXTRA - len(rows), 128), jnp.float32))
    tail = jnp.concatenate(rows, axis=0).astype(jnp.bfloat16)
    for d in range(TP):
        outs[d][0, :BLK] = quarters[lax.rem(rank_ref[0] + d, TP)]
        outs[d][0, BLK:] = tail


def attend(body, scalars, query, lq, pieces, extra, outs, out_specs, scratch, name):
    blocks = lq.shape[0]
    extra_specs = []
    if extra:
        extra_specs = [
            pl.BlockSpec((BLK, E), lambda i, *_: (i, 0)),
            pl.BlockSpec((1, 8, BLK), lambda i, *_: (i, 0, 0)),
            pl.BlockSpec((1, 1, BLK), lambda i, *_: (i, 0, 0)),
        ]
    return pl.pallas_call(
        body,
        grid_spec=pltpu.PrefetchScalarGridSpec(
            num_scalar_prefetch=len(scalars),
            grid=(blocks,),
            in_specs=[
                pl.BlockSpec((TP, BLK, 128), lambda i, *_: (0, i, 0)),
                pl.BlockSpec((1, 1, COLS), lambda i, *_: (i, 0, 0)),
            ]
            + [pl.BlockSpec(memory_space=pl.ANY)] * PIECES
            + extra_specs,
            out_specs=out_specs,
            scratch_shapes=[
                pltpu.VMEM((256, ROWS, E), jnp.bfloat16),
                pltpu.VMEM((COLS, E), jnp.bfloat16),
                pltpu.VMEM((BLK, COLS), jnp.float32),
                pltpu.SemaphoreType.DMA((PIECES,)),
            ]
            + scratch,
        ),
        out_shape=outs,
        compiler_params=pltpu.CompilerParams(
            dimension_semantics=("arbitrary",), vmem_limit_bytes=24 << 20
        ),
        cost_estimate=pl.CostEstimate(
            flops=blocks * 4 * BLK * COLS * E,
            bytes_accessed=12 << 20,
            transcendentals=blocks * BLK * COLS,
        ),
        name=name,
    )(*scalars, query, lq, *pieces, *extra)


def last_kernel(*refs):
    parts, positive_ref, loss_ref, grad_ref = refs[0:4], *refs[4:]
    tails = [ref[0, BLK:].astype(jnp.float32) for ref in parts]
    tops = [joined_row(tail[0:6]) for tail in tails]
    totals = [joined_row(tail[6:12]) for tail in tails]
    shares = [joined_row(tail[12:18]) for tail in tails]
    pos = (shares[0] + shares[1] + shares[2] + shares[3]) * LOG2E
    joint = pos
    for top in tops:
        joint = jnp.maximum(joint, top)
    total = jnp.exp2(pos - joint)
    for top, one in zip(tops, totals):
        total += one * jnp.exp2(top - joint)
    log_total = joint + jnp.log(total) * LOG2E
    loss_ref[0] = (log_total - pos) * LN2
    factors = [jnp.exp2(top - log_total) * SCALE for top in tops]
    factors.append((jnp.exp2(pos - log_total) - 1.0) * SCALE)
    row = lax.broadcasted_iota(jnp.int32, (128, BLK), 0)
    packed = jnp.zeros((128, BLK), jnp.float32)
    for n, factor in enumerate(factors):
        packed = jnp.where(row == n, factor, packed)
    by = jnp.transpose(packed)
    grad = by[:, 4:5] * positive_ref[...].astype(jnp.float32)
    for n in range(4):
        grad += by[:, n : n + 1] * parts[n][0, :BLK].astype(jnp.float32)
    grad_ref[...] = grad.astype(jnp.bfloat16)


def last(parts, positive):
    blocks = parts[0].shape[0]
    flat = pl.BlockSpec((BLK, 128), lambda i: (i, 0))
    return pl.pallas_call(
        last_kernel,
        grid=(blocks,),
        in_specs=[pl.BlockSpec((1, BLK + EXTRA, 128), lambda i: (i, 0, 0))] * 4 + [flat],
        out_specs=(pl.BlockSpec((1, 1, BLK), lambda i: (i, 0, 0)), flat),
        out_shape=(
            jax.ShapeDtypeStruct((blocks, 1, BLK), jnp.float32),
            jax.ShapeDtypeStruct((blocks * BLK, 128), jnp.bfloat16),
        ),
        compiler_params=pltpu.CompilerParams(vmem_limit_bytes=32 << 20),
        name="last",
    )(*parts, positive)


STREAMS = (
    (("y", 1), ("y", 3), ("z", 1), ("z", 3)),
    (("y", 3), ("y", 1), ("z", 3), ("z", 1)),
    (("z", 1), ("z", 3), ("y", 1), ("y", 3)),
    (("z", 3), ("z", 1), ("y", 3), ("y", 1)),
)


def together(*values):
    return list(lax.optimization_barrier(tuple(values)))


def spread(items, query):
    held = [items[n * 4 : n * 4 + 4] for n in range(4)]
    queries = [query]
    for step in range(4):
        got = [send(h, **{st[step][0]: st[step][1]}) for h, st in zip(held, STREAMS)]
        if step == 3:
            break
        got = together(*got, send_x(query, step + 1), query)
        queries.append(got[4])
        query = got[5]
        held = together(*[jnp.concatenate([h, g]) for h, g in zip(held, got)])
    return held, got, jnp.stack(queries)


def place_of(flipped, first):
    return jnp.where(
        flipped == 0, 0, jnp.where(flipped == 2, 3, jnp.where(flipped == first, 1, 2))
    )


def local(query_emb, positive_emb, item_hidden, item_weight, neg_blocks, block_home, sample_counts):
    rank = lax.axis_index("tp")
    place = lax.axis_index("cat")
    core, my_z, my_y = place % 2, (place // 2) % NZ, place // (2 * NZ)
    qblocks = neg_blocks.shape[0]
    total_blocks = block_home.shape[0]

    core_id = core.reshape(1).astype(jnp.int32)
    rank_id = rank.reshape(1).astype(jnp.int32)
    hidden = item_hidden.reshape(NBD, TP, 2, ROWS, -1)
    keep = lax.dynamic_index_in_dim(hidden, core, 2, keepdims=False)
    give = lax.dynamic_index_in_dim(hidden, 1 - core, 2, keepdims=False)
    half = lax.dynamic_slice_in_dim(item_weight, core * (HID // TP // 2), HID // TP // 2, 0)
    swapped = send(give, c=1)
    mine_w = [half] + [send_x(half, d) for d in (1, 2, 3)]
    both = jnp.concatenate([keep, swapped])

    def piece(d):
        cut = lax.dynamic_index_in_dim(both, (rank + d) % TP, 1, keepdims=False)
        return cut.reshape(2 * NBD * ROWS, -1)

    hiddens = [piece(0)] + [send_x(piece(d), d) for d in (1, 2, 3)]
    theirs_w = send(together(jnp.stack(mine_w), hiddens[1], hiddens[3])[0], c=1)
    picks = jnp.concatenate([send(neg_blocks, c=1), neg_blocks])
    items, late_query, picks = together(
        tower(core_id, hiddens, mine_w, theirs_w), query_emb, picks
    )
    held, got, query = spread(items, late_query)
    pieces = []
    for pair in zip(held, got):
        pieces += list(pair)
    other_query = send(query, c=1)
    pos_part = SCALE * jnp.sum(
        query_emb.astype(jnp.float32) * positive_emb.astype(jnp.float32), axis=1
    ).reshape(qblocks, 1, BLK)

    matches = picks[:, :, None] == jnp.arange(total_blocks, dtype=jnp.int32)[None, None, :]
    home = jnp.sum(jnp.where(matches, block_home[None, None, :], 0), axis=2)
    slot, owner = home % NBD, home // NBD
    flip_z = ((owner // 2) % NZ) ^ my_z
    flip_y = (owner // (2 * NZ)) ^ my_y
    late = slot // (NBD // 2)
    at_y = place_of(flip_y, jnp.where(late == 0, 1, 3))
    at_z = place_of(flip_z, jnp.where(late == 0, 1, 3))
    near = owner % 2 == core
    rows = jnp.where(near, at_z * 4 + at_y, 128 // 4 + at_y * 4 + at_z)
    rows = (rows * 4 + late * 64 + slot % 4).astype(jnp.int32)
    log_table = (jnp.log(sample_counts.astype(jnp.float32)) * LOG2E).reshape(
        total_blocks, TP * 2, ROWS
    )
    my_log = lax.dynamic_index_in_dim(log_table, rank * 2 + core, 1, keepdims=False)
    lq = my_log[home].reshape(2 * qblocks, 1, COLS)

    first_rows, own_rows = rows[:qblocks].reshape(-1), rows[qblocks:].reshape(-1)
    first_lq, own_lq = lq[:qblocks], lq[qblocks:]
    pieces[-1], pos_part, first_rows, own_rows, first_lq, own_lq = together(
        pieces[-1], pos_part, first_rows, own_rows, first_lq, own_lq
    )

    bf16 = jnp.bfloat16
    theirs, their_stat = attend(
        first_kernel,
        (first_rows, rank_id),
        other_query,
        first_lq,
        pieces,
        (),
        (
            jax.ShapeDtypeStruct((qblocks * BLK, E), bf16),
            jax.ShapeDtypeStruct((qblocks, 8, BLK), jnp.float32),
        ),
        (
            pl.BlockSpec((BLK, E), lambda i, *_: (i, 0)),
            pl.BlockSpec((1, 8, BLK), lambda i, *_: (i, 0, 0)),
        ),
        [],
        "attend_other",
    )
    from_other = send(theirs, c=1)
    from_other_stat = send(their_stat, c=1)
    shares = attend(
        second_kernel,
        (own_rows, rank_id),
        query,
        own_lq,
        pieces,
        (from_other, from_other_stat, pos_part),
        (jax.ShapeDtypeStruct((qblocks, BLK + EXTRA, 128), bf16),) * TP,
        (pl.BlockSpec((1, BLK + EXTRA, 128), lambda i, *_: (i, 0, 0)),) * TP,
        [pltpu.VMEM((TP, BLK, 128), bf16)],
        "attend_own",
    )
    parts = [shares[0]] + [send_x(shares[d], d) for d in (1, 2, 3)]
    loss, grad = last(parts, positive_emb)
    return loss.reshape(-1), grad


def solution(mesh):
    placed = (
        P("cat", "tp"),
        P("cat", "tp"),
        P("cat", "tp"),
        P("tp", None),
        P("cat", None),
        P(),
        P(),
    )
    return jax.shard_map(
        local, mesh=mesh, in_specs=placed, out_specs=(P("cat"), P("cat", "tp")), check_vma=False
    )
```

```python
import functools
import math

import jax
import jax.numpy as jnp
from jax import lax
from jax.experimental import pallas as pl
from jax.experimental.pallas import tpu as pltpu
from jax.sharding import PartitionSpec as P

BLK = 256
TP = 4
NY = 4
NZ = 4
E = 512
LOG2E = math.log2(math.e)
LN2 = math.log(2.0)
SCALE = 2.0 / math.sqrt(E)
LOW = -1e30
ROWS = BLK // TP // 2
NBD = 8
PICKS = 64
COLS = PICKS * ROWS
TILE = 512
HID = 1024
EXTRA = 32


def cat_perm(flip_y, flip_z, flip_c):
    def at(y, z, c):
        return (y * NZ + z) * 2 + c

    return [
        (at(y, z, c), at(y ^ flip_y, z ^ flip_z, c ^ flip_c))
        for y in range(NY)
        for z in range(NZ)
        for c in range(2)
    ]


def send(value, y=0, z=0, c=0):
    return lax.ppermute(value, "cat", cat_perm(y, z, c))


def send_x(value, d):
    return lax.ppermute(value, "tp", [(i, (i + d) % TP) for i in range(TP)])


def tower_kernel(core_ref, *refs):
    hidden = refs[0:4]
    mine, theirs = refs[4:8], refs[8]
    out_ref = refs[9]
    core = core_ref[0]
    half = HID // TP // 2
    acc = jnp.zeros((NBD * 2 * ROWS, E), jnp.float32)
    for d in range(TP):
        low = jnp.where(core == 0, mine[d][...], theirs[d])
        high = jnp.where(core == 0, theirs[d], mine[d][...])
        acc += jnp.dot(hidden[d][:, :half], low, preferred_element_type=jnp.float32)
        acc += jnp.dot(hidden[d][:, half:], high, preferred_element_type=jnp.float32)
    out_ref[...] = acc.astype(jnp.bfloat16).reshape(out_ref.shape)


def tower(core, hidden, mine, theirs):
    return pl.pallas_call(
        tower_kernel,
        out_shape=jax.ShapeDtypeStruct((2 * NBD, ROWS, E), jnp.bfloat16),
        in_specs=[pl.BlockSpec(memory_space=pltpu.SMEM)]
        + [pl.BlockSpec(memory_space=pltpu.VMEM)] * 9,
        out_specs=pl.BlockSpec(memory_space=pltpu.VMEM),
        compiler_params=pltpu.CompilerParams(vmem_limit_bytes=40 << 20),
        cost_estimate=pl.CostEstimate(
            flops=2 * 512 * 1024 * 512, bytes_accessed=3 << 20, transcendentals=0
        ),
        name="tower",
    )(core, *hidden, *mine, theirs)


PART = 2


def one_block(rank, block, base, q_ref, lq_ref, row_ref, table, picked, scores):
    for j in range(PICKS):
        picked[pl.ds(j * ROWS, ROWS), :] = table[row_ref[(base + block) * PICKS + j]]
    here = pl.ds(pl.multiple_of(block * BLK, BLK), BLK)
    query = jnp.concatenate([q_ref[lax.rem(rank + TP - s, TP), here] for s in range(TP)], axis=1)
    top = jnp.full((BLK, 128), LOW, jnp.float32)
    for n in range(COLS // TILE):
        cols = pl.ds(n * TILE, TILE)
        part = lax.dot_general(
            query,
            picked[cols, :],
            (((1,), (1,)), ((), ())),
            preferred_element_type=jnp.float32,
        )
        part = part * (SCALE * LOG2E) - lq_ref[pl.ds(base + block, 1), cols]
        scores[:, cols] = part
        for g in range(TILE // 128):
            top = jnp.maximum(top, part[:, g * 128 : (g + 1) * 128])
    top = jnp.max(top, axis=1, keepdims=True)
    total = jnp.zeros((BLK, 128), jnp.float32)
    acc = jnp.zeros((BLK, E), jnp.float32)
    for n in range(COLS // TILE):
        cols = pl.ds(n * TILE, TILE)
        weight = jnp.exp2(scores[:, cols] - top)
        for g in range(TILE // 128):
            total += weight[:, g * 128 : (g + 1) * 128]
        acc += jnp.dot(
            weight.astype(jnp.bfloat16), picked[cols, :], preferred_element_type=jnp.float32
        )
    return top, jnp.sum(total, axis=1, keepdims=True), acc


def rows_of(top, total):
    lane = lax.broadcasted_iota(jnp.int32, (BLK, 128), 1)
    both = jnp.where(lane == 0, top, jnp.where(lane == 1, total, 0.0))
    return jnp.transpose(both)[:8]


def pack_kernel(places, *refs):
    count = len(places)
    pieces, table, sems = refs[:count], refs[-2], refs[-1]
    copies = [
        pltpu.make_async_copy(piece, table.at[pl.ds(place * 16, 16)], sems.at[n])
        for n, (piece, place) in enumerate(zip(pieces, places))
    ]
    for copy in copies:
        copy.start()
    for copy in copies:
        copy.wait()


def pack(pieces, places):
    return pl.pallas_call(
        functools.partial(pack_kernel, places),
        out_shape=jax.ShapeDtypeStruct((256, ROWS, E), jnp.bfloat16),
        in_specs=[pl.BlockSpec(memory_space=pl.ANY)] * len(pieces),
        out_specs=pl.BlockSpec(memory_space=pltpu.VMEM),
        scratch_shapes=[pltpu.SemaphoreType.DMA((len(pieces),))],
        compiler_params=pltpu.CompilerParams(vmem_limit_bytes=12 << 20),
        cost_estimate=pl.CostEstimate(flops=0, bytes_accessed=16 << 20, transcendentals=0),
        name="pack",
    )(*pieces)


def first_kernel(start, row_ref, rank_ref, q_ref, lq_ref, table, *refs):
    out_ref, stat_ref, picked, scores = refs

    @pl.loop(0, PART)
    def _(n):
        top, total, acc = one_block(
            rank_ref[0], start + n, 0, q_ref, lq_ref, row_ref, table, picked, scores
        )
        out_ref[n] = acc.astype(jnp.bfloat16)
        stat_ref[n] = rows_of(top, total)


def split_rows(row):
    out = []
    for _ in range(3):
        part = row.astype(jnp.bfloat16).astype(jnp.float32)
        out += [part[:, :128], part[:, 128:]]
        row = row - part
    return out


def joined_row(rows):
    halves = [rows[n : n + 1] + (rows[n + 2 : n + 3] + rows[n + 4 : n + 5]) for n in range(2)]
    return jnp.concatenate(halves, axis=1)


def second_kernel(start, row_ref, rank_ref, q_ref, lq_ref, table, *refs):
    other_ref, other_stat_ref, pos_ref = refs[:3]
    outs = refs[3:7]
    picked, scores, quarters = refs[7:]

    @pl.loop(0, PART)
    def _(n):
        top, total, acc = one_block(
            rank_ref[0], start + n, 2 * PART, q_ref, lq_ref, row_ref, table, picked, scores
        )
        theirs = jnp.transpose(jnp.concatenate([other_stat_ref[n]] * 16, axis=0))
        their_top, their_total = theirs[:, 0:1], theirs[:, 1:2]
        joint = jnp.maximum(top, their_top)
        mine_by, theirs_by = jnp.exp2(top - joint), jnp.exp2(their_top - joint)
        acc = acc * mine_by + other_ref[n].astype(jnp.float32) * theirs_by
        for s in range(TP):
            quarters[s] = acc[:, s * 128 : (s + 1) * 128].astype(jnp.bfloat16)
        stat = rows_of(joint, total * mine_by + their_total * theirs_by)
        rows = split_rows(stat[0:1]) + split_rows(stat[1:2]) + split_rows(pos_ref[start + n])
        rows.append(jnp.zeros((EXTRA - len(rows), 128), jnp.float32))
        tail = jnp.concatenate(rows, axis=0).astype(jnp.bfloat16)
        for d in range(TP):
            outs[d][n, :BLK] = quarters[lax.rem(rank_ref[0] + d, TP)]
            outs[d][n, BLK:] = tail


def attend(body, start, scalars, inputs, outs, scratch, name):
    vmem = pl.BlockSpec(memory_space=pltpu.VMEM)
    return pl.pallas_call(
        functools.partial(body, start),
        in_specs=[pl.BlockSpec(memory_space=pltpu.SMEM)] * len(scalars) + [vmem] * len(inputs),
        out_specs=(vmem,) * len(outs),
        out_shape=outs,
        scratch_shapes=[
            pltpu.VMEM((COLS, E), jnp.bfloat16),
            pltpu.VMEM((BLK, COLS), jnp.float32),
        ]
        + scratch,
        compiler_params=pltpu.CompilerParams(vmem_limit_bytes=32 << 20),
        cost_estimate=pl.CostEstimate(
            flops=PART * 4 * BLK * COLS * E,
            bytes_accessed=2 << 20,
            transcendentals=PART * BLK * COLS,
        ),
        name=name,
    )(*scalars, *inputs)


def last_kernel(*refs):
    positive_ref, loss_ref, grad_ref = refs[8:]
    for block in range(2 * PART):
        parts = refs[0:4] if block < PART else refs[4:8]
        finish(parts, block % PART, block, positive_ref, loss_ref, grad_ref)


def finish(parts, n, block, positive_ref, loss_ref, grad_ref):
    here = pl.ds(block * BLK, BLK)
    tails = [ref[n, BLK:].astype(jnp.float32) for ref in parts]
    tops = [joined_row(tail[0:6]) for tail in tails]
    totals = [joined_row(tail[6:12]) for tail in tails]
    shares = [joined_row(tail[12:18]) for tail in tails]
    pos = (shares[0] + shares[1] + shares[2] + shares[3]) * LOG2E
    joint = pos
    for top in tops:
        joint = jnp.maximum(joint, top)
    total = jnp.exp2(pos - joint)
    for top, one in zip(tops, totals):
        total += one * jnp.exp2(top - joint)
    log_total = joint + jnp.log(total) * LOG2E
    loss_ref[block] = (log_total - pos) * LN2
    factors = [jnp.exp2(top - log_total) * SCALE for top in tops]
    factors.append((jnp.exp2(pos - log_total) - 1.0) * SCALE)
    row = lax.broadcasted_iota(jnp.int32, (128, BLK), 0)
    packed = jnp.zeros((128, BLK), jnp.float32)
    for at, factor in enumerate(factors):
        packed = jnp.where(row == at, factor, packed)
    by = jnp.transpose(packed)
    grad = by[:, 4:5] * positive_ref[here].astype(jnp.float32)
    for s in range(4):
        grad += by[:, s : s + 1] * parts[s][n, :BLK].astype(jnp.float32)
    grad_ref[here] = grad.astype(jnp.bfloat16)


def last(parts, positive):
    vmem = pl.BlockSpec(memory_space=pltpu.VMEM)
    blocks = positive.shape[0] // BLK
    return pl.pallas_call(
        last_kernel,
        in_specs=[vmem] * 9,
        out_specs=(vmem, vmem),
        out_shape=(
            jax.ShapeDtypeStruct((blocks, 1, BLK), jnp.float32),
            jax.ShapeDtypeStruct((blocks * BLK, 128), jnp.bfloat16),
        ),
        compiler_params=pltpu.CompilerParams(vmem_limit_bytes=16 << 20),
        name="last",
    )(*parts, positive)


STREAMS = (
    (("y", 1), ("y", 3), ("z", 1), ("z", 3)),
    (("y", 3), ("y", 1), ("z", 3), ("z", 1)),
    (("z", 1), ("z", 3), ("y", 1), ("y", 3)),
    (("z", 3), ("z", 1), ("y", 3), ("y", 1)),
)


def together(*values):
    return list(lax.optimization_barrier(tuple(values)))


def spread(items, query):
    held = [items[n * 4 : n * 4 + 4] for n in range(4)]
    queries = [query]
    for step in range(3):
        got = [send(h, **{st[step][0]: st[step][1]}) for h, st in zip(held, STREAMS)]
        got = together(*got, send_x(query, step + 1), query)
        queries.append(got[4])
        query = got[5]
        if step < 2:
            held = together(*[jnp.concatenate([h, g]) for h, g in zip(held, got)])
    third = got[:4]
    fourth = [send(h, **{st[3][0]: st[3][1]}) for h, st in zip(held, STREAMS)]
    fifth = [send(h, **{st[3][0]: st[3][1]}) for h, st in zip(third, STREAMS)]
    places = (0, 4, 8, 12, 1, 5, 9, 13, 2, 6, 10, 14, 3, 7, 11, 15)
    table = pack(held + third + fourth + fifth, places)
    return table, jnp.stack(queries)


def place_of(flipped, first):
    return jnp.where(
        flipped == 0, 0, jnp.where(flipped == 2, 3, jnp.where(flipped == first, 1, 2))
    )


def local(query_emb, positive_emb, item_hidden, item_weight, neg_blocks, block_home, sample_counts):
    rank = lax.axis_index("tp")
    place = lax.axis_index("cat")
    core, my_z, my_y = place % 2, (place // 2) % NZ, place // (2 * NZ)
    qblocks = neg_blocks.shape[0]
    total_blocks = block_home.shape[0]

    core_id = core.reshape(1).astype(jnp.int32)
    rank_id = rank.reshape(1).astype(jnp.int32)
    hidden = item_hidden.reshape(NBD, TP, 2, ROWS, -1)
    keep = lax.dynamic_index_in_dim(hidden, core, 2, keepdims=False)
    give = lax.dynamic_index_in_dim(hidden, 1 - core, 2, keepdims=False)
    half = lax.dynamic_slice_in_dim(item_weight, core * (HID // TP // 2), HID // TP // 2, 0)
    swapped = send(give, c=1)
    mine_w = [half] + [send_x(half, d) for d in (1, 2, 3)]
    both = jnp.concatenate([keep, swapped])

    def piece(d):
        cut = lax.dynamic_index_in_dim(both, (rank + d) % TP, 1, keepdims=False)
        return cut.reshape(2 * NBD * ROWS, -1)

    hiddens = [piece(0)] + [send_x(piece(d), d) for d in (1, 2, 3)]
    theirs_w = send(together(jnp.stack(mine_w), hiddens[1], hiddens[3])[0], c=1)
    picks = jnp.concatenate([send(neg_blocks, c=1), neg_blocks])
    items, late_query, picks = together(
        tower(core_id, hiddens, mine_w, theirs_w), query_emb, picks
    )
    table, query = spread(items, late_query)
    other_query = send(query, c=1)
    pos_part = SCALE * jnp.sum(
        query_emb.astype(jnp.float32) * positive_emb.astype(jnp.float32), axis=1
    ).reshape(qblocks, 1, BLK)

    matches = picks[:, :, None] == jnp.arange(total_blocks, dtype=jnp.int32)[None, None, :]
    home = jnp.sum(jnp.where(matches, block_home[None, None, :], 0), axis=2)
    slot, owner = home % NBD, home // NBD
    flip_z = ((owner // 2) % NZ) ^ my_z
    flip_y = (owner // (2 * NZ)) ^ my_y
    late = slot // (NBD // 2)
    at_y = place_of(flip_y, jnp.where(late == 0, 1, 3))
    at_z = place_of(flip_z, jnp.where(late == 0, 1, 3))
    near = owner % 2 == core
    rows = jnp.where(near, at_z * 4 + at_y, 128 // 4 + at_y * 4 + at_z)
    rows = (rows * 4 + late * 64 + slot % 4).astype(jnp.int32)
    log_table = (jnp.log(sample_counts.astype(jnp.float32)) * LOG2E).reshape(
        total_blocks, TP * 2, ROWS
    )
    my_log = lax.dynamic_index_in_dim(log_table, rank * 2 + core, 1, keepdims=False)
    lq = my_log[home].reshape(2 * qblocks, COLS)

    rows = rows.reshape(-1)
    table, pos_part, rows, lq = together(table, pos_part, rows, lq)

    raw = (
        jax.ShapeDtypeStruct((PART, BLK, E), jnp.bfloat16),
        jax.ShapeDtypeStruct((PART, 8, BLK), jnp.float32),
    )
    share = jax.ShapeDtypeStruct((PART, BLK + EXTRA, 128), jnp.bfloat16)
    others = []
    for start in (0, PART):
        made = attend(
            first_kernel,
            start,
            (rows, rank_id),
            (other_query, lq, table),
            raw,
            [],
            "attend_other",
        )
        others.append([send(one, c=1) for one in made])
    parts = []
    for start, other in zip((0, PART), others):
        shares = attend(
            second_kernel,
            start,
            (rows, rank_id),
            (query, lq, table, *other, pos_part),
            (share,) * TP,
            [pltpu.VMEM((TP, BLK, 128), jnp.bfloat16)],
            "attend_own",
        )
        parts += [shares[0]] + [send_x(shares[d], d) for d in (1, 2, 3)]
    loss, grad = last(parts, positive_emb)
    return loss.reshape(-1), grad


def solution(mesh):
    placed = (
        P("cat", "tp"),
        P("cat", "tp"),
        P("cat", "tp"),
        P("tp", None),
        P("cat", None),
        P(),
        P(),
    )
    return jax.shard_map(
        local, mesh=mesh, in_specs=placed, out_specs=(P("cat"), P("cat", "tp")), check_vma=False
    )
```

```python
import functools
import math

import jax
import jax.numpy as jnp
from jax import lax
from jax.experimental import pallas as pl
from jax.experimental.pallas import tpu as pltpu
from jax.sharding import PartitionSpec as P

BLK = 256
TP = 4
NY = 4
NZ = 4
E = 512
LOG2E = math.log2(math.e)
LN2 = math.log(2.0)
SCALE = 2.0 / math.sqrt(E)
LOW = -1e30
ROWS = BLK // TP // 2
NBD = 8
PICKS = 64
COLS = PICKS * ROWS
TILE = 512
HID = 1024
EXTRA = 32


def cat_perm(flip_y, flip_z, flip_c):
    def at(y, z, c):
        return (y * NZ + z) * 2 + c

    return [
        (at(y, z, c), at(y ^ flip_y, z ^ flip_z, c ^ flip_c))
        for y in range(NY)
        for z in range(NZ)
        for c in range(2)
    ]


def send(value, y=0, z=0, c=0):
    return lax.ppermute(value, "cat", cat_perm(y, z, c))


def send_x(value, d):
    return lax.ppermute(value, "tp", [(i, (i + d) % TP) for i in range(TP)])


def tower_kernel(core_ref, *refs):
    hidden = refs[0:4]
    mine, theirs = refs[4:8], refs[8]
    out_ref = refs[9]
    core = core_ref[0]
    half = HID // TP // 2
    acc = jnp.zeros((NBD * 2 * ROWS, E), jnp.float32)
    for d in range(TP):
        low = jnp.where(core == 0, mine[d][...], theirs[d])
        high = jnp.where(core == 0, theirs[d], mine[d][...])
        acc += jnp.dot(hidden[d][:, :half], low, preferred_element_type=jnp.float32)
        acc += jnp.dot(hidden[d][:, half:], high, preferred_element_type=jnp.float32)
    out_ref[...] = acc.astype(jnp.bfloat16).reshape(out_ref.shape)


def tower(core, hidden, mine, theirs):
    return pl.pallas_call(
        tower_kernel,
        out_shape=jax.ShapeDtypeStruct((2 * NBD, ROWS, E), jnp.bfloat16),
        in_specs=[pl.BlockSpec(memory_space=pltpu.SMEM)]
        + [pl.BlockSpec(memory_space=pltpu.VMEM)] * 9,
        out_specs=pl.BlockSpec(memory_space=pltpu.VMEM),
        compiler_params=pltpu.CompilerParams(vmem_limit_bytes=40 << 20),
        cost_estimate=pl.CostEstimate(
            flops=2 * 512 * 1024 * 512, bytes_accessed=3 << 20, transcendentals=0
        ),
        name="tower",
    )(core, *hidden, *mine, theirs)


PART = 2


def one_block(rank, block, base, q_ref, lq_ref, row_ref, table, picked, scores):
    for j in range(PICKS):
        picked[pl.ds(j * ROWS, ROWS), :] = table[row_ref[(base + block) * PICKS + j]]
    here = pl.ds(block * BLK, BLK)
    query = jnp.concatenate([q_ref[lax.rem(rank + TP - s, TP), here] for s in range(TP)], axis=1)
    top = jnp.full((BLK, 128), LOW, jnp.float32)
    for n in range(COLS // TILE):
        cols = pl.ds(n * TILE, TILE)
        part = lax.dot_general(
            query,
            picked[cols, :],
            (((1,), (1,)), ((), ())),
            preferred_element_type=jnp.float32,
        )
        part = part * (SCALE * LOG2E) - lq_ref[pl.ds(base + block, 1), cols]
        scores[:, cols] = part
        for g in range(TILE // 128):
            top = jnp.maximum(top, part[:, g * 128 : (g + 1) * 128])
    top = jnp.max(top, axis=1, keepdims=True)
    total = jnp.zeros((BLK, 128), jnp.float32)
    acc = jnp.zeros((BLK, E), jnp.float32)
    for n in range(COLS // TILE):
        cols = pl.ds(n * TILE, TILE)
        weight = jnp.exp2(scores[:, cols] - top)
        for g in range(TILE // 128):
            total += weight[:, g * 128 : (g + 1) * 128]
        acc += jnp.dot(
            weight.astype(jnp.bfloat16), picked[cols, :], preferred_element_type=jnp.float32
        )
    return top, jnp.sum(total, axis=1, keepdims=True), acc


def rows_of(top, total):
    lane = lax.broadcasted_iota(jnp.int32, (BLK, 128), 1)
    both = jnp.where(lane == 0, top, jnp.where(lane == 1, total, 0.0))
    return jnp.transpose(both)[:8]


def pack_kernel(places, *refs):
    count = len(places)
    pieces, table, sems = refs[:count], refs[-2], refs[-1]
    copies = [
        pltpu.make_async_copy(piece, table.at[pl.ds(place * 16, 16)], sems.at[n])
        for n, (piece, place) in enumerate(zip(pieces, places))
    ]
    for copy in copies:
        copy.start()
    for copy in copies:
        copy.wait()


def pack(pieces, places, table=None):
    given = () if table is None else (table,)
    vmem = pl.BlockSpec(memory_space=pltpu.VMEM)
    return pl.pallas_call(
        functools.partial(pack_kernel, places),
        out_shape=jax.ShapeDtypeStruct((256, ROWS, E), jnp.bfloat16),
        in_specs=[pl.BlockSpec(memory_space=pl.ANY)] * len(pieces) + [vmem] * len(given),
        out_specs=vmem,
        scratch_shapes=[pltpu.SemaphoreType.DMA((len(pieces),))],
        input_output_aliases={len(pieces): 0} if given else {},
        compiler_params=pltpu.CompilerParams(vmem_limit_bytes=20 << 20),
        cost_estimate=pl.CostEstimate(flops=0, bytes_accessed=8 << 20, transcendentals=0),
        name="pack",
    )(*pieces, *given)


def first_kernel(start, row_ref, rank_ref, q_ref, lq_ref, table, *refs):
    out_ref, stat_ref, picked, scores = refs

    for n in range(PART):
        top, total, acc = one_block(
            rank_ref[0], start + n, 0, q_ref, lq_ref, row_ref, table, picked.at[n], scores.at[n]
        )
        out_ref[n] = acc.astype(jnp.bfloat16)
        stat_ref[n] = rows_of(top, total)


def split_rows(row):
    out = []
    for _ in range(3):
        part = row.astype(jnp.bfloat16).astype(jnp.float32)
        out += [part[:, :128], part[:, 128:]]
        row = row - part
    return out


def joined_row(rows):
    halves = [rows[n : n + 1] + (rows[n + 2 : n + 3] + rows[n + 4 : n + 5]) for n in range(2)]
    return jnp.concatenate(halves, axis=1)


def second_kernel(start, row_ref, rank_ref, q_ref, lq_ref, table, *refs):
    other_ref, other_stat_ref, pos_ref = refs[:3]
    outs = refs[3:7]
    picked, scores, quarters = refs[7:]

    for n in range(PART):
        top, total, acc = one_block(
            rank_ref[0], start + n, 2 * PART, q_ref, lq_ref, row_ref, table, picked.at[n], scores.at[n]
        )
        theirs = jnp.transpose(jnp.concatenate([other_stat_ref[n]] * 16, axis=0))
        their_top, their_total = theirs[:, 0:1], theirs[:, 1:2]
        joint = jnp.maximum(top, their_top)
        mine_by, theirs_by = jnp.exp2(top - joint), jnp.exp2(their_top - joint)
        acc = acc * mine_by + other_ref[n].astype(jnp.float32) * theirs_by
        for s in range(TP):
            quarters[s] = acc[:, s * 128 : (s + 1) * 128].astype(jnp.bfloat16)
        stat = rows_of(joint, total * mine_by + their_total * theirs_by)
        rows = split_rows(stat[0:1]) + split_rows(stat[1:2]) + split_rows(pos_ref[start + n])
        rows.append(jnp.zeros((EXTRA - len(rows), 128), jnp.float32))
        tail = jnp.concatenate(rows, axis=0).astype(jnp.bfloat16)
        for d in range(TP):
            outs[d][n, :BLK] = quarters[lax.rem(rank_ref[0] + d, TP)]
            outs[d][n, BLK:] = tail


def attend(body, start, scalars, inputs, outs, scratch, name):
    vmem = pl.BlockSpec(memory_space=pltpu.VMEM)
    return pl.pallas_call(
        functools.partial(body, start),
        in_specs=[pl.BlockSpec(memory_space=pltpu.SMEM)] * len(scalars) + [vmem] * len(inputs),
        out_specs=(vmem,) * len(outs),
        out_shape=outs,
        scratch_shapes=[
            pltpu.VMEM((PART, COLS, E), jnp.bfloat16),
            pltpu.VMEM((PART, BLK, COLS), jnp.float32),
        ]
        + scratch,
        compiler_params=pltpu.CompilerParams(vmem_limit_bytes=32 << 20),
        cost_estimate=pl.CostEstimate(
            flops=PART * 4 * BLK * COLS * E,
            bytes_accessed=2 << 20,
            transcendentals=PART * BLK * COLS,
        ),
        name=name,
    )(*scalars, *inputs)


def last_kernel(*refs):
    positive_ref, loss_ref, grad_ref = refs[8:]
    for block in range(2 * PART):
        parts = refs[0:4] if block < PART else refs[4:8]
        finish(parts, block % PART, block, positive_ref, loss_ref, grad_ref)


def finish(parts, n, block, positive_ref, loss_ref, grad_ref):
    here = pl.ds(block * BLK, BLK)
    tails = [ref[n, BLK:].astype(jnp.float32) for ref in parts]
    tops = [joined_row(tail[0:6]) for tail in tails]
    totals = [joined_row(tail[6:12]) for tail in tails]
    shares = [joined_row(tail[12:18]) for tail in tails]
    pos = (shares[0] + shares[1] + shares[2] + shares[3]) * LOG2E
    joint = pos
    for top in tops:
        joint = jnp.maximum(joint, top)
    total = jnp.exp2(pos - joint)
    for top, one in zip(tops, totals):
        total += one * jnp.exp2(top - joint)
    log_total = joint + jnp.log(total) * LOG2E
    loss_ref[block] = (log_total - pos) * LN2
    factors = [jnp.exp2(top - log_total) * SCALE for top in tops]
    factors.append((jnp.exp2(pos - log_total) - 1.0) * SCALE)
    row = lax.broadcasted_iota(jnp.int32, (128, BLK), 0)
    packed = jnp.zeros((128, BLK), jnp.float32)
    for at, factor in enumerate(factors):
        packed = jnp.where(row == at, factor, packed)
    by = jnp.transpose(packed)
    grad = by[:, 4:5] * positive_ref[here].astype(jnp.float32)
    for s in range(4):
        grad += by[:, s : s + 1] * parts[s][n, :BLK].astype(jnp.float32)
    grad_ref[here] = grad.astype(jnp.bfloat16)


def last(parts, positive):
    vmem = pl.BlockSpec(memory_space=pltpu.VMEM)
    blocks = positive.shape[0] // BLK
    return pl.pallas_call(
        last_kernel,
        in_specs=[vmem] * 9,
        out_specs=(vmem, vmem),
        out_shape=(
            jax.ShapeDtypeStruct((blocks, 1, BLK), jnp.float32),
            jax.ShapeDtypeStruct((blocks * BLK, 128), jnp.bfloat16),
        ),
        compiler_params=pltpu.CompilerParams(vmem_limit_bytes=16 << 20),
        name="last",
    )(*parts, positive)


STREAMS = (
    (("y", 1), ("y", 3), ("z", 1), ("z", 3)),
    (("y", 3), ("y", 1), ("z", 3), ("z", 1)),
    (("z", 1), ("z", 3), ("y", 1), ("y", 3)),
    (("z", 3), ("z", 1), ("y", 3), ("y", 1)),
)


def together(*values):
    return list(lax.optimization_barrier(tuple(values)))


def spread(items, query):
    held = [items[n * 4 : n * 4 + 4] for n in range(4)]
    queries = [query]
    for step in range(3):
        got = [send(h, **{st[step][0]: st[step][1]}) for h, st in zip(held, STREAMS)]
        if step > 0:
            queries.append(send_x(query, step))
            got.append(queries.pop())
        got = together(*got, query)
        query = got.pop()
        queries += got[4:]
        if step < 2:
            held = together(*[jnp.concatenate([h, g]) for h, g in zip(held, got)])
    queries.append(send_x(query, 3))
    third = got[:4]
    fourth = [send(h, **{st[3][0]: st[3][1]}) for h, st in zip(held, STREAMS)]
    fifth = [send(h, **{st[3][0]: st[3][1]}) for h, st in zip(third, STREAMS)]
    table = pack(held + third, (0, 4, 8, 12, 1, 5, 9, 13))
    table = pack(fourth + fifth, (2, 6, 10, 14, 3, 7, 11, 15), table)
    return table, jnp.stack(queries)


def place_of(flipped, first):
    return jnp.where(
        flipped == 0, 0, jnp.where(flipped == 2, 3, jnp.where(flipped == first, 1, 2))
    )


def local(query_emb, positive_emb, item_hidden, item_weight, neg_blocks, block_home, sample_counts):
    rank = lax.axis_index("tp")
    place = lax.axis_index("cat")
    core, my_z, my_y = place % 2, (place // 2) % NZ, place // (2 * NZ)
    qblocks = neg_blocks.shape[0]
    total_blocks = block_home.shape[0]

    core_id = core.reshape(1).astype(jnp.int32)
    rank_id = rank.reshape(1).astype(jnp.int32)
    hidden = item_hidden.reshape(NBD, TP, 2, ROWS, -1)
    keep = lax.dynamic_index_in_dim(hidden, core, 2, keepdims=False)
    give = lax.dynamic_index_in_dim(hidden, 1 - core, 2, keepdims=False)
    half = lax.dynamic_slice_in_dim(item_weight, core * (HID // TP // 2), HID // TP // 2, 0)
    swapped = send(give, c=1)
    mine_w = [half] + [send_x(half, d) for d in (1, 2, 3)]
    both = jnp.concatenate([keep, swapped])

    def piece(d):
        cut = lax.dynamic_index_in_dim(both, (rank + d) % TP, 1, keepdims=False)
        return cut.reshape(2 * NBD * ROWS, -1)

    hiddens = [piece(0)] + [send_x(piece(d), d) for d in (1, 2, 3)]
    theirs_w = send(together(jnp.stack(mine_w), hiddens[1], hiddens[3])[0], c=1)
    picks = jnp.concatenate([send(neg_blocks, c=1), neg_blocks])
    items, late_query, picks = together(
        tower(core_id, hiddens, mine_w, theirs_w), query_emb, picks
    )
    table, query = spread(items, late_query)
    other_query = send(query, c=1)
    pos_part = SCALE * jnp.sum(
        query_emb.astype(jnp.float32) * positive_emb.astype(jnp.float32), axis=1
    ).reshape(qblocks, 1, BLK)

    matches = picks[:, :, None] == jnp.arange(total_blocks, dtype=jnp.int32)[None, None, :]
    home = jnp.sum(jnp.where(matches, block_home[None, None, :], 0), axis=2)
    slot, owner = home % NBD, home // NBD
    flip_z = ((owner // 2) % NZ) ^ my_z
    flip_y = (owner // (2 * NZ)) ^ my_y
    late = slot // (NBD // 2)
    at_y = place_of(flip_y, jnp.where(late == 0, 1, 3))
    at_z = place_of(flip_z, jnp.where(late == 0, 1, 3))
    near = owner % 2 == core
    rows = jnp.where(near, at_z * 4 + at_y, 128 // 4 + at_y * 4 + at_z)
    rows = (rows * 4 + late * 64 + slot % 4).astype(jnp.int32)
    count_rows = sample_counts.reshape(2 * total_blocks, 128)[home.reshape(-1) * 2 + rank // 2]
    counts = lax.dynamic_slice_in_dim(count_rows, (rank % 2 * 2 + core) * ROWS, ROWS, 1)
    lq = (jnp.log(counts.astype(jnp.float32)) * LOG2E).reshape(2 * qblocks, COLS)

    rows = rows.reshape(-1)
    table, pos_part, rows, lq = together(table, pos_part, rows, lq)

    raw = (
        jax.ShapeDtypeStruct((PART, BLK, E), jnp.bfloat16),
        jax.ShapeDtypeStruct((PART, 8, BLK), jnp.float32),
    )
    share = jax.ShapeDtypeStruct((PART, BLK + EXTRA, 128), jnp.bfloat16)
    others = []
    for start in (0, PART):
        made = attend(
            first_kernel,
            start,
            (rows, rank_id),
            (other_query, lq, table),
            raw,
            [],
            "attend_other",
        )
        others.append([send(one, c=1) for one in made])
    parts = []
    for start, other in zip((0, PART), others):
        shares = attend(
            second_kernel,
            start,
            (rows, rank_id),
            (query, lq, table, *other, pos_part),
            (share,) * TP,
            [pltpu.VMEM((TP, BLK, 128), jnp.bfloat16)],
            "attend_own",
        )
        parts += [shares[0]] + [send_x(shares[d], d) for d in (1, 2, 3)]
    loss, grad = last(parts, positive_emb)
    return loss.reshape(-1), grad


def solution(mesh):
    placed = (
        P("cat", "tp"),
        P("cat", "tp"),
        P("cat", "tp"),
        P("tp", None),
        P("cat", None),
        P(),
        P(),
    )
    return jax.shard_map(
        local, mesh=mesh, in_specs=placed, out_specs=(P("cat"), P("cat", "tp")), check_vma=False
    )
```

```python
import functools
import math

import jax
import jax.numpy as jnp
from jax import lax
from jax.experimental import pallas as pl
from jax.experimental.pallas import tpu as pltpu
from jax.sharding import PartitionSpec as P

BLK = 256
TP = 4
NY = 4
NZ = 4
E = 512
LOG2E = math.log2(math.e)
LN2 = math.log(2.0)
SCALE = 2.0 / math.sqrt(E)
LOW = -1e30
ROWS = BLK // TP // 2
NBD = 8
PICKS = 64
COLS = PICKS * ROWS
TILE = 512
HID = 1024
EXTRA = 32


def cat_perm(flip_y, flip_z, flip_c):
    def at(y, z, c):
        return (y * NZ + z) * 2 + c

    return [
        (at(y, z, c), at(y ^ flip_y, z ^ flip_z, c ^ flip_c))
        for y in range(NY)
        for z in range(NZ)
        for c in range(2)
    ]


def send(value, y=0, z=0, c=0):
    return lax.ppermute(value, "cat", cat_perm(y, z, c))


def send_x(value, d):
    return lax.ppermute(value, "tp", [(i, (i + d) % TP) for i in range(TP)])


def tower_kernel(core_ref, *refs):
    hidden = refs[0:4]
    mine, theirs = refs[4:8], refs[8]
    out_ref = refs[9]
    core = core_ref[0]
    half = HID // TP // 2
    acc = jnp.zeros((NBD * 2 * ROWS, E), jnp.float32)
    for d in range(TP):
        low = jnp.where(core == 0, mine[d][...], theirs[d])
        high = jnp.where(core == 0, theirs[d], mine[d][...])
        acc += jnp.dot(hidden[d][:, :half], low, preferred_element_type=jnp.float32)
        acc += jnp.dot(hidden[d][:, half:], high, preferred_element_type=jnp.float32)
    out_ref[...] = acc.astype(jnp.bfloat16).reshape(out_ref.shape)


def tower(core, hidden, mine, theirs):
    return pl.pallas_call(
        tower_kernel,
        out_shape=jax.ShapeDtypeStruct((2 * NBD, ROWS, E), jnp.bfloat16),
        in_specs=[pl.BlockSpec(memory_space=pltpu.SMEM)]
        + [pl.BlockSpec(memory_space=pltpu.VMEM)] * 9,
        out_specs=pl.BlockSpec(memory_space=pltpu.VMEM),
        compiler_params=pltpu.CompilerParams(vmem_limit_bytes=40 << 20),
        cost_estimate=pl.CostEstimate(
            flops=2 * 512 * 1024 * 512, bytes_accessed=3 << 20, transcendentals=0
        ),
        name="tower",
    )(core, *hidden, *mine, theirs)


PART = 2


def one_block(rank, block, base, q_ref, lq_ref, row_ref, table, picked, scores):
    for j in range(PICKS):
        picked[pl.ds(j * ROWS, ROWS), :] = table[row_ref[(base + block) * PICKS + j]]
    here = pl.ds(block * BLK, BLK)
    query = jnp.concatenate([q_ref[lax.rem(rank + TP - s, TP), here] for s in range(TP)], axis=1)
    top = jnp.full((BLK, 128), LOW, jnp.float32)
    for n in range(COLS // TILE):
        cols = pl.ds(n * TILE, TILE)
        part = lax.dot_general(
            query,
            picked[cols, :],
            (((1,), (1,)), ((), ())),
            preferred_element_type=jnp.float32,
        )
        part = part * (SCALE * LOG2E) - lq_ref[pl.ds(base + block, 1), cols]
        scores[:, cols] = part
        for g in range(TILE // 128):
            top = jnp.maximum(top, part[:, g * 128 : (g + 1) * 128])
    top = jnp.max(top, axis=1, keepdims=True)
    total = jnp.zeros((BLK, 128), jnp.float32)
    acc = jnp.zeros((BLK, E), jnp.float32)
    for n in range(COLS // TILE):
        cols = pl.ds(n * TILE, TILE)
        weight = jnp.exp2(scores[:, cols] - top)
        for g in range(TILE // 128):
            total += weight[:, g * 128 : (g + 1) * 128]
        acc += jnp.dot(
            weight.astype(jnp.bfloat16), picked[cols, :], preferred_element_type=jnp.float32
        )
    return top, jnp.sum(total, axis=1, keepdims=True), acc


def rows_of(top, total):
    lane = lax.broadcasted_iota(jnp.int32, (BLK, 128), 1)
    both = jnp.where(lane == 0, top, jnp.where(lane == 1, total, 0.0))
    return jnp.transpose(both)[:8]


def pack_kernel(places, *refs):
    count = len(places)
    pieces, table, sems = refs[:count], refs[-2], refs[-1]
    copies = [
        pltpu.make_async_copy(piece, table.at[pl.ds(place * 16, 16)], sems.at[n])
        for n, (piece, place) in enumerate(zip(pieces, places))
    ]
    for copy in copies:
        copy.start()
    for copy in copies:
        copy.wait()


def pack(pieces, places, table=None):
    given = () if table is None else (table,)
    vmem = pl.BlockSpec(memory_space=pltpu.VMEM)
    return pl.pallas_call(
        functools.partial(pack_kernel, places),
        out_shape=jax.ShapeDtypeStruct((256, ROWS, E), jnp.bfloat16),
        in_specs=[pl.BlockSpec(memory_space=pltpu.HBM)] * len(pieces) + [vmem] * len(given),
        out_specs=vmem,
        scratch_shapes=[pltpu.SemaphoreType.DMA((len(pieces),))],
        input_output_aliases={len(pieces): 0} if given else {},
        compiler_params=pltpu.CompilerParams(vmem_limit_bytes=20 << 20),
        cost_estimate=pl.CostEstimate(flops=0, bytes_accessed=8 << 20, transcendentals=0),
        name="pack",
    )(*pieces, *given)


def first_kernel(start, row_ref, rank_ref, q_ref, lq_ref, table, *refs):
    out_ref, stat_ref, picked, scores = refs

    for n in range(PART):
        top, total, acc = one_block(
            rank_ref[0], start + n, 0, q_ref, lq_ref, row_ref, table, picked.at[n], scores.at[n]
        )
        out_ref[n] = acc.astype(jnp.bfloat16)
        stat_ref[n] = rows_of(top, total)


def split_rows(row):
    out = []
    for _ in range(3):
        part = row.astype(jnp.bfloat16).astype(jnp.float32)
        out += [part[:, :128], part[:, 128:]]
        row = row - part
    return out


def joined_row(rows):
    halves = [rows[n : n + 1] + (rows[n + 2 : n + 3] + rows[n + 4 : n + 5]) for n in range(2)]
    return jnp.concatenate(halves, axis=1)


def second_kernel(start, row_ref, rank_ref, q_ref, lq_ref, table, *refs):
    other_ref, other_stat_ref, pos_ref = refs[:3]
    outs = refs[3:7]
    picked, scores, quarters = refs[7:]

    for n in range(PART):
        top, total, acc = one_block(
            rank_ref[0], start + n, 2 * PART, q_ref, lq_ref, row_ref, table, picked.at[n], scores.at[n]
        )
        theirs = jnp.transpose(jnp.concatenate([other_stat_ref[n]] * 16, axis=0))
        their_top, their_total = theirs[:, 0:1], theirs[:, 1:2]
        joint = jnp.maximum(top, their_top)
        mine_by, theirs_by = jnp.exp2(top - joint), jnp.exp2(their_top - joint)
        acc = acc * mine_by + other_ref[n].astype(jnp.float32) * theirs_by
        for s in range(TP):
            quarters[s] = acc[:, s * 128 : (s + 1) * 128].astype(jnp.bfloat16)
        stat = rows_of(joint, total * mine_by + their_total * theirs_by)
        rows = split_rows(stat[0:1]) + split_rows(stat[1:2]) + split_rows(pos_ref[start + n])
        rows.append(jnp.zeros((EXTRA - len(rows), 128), jnp.float32))
        tail = jnp.concatenate(rows, axis=0).astype(jnp.bfloat16)
        for d in range(TP):
            outs[d][n, :BLK] = quarters[lax.rem(rank_ref[0] + d, TP)]
            outs[d][n, BLK:] = tail


def attend(body, start, scalars, inputs, outs, scratch, name):
    vmem = pl.BlockSpec(memory_space=pltpu.VMEM)
    return pl.pallas_call(
        functools.partial(body, start),
        in_specs=[pl.BlockSpec(memory_space=pltpu.SMEM)] * len(scalars) + [vmem] * len(inputs),
        out_specs=(vmem,) * len(outs),
        out_shape=outs,
        scratch_shapes=[
            pltpu.VMEM((PART, COLS, E), jnp.bfloat16),
            pltpu.VMEM((PART, BLK, COLS), jnp.float32),
        ]
        + scratch,
        compiler_params=pltpu.CompilerParams(vmem_limit_bytes=32 << 20),
        cost_estimate=pl.CostEstimate(
            flops=PART * 4 * BLK * COLS * E,
            bytes_accessed=2 << 20,
            transcendentals=PART * BLK * COLS,
        ),
        name=name,
    )(*scalars, *inputs)


def last_kernel(*refs):
    positive_ref, loss_ref, grad_ref = refs[8:]
    for block in range(2 * PART):
        parts = refs[0:4] if block < PART else refs[4:8]
        finish(parts, block % PART, block, positive_ref, loss_ref, grad_ref)


def finish(parts, n, block, positive_ref, loss_ref, grad_ref):
    here = pl.ds(block * BLK, BLK)
    tails = [ref[n, BLK:].astype(jnp.float32) for ref in parts]
    tops = [joined_row(tail[0:6]) for tail in tails]
    totals = [joined_row(tail[6:12]) for tail in tails]
    shares = [joined_row(tail[12:18]) for tail in tails]
    pos = (shares[0] + shares[1] + shares[2] + shares[3]) * LOG2E
    joint = pos
    for top in tops:
        joint = jnp.maximum(joint, top)
    total = jnp.exp2(pos - joint)
    for top, one in zip(tops, totals):
        total += one * jnp.exp2(top - joint)
    log_total = joint + jnp.log(total) * LOG2E
    loss_ref[block] = (log_total - pos) * LN2
    factors = [jnp.exp2(top - log_total) * SCALE for top in tops]
    factors.append((jnp.exp2(pos - log_total) - 1.0) * SCALE)
    row = lax.broadcasted_iota(jnp.int32, (128, BLK), 0)
    packed = jnp.zeros((128, BLK), jnp.float32)
    for at, factor in enumerate(factors):
        packed = jnp.where(row == at, factor, packed)
    by = jnp.transpose(packed)
    grad = by[:, 4:5] * positive_ref[here].astype(jnp.float32)
    for s in range(4):
        grad += by[:, s : s + 1] * parts[s][n, :BLK].astype(jnp.float32)
    grad_ref[here] = grad.astype(jnp.bfloat16)


def last(parts, positive):
    vmem = pl.BlockSpec(memory_space=pltpu.VMEM)
    blocks = positive.shape[0] // BLK
    return pl.pallas_call(
        last_kernel,
        in_specs=[vmem] * 9,
        out_specs=(vmem, vmem),
        out_shape=(
            jax.ShapeDtypeStruct((blocks, 1, BLK), jnp.float32),
            jax.ShapeDtypeStruct((blocks * BLK, 128), jnp.bfloat16),
        ),
        compiler_params=pltpu.CompilerParams(vmem_limit_bytes=16 << 20),
        name="last",
    )(*parts, positive)


def together(*values):
    return list(lax.optimization_barrier(tuple(values)))


def spread(items, query):
    near, far = items[:NBD], items[NBD:]
    near_1, far_1 = together(send(near, y=1), send(far, z=1))
    near, far = together(jnp.concatenate([near, near_1]), jnp.concatenate([far, far_1]))
    near_b, far_b, near_z1, far_y1, query_1, query = together(
        send(near, y=3),
        send(far, z=3),
        send(near, z=1),
        send(far, y=1),
        send_x(query, 1),
        query,
    )
    near_b1, near_b3, far_b1, far_b3, query_2, query = together(
        send(near_b, z=1),
        send(near_b, z=3),
        send(far_b, y=1),
        send(far_b, y=3),
        send_x(query, 2),
        query,
    )
    near_z3, far_y3, near_b31, far_b31, last_near, last_far, query_3 = together(
        send(near, z=3),
        send(far, y=3),
        send(near_b3, z=1),
        send(far_b3, y=1),
        near_z1,
        far_y1,
        send_x(query, 3),
    )
    near_z13, far_y13 = send(last_near, z=3), send(last_far, y=3)
    early = [near, near_b, near_z1, near_b1, near_b3, far, far_b, far_y1, far_b1, far_b3]
    table = pack(early, (0, 1, 2, 3, 5, 8, 9, 10, 11, 13))
    late = [near_z3, near_z13, near_b31, far_y3, far_y13, far_b31]
    table = pack(late, (4, 6, 7, 12, 14, 15), table)
    return table, jnp.stack([query, query_1, query_2, query_3])


def place_of(flipped):
    return jnp.where(flipped >= 2, 5 - flipped, flipped)


def local(query_emb, positive_emb, item_hidden, item_weight, neg_blocks, block_home, sample_counts):
    rank = lax.axis_index("tp")
    place = lax.axis_index("cat")
    core, my_z, my_y = place % 2, (place // 2) % NZ, place // (2 * NZ)
    qblocks = neg_blocks.shape[0]
    total_blocks = block_home.shape[0]

    core_id = core.reshape(1).astype(jnp.int32)
    rank_id = rank.reshape(1).astype(jnp.int32)
    hidden = item_hidden.reshape(NBD, TP, 2, ROWS, -1)
    keep = lax.dynamic_index_in_dim(hidden, core, 2, keepdims=False)
    give = lax.dynamic_index_in_dim(hidden, 1 - core, 2, keepdims=False)
    half = lax.dynamic_slice_in_dim(item_weight, core * (HID // TP // 2), HID // TP // 2, 0)
    swapped = send(give, c=1)
    mine_w = [half] + [send_x(half, d) for d in (1, 2, 3)]
    both = jnp.concatenate([keep, swapped])

    def piece(d):
        cut = lax.dynamic_index_in_dim(both, (rank + d) % TP, 1, keepdims=False)
        return cut.reshape(2 * NBD * ROWS, -1)

    hiddens = [piece(0)] + [send_x(piece(d), d) for d in (1, 2, 3)]
    theirs_w = send(together(jnp.stack(mine_w), hiddens[1], hiddens[2])[0], c=1)
    picks = jnp.concatenate([send(neg_blocks, c=1), neg_blocks])
    items, late_query, picks = together(
        tower(core_id, hiddens, mine_w, theirs_w), query_emb, picks
    )
    table, query = spread(items, late_query)
    other_query = send(query, c=1)
    pos_part = SCALE * jnp.sum(
        query_emb.astype(jnp.float32) * positive_emb.astype(jnp.float32), axis=1
    ).reshape(qblocks, 1, BLK)

    matches = picks[:, :, None] == jnp.arange(total_blocks, dtype=jnp.int32)[None, None, :]
    home = jnp.sum(jnp.where(matches, block_home[None, None, :], 0), axis=2)
    slot, owner = home % NBD, home // NBD
    flip_z = ((owner // 2) % NZ) ^ my_z
    flip_y = (owner // (2 * NZ)) ^ my_y
    at_y, at_z = place_of(flip_y), place_of(flip_z)
    near = owner % 2 == core
    rows = jnp.where(near, at_z * 4 + at_y, 16 + at_y * 4 + at_z)
    rows = (rows * NBD + slot).astype(jnp.int32)
    count_rows = sample_counts.reshape(2 * total_blocks, 128)[home.reshape(-1) * 2 + rank // 2]
    counts = lax.dynamic_slice_in_dim(count_rows, (rank % 2 * 2 + core) * ROWS, ROWS, 1)
    lq = (jnp.log(counts.astype(jnp.float32)) * LOG2E).reshape(2 * qblocks, COLS)

    rows = rows.reshape(-1)
    table, pos_part, rows, lq = together(table, pos_part, rows, lq)

    raw = (
        jax.ShapeDtypeStruct((PART, BLK, E), jnp.bfloat16),
        jax.ShapeDtypeStruct((PART, 8, BLK), jnp.float32),
    )
    share = jax.ShapeDtypeStruct((PART, BLK + EXTRA, 128), jnp.bfloat16)
    others = []
    for start in (0, PART):
        made = attend(
            first_kernel,
            start,
            (rows, rank_id),
            (other_query, lq, table),
            raw,
            [],
            "attend_other",
        )
        others.append([send(one, c=1) for one in made])
    parts = []
    for start, other in zip((0, PART), others):
        shares = attend(
            second_kernel,
            start,
            (rows, rank_id),
            (query, lq, table, *other, pos_part),
            (share,) * TP,
            [pltpu.VMEM((TP, BLK, 128), jnp.bfloat16)],
            "attend_own",
        )
        parts += [shares[0]] + [send_x(shares[d], d) for d in (1, 2, 3)]
    loss, grad = last(parts, positive_emb)
    return loss.reshape(-1), grad


def solution(mesh):
    placed = (
        P("cat", "tp"),
        P("cat", "tp"),
        P("cat", "tp"),
        P("tp", None),
        P("cat", None),
        P(),
        P(),
    )
    return jax.shard_map(
        local, mesh=mesh, in_specs=placed, out_specs=(P("cat"), P("cat", "tp")), check_vma=False
    )
```

```python
import functools
import math

import jax
import jax.numpy as jnp
from jax import lax
from jax.experimental import pallas as pl
from jax.experimental.pallas import tpu as pltpu
from jax.sharding import PartitionSpec as P

BLK = 256
TP = 4
NY = 4
NZ = 4
E = 512
LOG2E = math.log2(math.e)
LN2 = math.log(2.0)
SCALE = 2.0 / math.sqrt(E)
LOW = -1e30
ROWS = BLK // TP // 2
NBD = 8
PICKS = 64
COLS = PICKS * ROWS
TILE = 512
HID = 1024
EXTRA = 32


def cat_perm(flip_y, flip_z, flip_c):
    def at(y, z, c):
        return (y * NZ + z) * 2 + c

    return [
        (at(y, z, c), at(y ^ flip_y, z ^ flip_z, c ^ flip_c))
        for y in range(NY)
        for z in range(NZ)
        for c in range(2)
    ]


def send(value, y=0, z=0, c=0):
    return lax.ppermute(value, "cat", cat_perm(y, z, c))


def send_x(value, d):
    return lax.ppermute(value, "tp", [(i, (i + d) % TP) for i in range(TP)])


def tower_kernel(core_ref, *refs):
    hidden = refs[0:4]
    mine, theirs = refs[4:8], refs[8]
    out_ref = refs[9]
    core = core_ref[0]
    half = HID // TP // 2
    acc = jnp.zeros((NBD * 2 * ROWS, E), jnp.float32)
    for d in range(TP):
        low = jnp.where(core == 0, mine[d][...], theirs[d])
        high = jnp.where(core == 0, theirs[d], mine[d][...])
        acc += jnp.dot(hidden[d][:, :half], low, preferred_element_type=jnp.float32)
        acc += jnp.dot(hidden[d][:, half:], high, preferred_element_type=jnp.float32)
    out_ref[...] = acc.astype(jnp.bfloat16).reshape(out_ref.shape)


def tower(core, hidden, mine, theirs):
    return pl.pallas_call(
        tower_kernel,
        out_shape=jax.ShapeDtypeStruct((2 * NBD, ROWS, E), jnp.bfloat16),
        in_specs=[pl.BlockSpec(memory_space=pltpu.SMEM)]
        + [pl.BlockSpec(memory_space=pltpu.VMEM)] * 9,
        out_specs=pl.BlockSpec(memory_space=pltpu.VMEM),
        compiler_params=pltpu.CompilerParams(vmem_limit_bytes=40 << 20),
        cost_estimate=pl.CostEstimate(
            flops=2 * 512 * 1024 * 512, bytes_accessed=3 << 20, transcendentals=0
        ),
        name="tower",
    )(core, *hidden, *mine, theirs)


PART = 2


def one_block(rank, block, base, q_ref, lq_ref, row_ref, table, picked, scores):
    for j in range(PICKS):
        picked[pl.ds(j * ROWS, ROWS), :] = table[row_ref[(base + block) * PICKS + j]]
    here = pl.ds(block * BLK, BLK)
    query = jnp.concatenate([q_ref[lax.rem(rank + TP - s, TP), here] for s in range(TP)], axis=1)
    top = jnp.full((BLK, 128), LOW, jnp.float32)
    for n in range(COLS // TILE):
        cols = pl.ds(n * TILE, TILE)
        part = lax.dot_general(
            query,
            picked[cols, :],
            (((1,), (1,)), ((), ())),
            preferred_element_type=jnp.float32,
        )
        part = part * (SCALE * LOG2E) - lq_ref[pl.ds(base + block, 1), cols]
        scores[:, cols] = part
        for g in range(TILE // 128):
            top = jnp.maximum(top, part[:, g * 128 : (g + 1) * 128])
    top = jnp.max(top, axis=1, keepdims=True)
    total = jnp.zeros((BLK, 128), jnp.float32)
    acc = jnp.zeros((BLK, E), jnp.float32)
    for n in range(COLS // TILE):
        cols = pl.ds(n * TILE, TILE)
        weight = jnp.exp2(scores[:, cols] - top)
        for g in range(TILE // 128):
            total += weight[:, g * 128 : (g + 1) * 128]
        acc += jnp.dot(
            weight.astype(jnp.bfloat16), picked[cols, :], preferred_element_type=jnp.float32
        )
    return top, jnp.sum(total, axis=1, keepdims=True), acc


def rows_of(top, total):
    lane = lax.broadcasted_iota(jnp.int32, (BLK, 128), 1)
    both = jnp.where(lane == 0, top, jnp.where(lane == 1, total, 0.0))
    return jnp.transpose(both)[:8]


def pack_kernel(places, *refs):
    count = len(places)
    pieces, table, sems = refs[:count], refs[-2], refs[-1]
    copies = [
        pltpu.make_async_copy(piece, table.at[pl.ds(place * 16, 16)], sems.at[n])
        for n, (piece, place) in enumerate(zip(pieces, places))
    ]
    for copy in copies:
        copy.start()
    for copy in copies:
        copy.wait()


def pack(pieces, places, table=None):
    given = () if table is None else (table,)
    vmem = pl.BlockSpec(memory_space=pltpu.VMEM)
    return pl.pallas_call(
        functools.partial(pack_kernel, places),
        out_shape=jax.ShapeDtypeStruct((256, ROWS, E), jnp.bfloat16),
        in_specs=[pl.BlockSpec(memory_space=pl.ANY)] * len(pieces) + [vmem] * len(given),
        out_specs=vmem,
        scratch_shapes=[pltpu.SemaphoreType.DMA((len(pieces),))],
        input_output_aliases={len(pieces): 0} if given else {},
        compiler_params=pltpu.CompilerParams(vmem_limit_bytes=20 << 20),
        cost_estimate=pl.CostEstimate(flops=0, bytes_accessed=8 << 20, transcendentals=0),
        name="pack",
    )(*pieces, *given)


def first_kernel(start, row_ref, rank_ref, q_ref, lq_ref, table, *refs):
    out_ref, stat_ref, picked, scores = refs

    for n in range(PART):
        top, total, acc = one_block(
            rank_ref[0], start + n, 0, q_ref, lq_ref, row_ref, table, picked.at[n], scores.at[n]
        )
        out_ref[n] = acc.astype(jnp.bfloat16)
        stat_ref[n] = rows_of(top, total)


def split_rows(row):
    out = []
    for _ in range(3):
        part = row.astype(jnp.bfloat16).astype(jnp.float32)
        out += [part[:, :128], part[:, 128:]]
        row = row - part
    return out


def joined_row(rows):
    halves = [rows[n : n + 1] + (rows[n + 2 : n + 3] + rows[n + 4 : n + 5]) for n in range(2)]
    return jnp.concatenate(halves, axis=1)


def second_kernel(start, row_ref, rank_ref, q_ref, lq_ref, table, *refs):
    other_ref, other_stat_ref, pos_ref = refs[:3]
    outs = refs[3:7]
    picked, scores, quarters = refs[7:]

    for n in range(PART):
        top, total, acc = one_block(
            rank_ref[0], start + n, 2 * PART, q_ref, lq_ref, row_ref, table, picked.at[n], scores.at[n]
        )
        theirs = jnp.transpose(jnp.concatenate([other_stat_ref[n]] * 16, axis=0))
        their_top, their_total = theirs[:, 0:1], theirs[:, 1:2]
        joint = jnp.maximum(top, their_top)
        mine_by, theirs_by = jnp.exp2(top - joint), jnp.exp2(their_top - joint)
        acc = acc * mine_by + other_ref[n].astype(jnp.float32) * theirs_by
        for s in range(TP):
            quarters[s] = acc[:, s * 128 : (s + 1) * 128].astype(jnp.bfloat16)
        stat = rows_of(joint, total * mine_by + their_total * theirs_by)
        rows = split_rows(stat[0:1]) + split_rows(stat[1:2]) + split_rows(pos_ref[start + n])
        rows.append(jnp.zeros((EXTRA - len(rows), 128), jnp.float32))
        tail = jnp.concatenate(rows, axis=0).astype(jnp.bfloat16)
        for d in range(TP):
            outs[d][n, :BLK] = quarters[lax.rem(rank_ref[0] + d, TP)]
            outs[d][n, BLK:] = tail


def attend(body, start, scalars, inputs, outs, scratch, name):
    vmem = pl.BlockSpec(memory_space=pltpu.VMEM)
    return pl.pallas_call(
        functools.partial(body, start),
        in_specs=[pl.BlockSpec(memory_space=pltpu.SMEM)] * len(scalars) + [vmem] * len(inputs),
        out_specs=(vmem,) * len(outs),
        out_shape=outs,
        scratch_shapes=[
            pltpu.VMEM((PART, COLS, E), jnp.bfloat16),
            pltpu.VMEM((PART, BLK, COLS), jnp.float32),
        ]
        + scratch,
        compiler_params=pltpu.CompilerParams(vmem_limit_bytes=32 << 20),
        cost_estimate=pl.CostEstimate(
            flops=PART * 4 * BLK * COLS * E,
            bytes_accessed=2 << 20,
            transcendentals=PART * BLK * COLS,
        ),
        name=name,
    )(*scalars, *inputs)


def last_kernel(*refs):
    positive_ref, loss_ref, grad_ref = refs[8:]
    for block in range(2 * PART):
        parts = refs[0:4] if block < PART else refs[4:8]
        finish(parts, block % PART, block, positive_ref, loss_ref, grad_ref)


def finish(parts, n, block, positive_ref, loss_ref, grad_ref):
    here = pl.ds(block * BLK, BLK)
    tails = [ref[n, BLK:].astype(jnp.float32) for ref in parts]
    tops = [joined_row(tail[0:6]) for tail in tails]
    totals = [joined_row(tail[6:12]) for tail in tails]
    shares = [joined_row(tail[12:18]) for tail in tails]
    pos = (shares[0] + shares[1] + shares[2] + shares[3]) * LOG2E
    joint = pos
    for top in tops:
        joint = jnp.maximum(joint, top)
    total = jnp.exp2(pos - joint)
    for top, one in zip(tops, totals):
        total += one * jnp.exp2(top - joint)
    log_total = joint + jnp.log(total) * LOG2E
    loss_ref[block] = (log_total - pos) * LN2
    factors = [jnp.exp2(top - log_total) * SCALE for top in tops]
    factors.append((jnp.exp2(pos - log_total) - 1.0) * SCALE)
    row = lax.broadcasted_iota(jnp.int32, (128, BLK), 0)
    packed = jnp.zeros((128, BLK), jnp.float32)
    for at, factor in enumerate(factors):
        packed = jnp.where(row == at, factor, packed)
    by = jnp.transpose(packed)
    grad = by[:, 4:5] * positive_ref[here].astype(jnp.float32)
    for s in range(4):
        grad += by[:, s : s + 1] * parts[s][n, :BLK].astype(jnp.float32)
    grad_ref[here] = grad.astype(jnp.bfloat16)


def last(parts, positive):
    vmem = pl.BlockSpec(memory_space=pltpu.VMEM)
    blocks = positive.shape[0] // BLK
    return pl.pallas_call(
        last_kernel,
        in_specs=[vmem] * 9,
        out_specs=(vmem, vmem),
        out_shape=(
            jax.ShapeDtypeStruct((blocks, 1, BLK), jnp.float32),
            jax.ShapeDtypeStruct((blocks * BLK, 128), jnp.bfloat16),
        ),
        compiler_params=pltpu.CompilerParams(vmem_limit_bytes=16 << 20),
        name="last",
    )(*parts, positive)


STREAMS = (
    (("y", 1), ("y", 3), ("z", 1), ("z", 3)),
    (("y", 3), ("y", 1), ("z", 3), ("z", 1)),
    (("z", 1), ("z", 3), ("y", 1), ("y", 3)),
    (("z", 3), ("z", 1), ("y", 3), ("y", 1)),
)


def together(*values):
    return list(lax.optimization_barrier(tuple(values)))


def spread(items, query):
    held = [items[n * 4 : n * 4 + 4] for n in range(4)]
    queries = [query]
    for step in range(3):
        got = [send(h, **{st[step][0]: st[step][1]}) for h, st in zip(held, STREAMS)]
        got = together(*got, send_x(query, step + 1), query)
        queries.append(got[4])
        query = got[5]
        if step < 2:
            held = together(*[jnp.concatenate([h, g]) for h, g in zip(held, got)])
    third = got[:4]
    fourth = [send(h, **{st[3][0]: st[3][1]}) for h, st in zip(held, STREAMS)]
    fifth = [send(h, **{st[3][0]: st[3][1]}) for h, st in zip(third, STREAMS)]
    table = pack(held + third, (0, 4, 8, 12, 1, 5, 9, 13))
    table = pack(fourth + fifth, (2, 6, 10, 14, 3, 7, 11, 15), table)
    return table, jnp.stack(queries)


def place_of(flipped, first):
    return jnp.where(
        flipped == 0, 0, jnp.where(flipped == 2, 3, jnp.where(flipped == first, 1, 2))
    )


def local(query_emb, positive_emb, item_hidden, item_weight, neg_blocks, block_home, sample_counts):
    rank = lax.axis_index("tp")
    place = lax.axis_index("cat")
    core, my_z, my_y = place % 2, (place // 2) % NZ, place // (2 * NZ)
    qblocks = neg_blocks.shape[0]
    total_blocks = block_home.shape[0]

    core_id = core.reshape(1).astype(jnp.int32)
    rank_id = rank.reshape(1).astype(jnp.int32)
    hidden = item_hidden.reshape(NBD, TP, 2, ROWS, -1)
    keep = lax.dynamic_index_in_dim(hidden, core, 2, keepdims=False)
    give = lax.dynamic_index_in_dim(hidden, 1 - core, 2, keepdims=False)
    half = lax.dynamic_slice_in_dim(item_weight, core * (HID // TP // 2), HID // TP // 2, 0)
    swapped = send(give, c=1)
    mine_w = [half] + [send_x(half, d) for d in (1, 2, 3)]
    both = jnp.concatenate([keep, swapped])

    def piece(d):
        cut = lax.dynamic_index_in_dim(both, (rank + d) % TP, 1, keepdims=False)
        return cut.reshape(2 * NBD * ROWS, -1)

    hiddens = [piece(0)] + [send_x(piece(d), d) for d in (1, 2, 3)]
    theirs_w = send(together(jnp.stack(mine_w), hiddens[1], hiddens[3])[0], c=1)
    picks = jnp.concatenate([send(neg_blocks, c=1), neg_blocks])
    items, late_query, picks = together(
        tower(core_id, hiddens, mine_w, theirs_w), query_emb, picks
    )
    table, query = spread(items, late_query)
    other_query = send(query, c=1)
    pos_part = SCALE * jnp.sum(
        query_emb.astype(jnp.float32) * positive_emb.astype(jnp.float32), axis=1
    ).reshape(qblocks, 1, BLK)

    matches = picks[:, :, None] == jnp.arange(total_blocks, dtype=jnp.int32)[None, None, :]
    home = jnp.sum(jnp.where(matches, block_home[None, None, :], 0), axis=2)
    slot, owner = home % NBD, home // NBD
    flip_z = ((owner // 2) % NZ) ^ my_z
    flip_y = (owner // (2 * NZ)) ^ my_y
    late = slot // (NBD // 2)
    at_y = place_of(flip_y, jnp.where(late == 0, 1, 3))
    at_z = place_of(flip_z, jnp.where(late == 0, 1, 3))
    near = owner % 2 == core
    rows = jnp.where(near, at_z * 4 + at_y, 128 // 4 + at_y * 4 + at_z)
    rows = (rows * 4 + late * 64 + slot % 4).astype(jnp.int32)
    count_rows = sample_counts.reshape(2 * total_blocks, 128)[home.reshape(-1) * 2 + rank // 2]
    counts = lax.dynamic_slice_in_dim(count_rows, (rank % 2 * 2 + core) * ROWS, ROWS, 1)
    lq = (jnp.log(counts.astype(jnp.float32)) * LOG2E).reshape(2 * qblocks, COLS)

    rows = rows.reshape(-1)
    table, pos_part, rows, lq = together(table, pos_part, rows, lq)

    raw = (
        jax.ShapeDtypeStruct((PART, BLK, E), jnp.bfloat16),
        jax.ShapeDtypeStruct((PART, 8, BLK), jnp.float32),
    )
    share = jax.ShapeDtypeStruct((PART, BLK + EXTRA, 128), jnp.bfloat16)
    others = []
    for start in (0, PART):
        made = attend(
            first_kernel,
            start,
            (rows, rank_id),
            (other_query, lq, table),
            raw,
            [],
            "attend_other",
        )
        others.append([send(one, c=1) for one in made])
    parts = []
    for start, other in zip((0, PART), others):
        shares = attend(
            second_kernel,
            start,
            (rows, rank_id),
            (query, lq, table, *other, pos_part),
            (share,) * TP,
            [pltpu.VMEM((TP, BLK, 128), jnp.bfloat16)],
            "attend_own",
        )
        parts += [shares[0]] + [send_x(shares[d], d) for d in (1, 2, 3)]
    loss, grad = last(parts, positive_emb)
    return loss.reshape(-1), grad


def solution(mesh):
    placed = (
        P("cat", "tp"),
        P("cat", "tp"),
        P("cat", "tp"),
        P("tp", None),
        P("cat", None),
        P(),
        P(),
    )
    return jax.shard_map(
        local, mesh=mesh, in_specs=placed, out_specs=(P("cat"), P("cat", "tp")), check_vma=False
    )
```

```python
import functools
import math

import jax
import jax.numpy as jnp
from jax import lax
from jax.experimental import pallas as pl
from jax.experimental.pallas import tpu as pltpu
from jax.sharding import PartitionSpec as P

BLK = 256
TP = 4
NY = 4
NZ = 4
E = 512
LOG2E = math.log2(math.e)
LN2 = math.log(2.0)
SCALE = 2.0 / math.sqrt(E)
LOW = -1e30
ROWS = BLK // TP // 2
NBD = 8
PICKS = 64
COLS = PICKS * ROWS
TILE = 512
HID = 1024
EXTRA = 32


def cat_perm(flip_y, flip_z, flip_c):
    def at(y, z, c):
        return (y * NZ + z) * 2 + c

    return [
        (at(y, z, c), at(y ^ flip_y, z ^ flip_z, c ^ flip_c))
        for y in range(NY)
        for z in range(NZ)
        for c in range(2)
    ]


def send(value, y=0, z=0, c=0):
    return lax.ppermute(value, "cat", cat_perm(y, z, c))


def send_x(value, d):
    return lax.ppermute(value, "tp", [(i, (i + d) % TP) for i in range(TP)])


def tower_kernel(core_ref, *refs):
    hidden = refs[0:4]
    mine, theirs = refs[4:8], refs[8]
    out_ref = refs[9]
    core = core_ref[0]
    half = HID // TP // 2
    acc = jnp.zeros((NBD * 2 * ROWS, E), jnp.float32)
    for d in range(TP):
        low = jnp.where(core == 0, mine[d][...], theirs[d])
        high = jnp.where(core == 0, theirs[d], mine[d][...])
        acc += jnp.dot(hidden[d][:, :half], low, preferred_element_type=jnp.float32)
        acc += jnp.dot(hidden[d][:, half:], high, preferred_element_type=jnp.float32)
    out_ref[...] = acc.astype(jnp.bfloat16).reshape(out_ref.shape)


def tower(core, hidden, mine, theirs):
    return pl.pallas_call(
        tower_kernel,
        out_shape=jax.ShapeDtypeStruct((2 * NBD, ROWS, E), jnp.bfloat16),
        in_specs=[pl.BlockSpec(memory_space=pltpu.SMEM)]
        + [pl.BlockSpec(memory_space=pltpu.VMEM)] * 9,
        out_specs=pl.BlockSpec(memory_space=pltpu.VMEM),
        compiler_params=pltpu.CompilerParams(vmem_limit_bytes=40 << 20),
        cost_estimate=pl.CostEstimate(
            flops=2 * 512 * 1024 * 512, bytes_accessed=3 << 20, transcendentals=0
        ),
        name="tower",
    )(core, *hidden, *mine, theirs)


PART = 2


def one_block(rank, block, side, q_refs, lq_ref, row_ref, table, picked, scores, gathered):
    base = side * 2 * PART
    for j in range(PICKS):
        picked[pl.ds(j * ROWS, ROWS), :] = table[row_ref[(base + block) * PICKS + j]]
    here = pl.ds(block * BLK, BLK)
    for d in range(TP):
        gathered[lax.rem(rank + TP - d, TP)] = q_refs[d][side, here]
    query = jnp.concatenate([gathered[s] for s in range(TP)], axis=1)
    top = jnp.full((BLK, 128), LOW, jnp.float32)
    for n in range(COLS // TILE):
        cols = pl.ds(n * TILE, TILE)
        part = lax.dot_general(
            query,
            picked[cols, :],
            (((1,), (1,)), ((), ())),
            preferred_element_type=jnp.float32,
        )
        part = part * (SCALE * LOG2E) - lq_ref[pl.ds(base + block, 1), cols]
        scores[:, cols] = part
        for g in range(TILE // 128):
            top = jnp.maximum(top, part[:, g * 128 : (g + 1) * 128])
    top = jnp.max(top, axis=1, keepdims=True)
    total = jnp.zeros((BLK, 128), jnp.float32)
    acc = jnp.zeros((BLK, E), jnp.float32)
    for n in range(COLS // TILE):
        cols = pl.ds(n * TILE, TILE)
        weight = jnp.exp2(scores[:, cols] - top)
        for g in range(TILE // 128):
            total += weight[:, g * 128 : (g + 1) * 128]
        acc += jnp.dot(
            weight.astype(jnp.bfloat16), picked[cols, :], preferred_element_type=jnp.float32
        )
    return top, jnp.sum(total, axis=1, keepdims=True), acc


def rows_of(top, total):
    lane = lax.broadcasted_iota(jnp.int32, (BLK, 128), 1)
    both = jnp.where(lane == 0, top, jnp.where(lane == 1, total, 0.0))
    return jnp.transpose(both)[:8]


def pack_kernel(places, *refs):
    count = len(places)
    pieces, table, sems = refs[:count], refs[-2], refs[-1]
    copies = [
        pltpu.make_async_copy(piece, table.at[pl.ds(place * 16, 16)], sems.at[n])
        for n, (piece, place) in enumerate(zip(pieces, places))
    ]
    for copy in copies:
        copy.start()
    for copy in copies:
        copy.wait()


def pack(pieces, places, table=None):
    given = () if table is None else (table,)
    vmem = pl.BlockSpec(memory_space=pltpu.VMEM)
    return pl.pallas_call(
        functools.partial(pack_kernel, places),
        out_shape=jax.ShapeDtypeStruct((256, ROWS, E), jnp.bfloat16),
        in_specs=[pl.BlockSpec(memory_space=pl.ANY)] * len(pieces) + [vmem] * len(given),
        out_specs=vmem,
        scratch_shapes=[pltpu.SemaphoreType.DMA((len(pieces),))],
        input_output_aliases={len(pieces): 0} if given else {},
        compiler_params=pltpu.CompilerParams(vmem_limit_bytes=20 << 20),
        cost_estimate=pl.CostEstimate(flops=0, bytes_accessed=8 << 20, transcendentals=0),
        name="pack",
    )(*pieces, *given)


def first_kernel(start, row_ref, rank_ref, *refs):
    q_refs, (lq_ref, table) = refs[:TP], refs[TP : TP + 2]
    out_ref, stat_ref, picked, scores, gathered = refs[TP + 2 :]

    for n in range(PART):
        top, total, acc = one_block(
            rank_ref[0], start + n, 0, q_refs, lq_ref, row_ref, table,
            picked.at[n], scores.at[n], gathered.at[n],
        )
        out_ref[n] = acc.astype(jnp.bfloat16)
        stat_ref[n] = rows_of(top, total)


def split_rows(row):
    out = []
    for _ in range(3):
        part = row.astype(jnp.bfloat16).astype(jnp.float32)
        out += [part[:, :128], part[:, 128:]]
        row = row - part
    return out


def joined_row(rows):
    halves = [rows[n : n + 1] + (rows[n + 2 : n + 3] + rows[n + 4 : n + 5]) for n in range(2)]
    return jnp.concatenate(halves, axis=1)


def second_kernel(start, row_ref, rank_ref, *refs):
    q_refs, (lq_ref, table), refs = refs[:TP], refs[TP : TP + 2], refs[TP + 2 :]
    other_ref, other_stat_ref, pos_ref = refs[:3]
    outs = refs[3:7]
    picked, scores, gathered, quarters = refs[7:]

    for n in range(PART):
        top, total, acc = one_block(
            rank_ref[0], start + n, 1, q_refs, lq_ref, row_ref, table,
            picked.at[n], scores.at[n], gathered.at[n],
        )
        theirs = jnp.transpose(jnp.concatenate([other_stat_ref[n]] * 16, axis=0))
        their_top, their_total = theirs[:, 0:1], theirs[:, 1:2]
        joint = jnp.maximum(top, their_top)
        mine_by, theirs_by = jnp.exp2(top - joint), jnp.exp2(their_top - joint)
        acc = acc * mine_by + other_ref[n].astype(jnp.float32) * theirs_by
        for s in range(TP):
            quarters[s] = acc[:, s * 128 : (s + 1) * 128].astype(jnp.bfloat16)
        stat = rows_of(joint, total * mine_by + their_total * theirs_by)
        rows = split_rows(stat[0:1]) + split_rows(stat[1:2]) + split_rows(pos_ref[start + n])
        rows.append(jnp.zeros((EXTRA - len(rows), 128), jnp.float32))
        tail = jnp.concatenate(rows, axis=0).astype(jnp.bfloat16)
        for d in range(TP):
            outs[d][n, :BLK] = quarters[lax.rem(rank_ref[0] + d, TP)]
            outs[d][n, BLK:] = tail


def attend(body, start, scalars, inputs, outs, scratch, name):
    vmem = pl.BlockSpec(memory_space=pltpu.VMEM)
    return pl.pallas_call(
        functools.partial(body, start),
        in_specs=[pl.BlockSpec(memory_space=pltpu.SMEM)] * len(scalars) + [vmem] * len(inputs),
        out_specs=(vmem,) * len(outs),
        out_shape=outs,
        scratch_shapes=[
            pltpu.VMEM((PART, COLS, E), jnp.bfloat16),
            pltpu.VMEM((PART, BLK, COLS), jnp.float32),
            pltpu.VMEM((PART, TP, BLK, 128), jnp.bfloat16),
        ]
        + scratch,
        compiler_params=pltpu.CompilerParams(vmem_limit_bytes=32 << 20),
        cost_estimate=pl.CostEstimate(
            flops=PART * 4 * BLK * COLS * E,
            bytes_accessed=2 << 20,
            transcendentals=PART * BLK * COLS,
        ),
        name=name,
    )(*scalars, *inputs)


def last_kernel(*refs):
    positive_ref, loss_ref, grad_ref = refs[8:]
    for block in range(2 * PART):
        parts = refs[0:4] if block < PART else refs[4:8]
        finish(parts, block % PART, block, positive_ref, loss_ref, grad_ref)


def finish(parts, n, block, positive_ref, loss_ref, grad_ref):
    here = pl.ds(block * BLK, BLK)
    tails = [ref[n, BLK:].astype(jnp.float32) for ref in parts]
    tops = [joined_row(tail[0:6]) for tail in tails]
    totals = [joined_row(tail[6:12]) for tail in tails]
    shares = [joined_row(tail[12:18]) for tail in tails]
    pos = (shares[0] + shares[1] + shares[2] + shares[3]) * LOG2E
    joint = pos
    for top in tops:
        joint = jnp.maximum(joint, top)
    total = jnp.exp2(pos - joint)
    for top, one in zip(tops, totals):
        total += one * jnp.exp2(top - joint)
    log_total = joint + jnp.log(total) * LOG2E
    loss_ref[block] = (log_total - pos) * LN2
    factors = [jnp.exp2(top - log_total) * SCALE for top in tops]
    factors.append((jnp.exp2(pos - log_total) - 1.0) * SCALE)
    row = lax.broadcasted_iota(jnp.int32, (128, BLK), 0)
    packed = jnp.zeros((128, BLK), jnp.float32)
    for at, factor in enumerate(factors):
        packed = jnp.where(row == at, factor, packed)
    by = jnp.transpose(packed)
    grad = by[:, 4:5] * positive_ref[here].astype(jnp.float32)
    for s in range(4):
        grad += by[:, s : s + 1] * parts[s][n, :BLK].astype(jnp.float32)
    grad_ref[here] = grad.astype(jnp.bfloat16)


def last(parts, positive):
    vmem = pl.BlockSpec(memory_space=pltpu.VMEM)
    blocks = positive.shape[0] // BLK
    return pl.pallas_call(
        last_kernel,
        in_specs=[vmem] * 9,
        out_specs=(vmem, vmem),
        out_shape=(
            jax.ShapeDtypeStruct((blocks, 1, BLK), jnp.float32),
            jax.ShapeDtypeStruct((blocks * BLK, 128), jnp.bfloat16),
        ),
        compiler_params=pltpu.CompilerParams(vmem_limit_bytes=16 << 20),
        name="last",
    )(*parts, positive)


STREAMS = (
    (("y", 1), ("y", 3), ("z", 1), ("z", 3)),
    (("y", 3), ("y", 1), ("z", 3), ("z", 1)),
    (("z", 1), ("z", 3), ("y", 1), ("y", 3)),
    (("z", 3), ("z", 1), ("y", 3), ("y", 1)),
)


def together(*values):
    return list(lax.optimization_barrier(tuple(values)))


def spread(items, query):
    held = [items[n * 4 : n * 4 + 4] for n in range(4)]
    queries = [query]
    for step in range(2):
        got = [send(h, **{st[step][0]: st[step][1]}) for h, st in zip(held, STREAMS)]
        got = together(*got, send_x(query, step + 1), query)
        queries.append(got[4])
        query = got[5]
        held = together(*[jnp.concatenate([h, g]) for h, g in zip(held, got)], query)
        query = held.pop()
    third = [send(h, **{st[2][0]: st[2][1]}) for h, st in zip(held, STREAMS)]
    queries.append(send_x(query, 3))
    held, third = zip(*[together(h, t) for h, t in zip(held, third)])
    held, third = list(held), list(third)
    fourth = [send(h, **{st[3][0]: st[3][1]}) for h, st in zip(held, STREAMS)]
    third, fourth = zip(*[together(t, f) for t, f in zip(third, fourth)])
    third, fourth = list(third), list(fourth)
    fifth = [send(h, **{st[3][0]: st[3][1]}) for h, st in zip(third, STREAMS)]
    table = pack(held + third, (0, 4, 8, 12, 1, 5, 9, 13))
    table = pack(fourth + fifth, (2, 6, 10, 14, 3, 7, 11, 15), table)
    return table, queries


def place_of(flipped, first):
    return jnp.where(
        flipped == 0, 0, jnp.where(flipped == 2, 3, jnp.where(flipped == first, 1, 2))
    )


def local(query_emb, positive_emb, item_hidden, item_weight, neg_blocks, block_home, sample_counts):
    rank = lax.axis_index("tp")
    place = lax.axis_index("cat")
    core, my_z, my_y = place % 2, (place // 2) % NZ, place // (2 * NZ)
    qblocks = neg_blocks.shape[0]
    total_blocks = block_home.shape[0]

    core_id = core.reshape(1).astype(jnp.int32)
    rank_id = rank.reshape(1).astype(jnp.int32)
    hidden = item_hidden.reshape(NBD, TP, 2, ROWS, -1)
    keep = lax.dynamic_index_in_dim(hidden, core, 2, keepdims=False)
    give = lax.dynamic_index_in_dim(hidden, 1 - core, 2, keepdims=False)
    half = lax.dynamic_slice_in_dim(item_weight, core * (HID // TP // 2), HID // TP // 2, 0)
    swapped = send(give, c=1)
    mine_w = [half] + [send_x(half, d) for d in (1, 2, 3)]
    both = jnp.concatenate([keep, swapped])

    def piece(d):
        cut = lax.dynamic_index_in_dim(both, (rank + d) % TP, 1, keepdims=False)
        return cut.reshape(2 * NBD * ROWS, -1)

    hiddens = [piece(0)] + [send_x(piece(d), d) for d in (1, 2, 3)]
    theirs_w = send(together(jnp.stack(mine_w), hiddens[1], hiddens[3])[0], c=1)
    picks = jnp.concatenate([send(neg_blocks, c=1), neg_blocks])
    both_query = jnp.stack([send(query_emb, c=1), query_emb])
    items, late_query, picks = together(
        tower(core_id, hiddens, mine_w, theirs_w), both_query, picks
    )
    table, queries = spread(items, late_query)
    pos_part = SCALE * jnp.sum(
        query_emb.astype(jnp.float32) * positive_emb.astype(jnp.float32), axis=1
    ).reshape(qblocks, 1, BLK)

    matches = picks[:, :, None] == jnp.arange(total_blocks, dtype=jnp.int32)[None, None, :]
    home = jnp.sum(jnp.where(matches, block_home[None, None, :], 0), axis=2)
    slot, owner = home % NBD, home // NBD
    flip_z = ((owner // 2) % NZ) ^ my_z
    flip_y = (owner // (2 * NZ)) ^ my_y
    late = slot // (NBD // 2)
    at_y = place_of(flip_y, jnp.where(late == 0, 1, 3))
    at_z = place_of(flip_z, jnp.where(late == 0, 1, 3))
    near = owner % 2 == core
    rows = jnp.where(near, at_z * 4 + at_y, 128 // 4 + at_y * 4 + at_z)
    rows = (rows * 4 + late * 64 + slot % 4).astype(jnp.int32)
    count_rows = sample_counts.reshape(2 * total_blocks, 128)[home.reshape(-1) * 2 + rank // 2]
    counts = lax.dynamic_slice_in_dim(count_rows, (rank % 2 * 2 + core) * ROWS, ROWS, 1)
    lq = (jnp.log(counts.astype(jnp.float32)) * LOG2E).reshape(2 * qblocks, COLS)

    rows = rows.reshape(-1)
    table, pos_part, rows, lq = together(table, pos_part, rows, lq)

    raw = (
        jax.ShapeDtypeStruct((PART, BLK, E), jnp.bfloat16),
        jax.ShapeDtypeStruct((PART, 8, BLK), jnp.float32),
    )
    share = jax.ShapeDtypeStruct((PART, BLK + EXTRA, 128), jnp.bfloat16)
    others = []
    for start in (0, PART):
        made = attend(
            first_kernel,
            start,
            (rows, rank_id),
            (*queries, lq, table),
            raw,
            [],
            "attend_other",
        )
        others.append([send(one, c=1) for one in made])
    parts = []
    for start, other in zip((0, PART), others):
        shares = attend(
            second_kernel,
            start,
            (rows, rank_id),
            (*queries, lq, table, *other, pos_part),
            (share,) * TP,
            [pltpu.VMEM((TP, BLK, 128), jnp.bfloat16)],
            "attend_own",
        )
        parts += [shares[0]] + [send_x(shares[d], d) for d in (1, 2, 3)]
    loss, grad = last(parts, positive_emb)
    return loss.reshape(-1), grad


def solution(mesh):
    placed = (
        P("cat", "tp"),
        P("cat", "tp"),
        P("cat", "tp"),
        P("tp", None),
        P("cat", None),
        P(),
        P(),
    )
    return jax.shard_map(
        local, mesh=mesh, in_specs=placed, out_specs=(P("cat"), P("cat", "tp")), check_vma=False
    )
```

```python
import functools
import math

import jax
import jax.numpy as jnp
from jax import lax
from jax.experimental import pallas as pl
from jax.experimental.pallas import tpu as pltpu
from jax.sharding import PartitionSpec as P

BLK = 256
TP = 4
NY = 4
NZ = 4
E = 512
LOG2E = math.log2(math.e)
LN2 = math.log(2.0)
SCALE = 2.0 / math.sqrt(E)
LOW = -1e30
ROWS = BLK // TP // 2
NBD = 8
PICKS = 64
COLS = PICKS * ROWS
TILE = 512
HID = 1024
EXTRA = 32


def cat_perm(flip_y, flip_z, flip_c):
    def at(y, z, c):
        return (y * NZ + z) * 2 + c

    return [
        (at(y, z, c), at(y ^ flip_y, z ^ flip_z, c ^ flip_c))
        for y in range(NY)
        for z in range(NZ)
        for c in range(2)
    ]


def send(value, y=0, z=0, c=0):
    return lax.ppermute(value, "cat", cat_perm(y, z, c))


def send_x(value, d):
    return lax.ppermute(value, "tp", [(i, (i + d) % TP) for i in range(TP)])


def tower_kernel(core_ref, rank_ref, *refs):
    hidden = refs[0:4]
    mine, theirs = refs[4:8], refs[8]
    out_ref, quarters = refs[9:]
    core = core_ref[0]
    half = HID // TP // 2
    acc = jnp.zeros((NBD * 2 * ROWS, E), jnp.float32)
    for d in range(TP):
        low = jnp.where(core == 0, mine[d][...], theirs[d])
        high = jnp.where(core == 0, theirs[d], mine[d][...])
        acc += jnp.dot(hidden[d][:, :half], low, preferred_element_type=jnp.float32)
        acc += jnp.dot(hidden[d][:, half:], high, preferred_element_type=jnp.float32)
    for s in range(TP):
        quarters[s] = acc[:, s * 128 : (s + 1) * 128].astype(jnp.bfloat16).reshape(quarters.shape[1:])
    for d in range(TP):
        out_ref[:, :, d * 128 : (d + 1) * 128] = quarters[lax.rem(rank_ref[0] + TP - d, TP)]


def tower(core, rank, hidden, mine, theirs):
    return pl.pallas_call(
        tower_kernel,
        out_shape=jax.ShapeDtypeStruct((2 * NBD, ROWS, E), jnp.bfloat16),
        in_specs=[pl.BlockSpec(memory_space=pltpu.SMEM)] * 2
        + [pl.BlockSpec(memory_space=pltpu.VMEM)] * 9,
        scratch_shapes=[pltpu.VMEM((TP, 2 * NBD, ROWS, 128), jnp.bfloat16)],
        out_specs=pl.BlockSpec(memory_space=pltpu.VMEM),
        compiler_params=pltpu.CompilerParams(vmem_limit_bytes=40 << 20),
        cost_estimate=pl.CostEstimate(
            flops=2 * 512 * 1024 * 512, bytes_accessed=3 << 20, transcendentals=0
        ),
        name="tower",
    )(core, rank, *hidden, *mine, theirs)


PART = 2


def one_block(block, side, q_refs, lq_ref, row_ref, table, picked, scores):
    base = side * 2 * PART
    for j in range(PICKS):
        picked[pl.ds(j * ROWS, ROWS), :] = table[row_ref[(base + block) * PICKS + j]]
    here = pl.ds(block * BLK, BLK)
    query = jnp.concatenate([q_refs[d][side, here] for d in range(TP)], axis=1)
    top = jnp.full((BLK, 128), LOW, jnp.float32)
    for n in range(COLS // TILE):
        cols = pl.ds(n * TILE, TILE)
        part = lax.dot_general(
            query,
            picked[cols, :],
            (((1,), (1,)), ((), ())),
            preferred_element_type=jnp.float32,
        )
        part = part * (SCALE * LOG2E) - lq_ref[pl.ds(base + block, 1), cols]
        scores[:, cols] = part
        for g in range(TILE // 128):
            top = jnp.maximum(top, part[:, g * 128 : (g + 1) * 128])
    top = jnp.max(top, axis=1, keepdims=True)
    total = jnp.zeros((BLK, 128), jnp.float32)
    acc = jnp.zeros((BLK, E), jnp.float32)
    for n in range(COLS // TILE):
        cols = pl.ds(n * TILE, TILE)
        weight = jnp.exp2(scores[:, cols] - top)
        for g in range(TILE // 128):
            total += weight[:, g * 128 : (g + 1) * 128]
        acc += jnp.dot(
            weight.astype(jnp.bfloat16), picked[cols, :], preferred_element_type=jnp.float32
        )
    return top, jnp.sum(total, axis=1, keepdims=True), acc


def rows_of(top, total):
    lane = lax.broadcasted_iota(jnp.int32, (BLK, 128), 1)
    both = jnp.where(lane == 0, top, jnp.where(lane == 1, total, 0.0))
    return jnp.transpose(both)[:8]


def pack_kernel(places, *refs):
    count = len(places)
    pieces, table, sems = refs[:count], refs[-2], refs[-1]
    copies = [
        pltpu.make_async_copy(piece, table.at[pl.ds(place * 16, 16)], sems.at[n])
        for n, (piece, place) in enumerate(zip(pieces, places))
    ]
    for copy in copies:
        copy.start()
    for copy in copies:
        copy.wait()


def pack(pieces, places, table=None):
    given = () if table is None else (table,)
    vmem = pl.BlockSpec(memory_space=pltpu.VMEM)
    return pl.pallas_call(
        functools.partial(pack_kernel, places),
        out_shape=jax.ShapeDtypeStruct((256, ROWS, E), jnp.bfloat16),
        in_specs=[pl.BlockSpec(memory_space=pl.ANY)] * len(pieces) + [vmem] * len(given),
        out_specs=vmem,
        scratch_shapes=[pltpu.SemaphoreType.DMA((len(pieces),))],
        input_output_aliases={len(pieces): 0} if given else {},
        compiler_params=pltpu.CompilerParams(vmem_limit_bytes=20 << 20),
        cost_estimate=pl.CostEstimate(flops=0, bytes_accessed=8 << 20, transcendentals=0),
        name="pack",
    )(*pieces, *given)


def first_kernel(start, row_ref, *refs):
    q_refs, (lq_ref, table) = refs[:TP], refs[TP : TP + 2]
    out_ref, stat_ref, picked, scores = refs[TP + 2 :]

    for n in range(PART):
        top, total, acc = one_block(
            start + n, 0, q_refs, lq_ref, row_ref, table,
            picked.at[n], scores.at[n],
        )
        out_ref[n] = acc.astype(jnp.bfloat16)
        stat_ref[n] = rows_of(top, total)


def split_rows(row):
    out = []
    for _ in range(3):
        part = row.astype(jnp.bfloat16).astype(jnp.float32)
        out += [part[:, :128], part[:, 128:]]
        row = row - part
    return out


def joined_row(rows):
    halves = [rows[n : n + 1] + (rows[n + 2 : n + 3] + rows[n + 4 : n + 5]) for n in range(2)]
    return jnp.concatenate(halves, axis=1)


def second_kernel(start, row_ref, *refs):
    q_refs, (lq_ref, table), refs = refs[:TP], refs[TP : TP + 2], refs[TP + 2 :]
    other_ref, other_stat_ref, pos_ref = refs[:3]
    outs = refs[3:7]
    picked, scores = refs[7:]

    for n in range(PART):
        top, total, acc = one_block(
            start + n, 1, q_refs, lq_ref, row_ref, table,
            picked.at[n], scores.at[n],
        )
        theirs = jnp.transpose(jnp.concatenate([other_stat_ref[n]] * 16, axis=0))
        their_top, their_total = theirs[:, 0:1], theirs[:, 1:2]
        joint = jnp.maximum(top, their_top)
        mine_by, theirs_by = jnp.exp2(top - joint), jnp.exp2(their_top - joint)
        acc = acc * mine_by + other_ref[n].astype(jnp.float32) * theirs_by
        stat = rows_of(joint, total * mine_by + their_total * theirs_by)
        rows = split_rows(stat[0:1]) + split_rows(stat[1:2]) + split_rows(pos_ref[start + n])
        rows.append(jnp.zeros((EXTRA - len(rows), 128), jnp.float32))
        tail = jnp.concatenate(rows, axis=0).astype(jnp.bfloat16)
        for d in range(TP):
            at = (TP - d) % TP * 128
            outs[d][n, :BLK] = acc[:, at : at + 128].astype(jnp.bfloat16)
            outs[d][n, BLK:] = tail


def attend(body, start, scalars, inputs, outs, name):
    vmem = pl.BlockSpec(memory_space=pltpu.VMEM)
    return pl.pallas_call(
        functools.partial(body, start),
        in_specs=[pl.BlockSpec(memory_space=pltpu.SMEM)] * len(scalars) + [vmem] * len(inputs),
        out_specs=(vmem,) * len(outs),
        out_shape=outs,
        scratch_shapes=[
            pltpu.VMEM((PART, COLS, E), jnp.bfloat16),
            pltpu.VMEM((PART, BLK, COLS), jnp.float32),
        ],
        compiler_params=pltpu.CompilerParams(vmem_limit_bytes=32 << 20),
        cost_estimate=pl.CostEstimate(
            flops=PART * 4 * BLK * COLS * E,
            bytes_accessed=2 << 20,
            transcendentals=PART * BLK * COLS,
        ),
        name=name,
    )(*scalars, *inputs)


def last_kernel(*refs):
    positive_ref, loss_ref, grad_ref = refs[8:]
    for block in range(2 * PART):
        parts = refs[0:4] if block < PART else refs[4:8]
        finish(parts, block % PART, block, positive_ref, loss_ref, grad_ref)


def finish(parts, n, block, positive_ref, loss_ref, grad_ref):
    here = pl.ds(block * BLK, BLK)
    tails = [ref[n, BLK:].astype(jnp.float32) for ref in parts]
    tops = [joined_row(tail[0:6]) for tail in tails]
    totals = [joined_row(tail[6:12]) for tail in tails]
    shares = [joined_row(tail[12:18]) for tail in tails]
    pos = (shares[0] + shares[1] + shares[2] + shares[3]) * LOG2E
    joint = pos
    for top in tops:
        joint = jnp.maximum(joint, top)
    total = jnp.exp2(pos - joint)
    for top, one in zip(tops, totals):
        total += one * jnp.exp2(top - joint)
    log_total = joint + jnp.log(total) * LOG2E
    loss_ref[block] = (log_total - pos) * LN2
    factors = [jnp.exp2(top - log_total) * SCALE for top in tops]
    factors.append((jnp.exp2(pos - log_total) - 1.0) * SCALE)
    row = lax.broadcasted_iota(jnp.int32, (128, BLK), 0)
    packed = jnp.zeros((128, BLK), jnp.float32)
    for at, factor in enumerate(factors):
        packed = jnp.where(row == at, factor, packed)
    by = jnp.transpose(packed)
    grad = by[:, 4:5] * positive_ref[here].astype(jnp.float32)
    for s in range(4):
        grad += by[:, s : s + 1] * parts[s][n, :BLK].astype(jnp.float32)
    grad_ref[here] = grad.astype(jnp.bfloat16)


def last(parts, positive):
    vmem = pl.BlockSpec(memory_space=pltpu.VMEM)
    blocks = positive.shape[0] // BLK
    return pl.pallas_call(
        last_kernel,
        in_specs=[vmem] * 9,
        out_specs=(vmem, vmem),
        out_shape=(
            jax.ShapeDtypeStruct((blocks, 1, BLK), jnp.float32),
            jax.ShapeDtypeStruct((blocks * BLK, 128), jnp.bfloat16),
        ),
        compiler_params=pltpu.CompilerParams(vmem_limit_bytes=16 << 20),
        name="last",
    )(*parts, positive)


STREAMS = (
    (("y", 1), ("y", 3), ("z", 1), ("z", 3)),
    (("y", 3), ("y", 1), ("z", 3), ("z", 1)),
    (("z", 1), ("z", 3), ("y", 1), ("y", 3)),
    (("z", 3), ("z", 1), ("y", 3), ("y", 1)),
)


def together(*values):
    return list(lax.optimization_barrier(tuple(values)))


def spread(items, query):
    held = [items[n * 4 : n * 4 + 4] for n in range(4)]
    got = [send(h, **{st[0][0]: st[0][1]}) for h, st in zip(held, STREAMS)]
    query_1 = send_x(query, 1)
    got = together(*got)
    held = together(*[jnp.concatenate([h, g]) for h, g in zip(held, got)])
    got = [send(h, **{st[1][0]: st[1][1]}) for h, st in zip(held, STREAMS)]
    *got, query_1, query = together(*got, query_1, query)
    held = together(*[jnp.concatenate([h, g]) for h, g in zip(held, got)])
    third = [send(h, **{st[2][0]: st[2][1]}) for h, st in zip(held, STREAMS)]
    query_2 = send_x(query, 2)
    held, third = zip(*[together(h, t) for h, t in zip(held, third)])
    fourth = [send(h, **{st[3][0]: st[3][1]}) for h, st in zip(held, STREAMS)]
    held, third = list(held), list(third)
    third, fourth = zip(*[together(t, f) for t, f in zip(third, fourth)])
    third, fourth = list(third), list(fourth)
    query_2, query, fourth[0] = together(query_2, query, fourth[0])
    queries = [query, query_1, query_2, send_x(query, 3)]
    fifth = [send(h, **{st[3][0]: st[3][1]}) for h, st in zip(third, STREAMS)]
    table = pack(held + third, (0, 4, 8, 12, 1, 5, 9, 13))
    table = pack(fourth + fifth, (2, 6, 10, 14, 3, 7, 11, 15), table)
    return table, queries


def place_of(flipped, first):
    return jnp.where(
        flipped == 0, 0, jnp.where(flipped == 2, 3, jnp.where(flipped == first, 1, 2))
    )


def local(query_emb, positive_emb, item_hidden, item_weight, neg_blocks, block_home, sample_counts):
    rank = lax.axis_index("tp")
    place = lax.axis_index("cat")
    core, my_z, my_y = place % 2, (place // 2) % NZ, place // (2 * NZ)
    qblocks = neg_blocks.shape[0]
    total_blocks = block_home.shape[0]

    core_id = core.reshape(1).astype(jnp.int32)
    rank_id = rank.reshape(1).astype(jnp.int32)
    hidden = item_hidden.reshape(NBD, TP, 2, ROWS, -1)
    keep = lax.dynamic_index_in_dim(hidden, core, 2, keepdims=False)
    give = lax.dynamic_index_in_dim(hidden, 1 - core, 2, keepdims=False)
    half = lax.dynamic_slice_in_dim(item_weight, core * (HID // TP // 2), HID // TP // 2, 0)
    swapped = send(give, c=1)
    mine_w = [half] + [send_x(half, d) for d in (1, 2, 3)]
    both = jnp.concatenate([keep, swapped])

    def piece(d):
        cut = lax.dynamic_index_in_dim(both, (rank + d) % TP, 1, keepdims=False)
        return cut.reshape(2 * NBD * ROWS, -1)

    hiddens = [piece(0)] + [send_x(piece(d), d) for d in (1, 2, 3)]
    theirs_w = send(together(jnp.stack(mine_w), hiddens[1], hiddens[3])[0], c=1)
    picks = jnp.concatenate([send(neg_blocks, c=1), neg_blocks])
    both_query = jnp.stack([send(query_emb, c=1), query_emb])
    items, late_query, picks = together(
        tower(core_id, rank_id, hiddens, mine_w, theirs_w), both_query, picks
    )
    table, queries = spread(items, late_query)
    pos_part = SCALE * jnp.sum(
        query_emb.astype(jnp.float32) * positive_emb.astype(jnp.float32), axis=1
    ).reshape(qblocks, 1, BLK)

    matches = picks[:, :, None] == jnp.arange(total_blocks, dtype=jnp.int32)[None, None, :]
    home = jnp.sum(jnp.where(matches, block_home[None, None, :], 0), axis=2)
    slot, owner = home % NBD, home // NBD
    flip_z = ((owner // 2) % NZ) ^ my_z
    flip_y = (owner // (2 * NZ)) ^ my_y
    late = slot // (NBD // 2)
    at_y = place_of(flip_y, jnp.where(late == 0, 1, 3))
    at_z = place_of(flip_z, jnp.where(late == 0, 1, 3))
    near = owner % 2 == core
    rows = jnp.where(near, at_z * 4 + at_y, 128 // 4 + at_y * 4 + at_z)
    rows = (rows * 4 + late * 64 + slot % 4).astype(jnp.int32)
    count_rows = sample_counts.reshape(2 * total_blocks, 128)[home.reshape(-1) * 2 + rank // 2]
    counts = lax.dynamic_slice_in_dim(count_rows, (rank % 2 * 2 + core) * ROWS, ROWS, 1)
    lq = (jnp.log(counts.astype(jnp.float32)) * LOG2E).reshape(2 * qblocks, COLS)

    rows = rows.reshape(-1)
    table, pos_part, rows, lq = together(table, pos_part, rows, lq)

    raw = (
        jax.ShapeDtypeStruct((PART, BLK, E), jnp.bfloat16),
        jax.ShapeDtypeStruct((PART, 8, BLK), jnp.float32),
    )
    share = jax.ShapeDtypeStruct((PART, BLK + EXTRA, 128), jnp.bfloat16)
    others = []
    for start in (0, PART):
        made = attend(
            first_kernel,
            start,
            (rows,),
            (*queries, lq, table),
            raw,
            "attend_other",
        )
        others.append([send(one, c=1) for one in made])
    parts = []
    for start, other in zip((0, PART), others):
        shares = attend(
            second_kernel,
            start,
            (rows,),
            (*queries, lq, table, *other, pos_part),
            (share,) * TP,
            "attend_own",
        )
        parts += [shares[0]] + [send_x(shares[d], d) for d in (1, 2, 3)]
    loss, grad = last(parts, positive_emb)
    return loss.reshape(-1), grad


def solution(mesh):
    placed = (
        P("cat", "tp"),
        P("cat", "tp"),
        P("cat", "tp"),
        P("tp", None),
        P("cat", None),
        P(),
        P(),
    )
    return jax.shard_map(
        local, mesh=mesh, in_specs=placed, out_specs=(P("cat"), P("cat", "tp")), check_vma=False
    )
```

```python
import functools
import math

import jax
import jax.numpy as jnp
from jax import lax
from jax.experimental import pallas as pl
from jax.experimental.pallas import tpu as pltpu
from jax.sharding import PartitionSpec as P

BLK = 256
TP = 4
NY = 4
NZ = 4
E = 512
LOG2E = math.log2(math.e)
LN2 = math.log(2.0)
SCALE = 2.0 / math.sqrt(E)
LOW = -1e30
ROWS = BLK // TP // 2
NBD = 8
PICKS = 64
COLS = PICKS * ROWS
TILE = 512
HID = 1024
TAIL = 16
EXTRA = 32


def cat_perm(flip_y, flip_z, flip_c):
    def at(y, z, c):
        return (y * NZ + z) * 2 + c

    return [
        (at(y, z, c), at(y ^ flip_y, z ^ flip_z, c ^ flip_c))
        for y in range(NY)
        for z in range(NZ)
        for c in range(2)
    ]


def send(value, y=0, z=0, c=0):
    return lax.ppermute(value, "cat", cat_perm(y, z, c))


def send_x(value, d):
    return lax.ppermute(value, "tp", [(i, (i + d) % TP) for i in range(TP)])


def tower_kernel(core_ref, rank_ref, *refs):
    hidden = refs[0:4]
    mine, theirs = refs[4:8], refs[8]
    out_ref, quarters = refs[9:]
    core = core_ref[0]
    half = HID // TP // 2
    acc = jnp.zeros((NBD * 2 * ROWS, E), jnp.float32)
    for d in range(TP):
        low = jnp.where(core == 0, mine[d][...], theirs[d])
        high = jnp.where(core == 0, theirs[d], mine[d][...])
        acc += jnp.dot(hidden[d][:, :half], low, preferred_element_type=jnp.float32)
        acc += jnp.dot(hidden[d][:, half:], high, preferred_element_type=jnp.float32)
    for s in range(TP):
        quarters[s] = acc[:, s * 128 : (s + 1) * 128].astype(jnp.bfloat16).reshape(quarters.shape[1:])
    for d in range(TP):
        out_ref[:, :, d * 128 : (d + 1) * 128] = quarters[lax.rem(rank_ref[0] + TP - d, TP)]


def tower(core, rank, hidden, mine, theirs):
    return pl.pallas_call(
        tower_kernel,
        out_shape=jax.ShapeDtypeStruct((2 * NBD, ROWS, E), jnp.bfloat16),
        in_specs=[pl.BlockSpec(memory_space=pltpu.SMEM)] * 2
        + [pl.BlockSpec(memory_space=pltpu.VMEM)] * 9,
        scratch_shapes=[pltpu.VMEM((TP, 2 * NBD, ROWS, 128), jnp.bfloat16)],
        out_specs=pl.BlockSpec(memory_space=pltpu.VMEM),
        compiler_params=pltpu.CompilerParams(vmem_limit_bytes=40 << 20),
        cost_estimate=pl.CostEstimate(
            flops=2 * 512 * 1024 * 512, bytes_accessed=3 << 20, transcendentals=0
        ),
        name="tower",
    )(core, rank, *hidden, *mine, theirs)


PART = 2


def one_block(block, side, q_refs, lq_ref, row_ref, table, picked, scores):
    base = side * 2 * PART
    for j in range(PICKS):
        picked[pl.ds(j * ROWS, ROWS), :] = table[row_ref[(base + block) * PICKS + j]]
    here = pl.ds(block * BLK, BLK)
    query = jnp.concatenate([q_refs[d][side, here] for d in range(TP)], axis=1)
    top = jnp.full((BLK, 128), LOW, jnp.float32)
    for n in range(COLS // TILE):
        cols = pl.ds(n * TILE, TILE)
        part = lax.dot_general(
            query,
            picked[cols, :],
            (((1,), (1,)), ((), ())),
            preferred_element_type=jnp.float32,
        )
        part = part * (SCALE * LOG2E) - lq_ref[pl.ds(base + block, 1), cols]
        scores[:, cols] = part
        for g in range(TILE // 128):
            top = jnp.maximum(top, part[:, g * 128 : (g + 1) * 128])
    top = jnp.max(top, axis=1, keepdims=True)
    total = jnp.zeros((BLK, 128), jnp.float32)
    acc = jnp.zeros((BLK, E), jnp.float32)
    for n in range(COLS // TILE):
        cols = pl.ds(n * TILE, TILE)
        weight = jnp.exp2(scores[:, cols] - top)
        for g in range(TILE // 128):
            total += weight[:, g * 128 : (g + 1) * 128]
        acc += jnp.dot(
            weight.astype(jnp.bfloat16), picked[cols, :], preferred_element_type=jnp.float32
        )
    return top, jnp.sum(total, axis=1, keepdims=True), acc


def rows_of(top, total):
    lane = lax.broadcasted_iota(jnp.int32, (BLK, 128), 1)
    both = jnp.where(lane == 0, top, jnp.where(lane == 1, total, 0.0))
    return jnp.transpose(both)[:8]


def pack_kernel(places, *refs):
    count = len(places)
    pieces, table, sems = refs[:count], refs[-2], refs[-1]
    copies = [
        pltpu.make_async_copy(piece, table.at[pl.ds(place * 16, 16)], sems.at[n])
        for n, (piece, place) in enumerate(zip(pieces, places))
    ]
    for copy in copies:
        copy.start()
    for copy in copies:
        copy.wait()


def pack(pieces, places, table=None):
    given = () if table is None else (table,)
    vmem = pl.BlockSpec(memory_space=pltpu.VMEM)
    return pl.pallas_call(
        functools.partial(pack_kernel, places),
        out_shape=jax.ShapeDtypeStruct((256, ROWS, E), jnp.bfloat16),
        in_specs=[pl.BlockSpec(memory_space=pl.ANY)] * len(pieces) + [vmem] * len(given),
        out_specs=vmem,
        scratch_shapes=[pltpu.SemaphoreType.DMA((len(pieces),))],
        input_output_aliases={len(pieces): 0} if given else {},
        compiler_params=pltpu.CompilerParams(vmem_limit_bytes=20 << 20),
        cost_estimate=pl.CostEstimate(flops=0, bytes_accessed=8 << 20, transcendentals=0),
        name="pack",
    )(*pieces, *given)


def first_kernel(start, row_ref, *refs):
    q_refs, (lq_ref, table) = refs[:TP], refs[TP : TP + 2]
    out_ref, picked, scores = refs[TP + 2 :]

    for n in range(PART):
        top, total, acc = one_block(
            start + n, 0, q_refs, lq_ref, row_ref, table,
            picked.at[n], scores.at[n],
        )
        stat = rows_of(top, total)
        parts = parts_of(stat[0:1]) + parts_of(stat[1:2])
        rows = [jnp.concatenate(parts[at : at + 2], axis=1) for at in (0, 2, 4)]
        rows.append(jnp.zeros((TAIL - 3, E), jnp.float32))
        out_ref[n, :BLK] = acc.astype(jnp.bfloat16)
        out_ref[n, BLK:] = jnp.concatenate(rows, axis=0).astype(jnp.bfloat16)


def parts_of(row):
    out = []
    for _ in range(3):
        part = row.astype(jnp.bfloat16).astype(jnp.float32)
        out.append(part)
        row = row - part
    return out


def split_rows(row):
    return [part[:, at : at + 128] for part in parts_of(row) for at in (0, 128)]


def joined_row(rows):
    halves = [rows[n : n + 1] + (rows[n + 2 : n + 3] + rows[n + 4 : n + 5]) for n in range(2)]
    return jnp.concatenate(halves, axis=1)


def second_kernel(start, row_ref, *refs):
    q_refs, (lq_ref, table), refs = refs[:TP], refs[TP : TP + 2], refs[TP + 2 :]
    other_ref, pos_ref = refs[:2]
    outs = refs[2:6]
    picked, scores = refs[6:]

    for n in range(PART):
        top, total, acc = one_block(
            start + n, 1, q_refs, lq_ref, row_ref, table,
            picked.at[n], scores.at[n],
        )
        tail = other_ref[n, BLK:].astype(jnp.float32)
        left, right = tail[:, :BLK], tail[:, BLK:]
        row = lax.broadcasted_iota(jnp.int32, (128, BLK), 0)
        their_top = left[0:1] + (right[0:1] + left[1:2])
        their_total = right[1:2] + (left[2:3] + right[2:3])
        theirs = jnp.where(row == 0, their_top, jnp.where(row == 1, their_total, 0.0))
        theirs = jnp.transpose(theirs)
        their_top, their_total = theirs[:, 0:1], theirs[:, 1:2]
        joint = jnp.maximum(top, their_top)
        mine_by, theirs_by = jnp.exp2(top - joint), jnp.exp2(their_top - joint)
        acc = acc * mine_by + other_ref[n, :BLK].astype(jnp.float32) * theirs_by
        stat = rows_of(joint, total * mine_by + their_total * theirs_by)
        rows = split_rows(stat[0:1]) + split_rows(stat[1:2]) + split_rows(pos_ref[start + n])
        rows.append(jnp.zeros((EXTRA - len(rows), 128), jnp.float32))
        tail = jnp.concatenate(rows, axis=0).astype(jnp.bfloat16)
        for d in range(TP):
            at = (TP - d) % TP * 128
            outs[d][n, :BLK] = acc[:, at : at + 128].astype(jnp.bfloat16)
            outs[d][n, BLK:] = tail


def attend(body, start, scalars, inputs, outs, name):
    vmem = pl.BlockSpec(memory_space=pltpu.VMEM)
    return pl.pallas_call(
        functools.partial(body, start),
        in_specs=[pl.BlockSpec(memory_space=pltpu.SMEM)] * len(scalars) + [vmem] * len(inputs),
        out_specs=(vmem,) * len(outs),
        out_shape=outs,
        scratch_shapes=[
            pltpu.VMEM((PART, COLS, E), jnp.bfloat16),
            pltpu.VMEM((PART, BLK, COLS), jnp.float32),
        ],
        compiler_params=pltpu.CompilerParams(vmem_limit_bytes=32 << 20),
        cost_estimate=pl.CostEstimate(
            flops=PART * 4 * BLK * COLS * E,
            bytes_accessed=2 << 20,
            transcendentals=PART * BLK * COLS,
        ),
        name=name,
    )(*scalars, *inputs)


def last_kernel(*refs):
    positive_ref, loss_ref, grad_ref = refs[8:]
    for block in range(2 * PART):
        parts = refs[0:4] if block < PART else refs[4:8]
        finish(parts, block % PART, block, positive_ref, loss_ref, grad_ref)


def finish(parts, n, block, positive_ref, loss_ref, grad_ref):
    here = pl.ds(block * BLK, BLK)
    tails = [ref[n, BLK:].astype(jnp.float32) for ref in parts]
    tops = [joined_row(tail[0:6]) for tail in tails]
    totals = [joined_row(tail[6:12]) for tail in tails]
    shares = [joined_row(tail[12:18]) for tail in tails]
    pos = (shares[0] + shares[1] + shares[2] + shares[3]) * LOG2E
    joint = pos
    for top in tops:
        joint = jnp.maximum(joint, top)
    total = jnp.exp2(pos - joint)
    for top, one in zip(tops, totals):
        total += one * jnp.exp2(top - joint)
    log_total = joint + jnp.log(total) * LOG2E
    loss_ref[block] = (log_total - pos) * LN2
    factors = [jnp.exp2(top - log_total) * SCALE for top in tops]
    factors.append((jnp.exp2(pos - log_total) - 1.0) * SCALE)
    row = lax.broadcasted_iota(jnp.int32, (128, BLK), 0)
    packed = jnp.zeros((128, BLK), jnp.float32)
    for at, factor in enumerate(factors):
        packed = jnp.where(row == at, factor, packed)
    by = jnp.transpose(packed)
    grad = by[:, 4:5] * positive_ref[here].astype(jnp.float32)
    for s in range(4):
        grad += by[:, s : s + 1] * parts[s][n, :BLK].astype(jnp.float32)
    grad_ref[here] = grad.astype(jnp.bfloat16)


def last(parts, positive):
    vmem = pl.BlockSpec(memory_space=pltpu.VMEM)
    blocks = positive.shape[0] // BLK
    return pl.pallas_call(
        last_kernel,
        in_specs=[vmem] * 9,
        out_specs=(vmem, vmem),
        out_shape=(
            jax.ShapeDtypeStruct((blocks, 1, BLK), jnp.float32),
            jax.ShapeDtypeStruct((blocks * BLK, 128), jnp.bfloat16),
        ),
        compiler_params=pltpu.CompilerParams(vmem_limit_bytes=16 << 20),
        name="last",
    )(*parts, positive)


STREAMS = (
    (("y", 1), ("y", 3), ("z", 1), ("z", 3)),
    (("y", 3), ("y", 1), ("z", 3), ("z", 1)),
    (("z", 1), ("z", 3), ("y", 1), ("y", 3)),
    (("z", 3), ("z", 1), ("y", 3), ("y", 1)),
)


def together(*values):
    return list(lax.optimization_barrier(tuple(values)))


def spread(items, query):
    held = [items[n * 4 : n * 4 + 4] for n in range(4)]
    got = [send(h, **{st[0][0]: st[0][1]}) for h, st in zip(held, STREAMS)]
    query_1 = send_x(query, 1)
    got = together(*got)
    held = together(*[jnp.concatenate([h, g]) for h, g in zip(held, got)])
    got = [send(h, **{st[1][0]: st[1][1]}) for h, st in zip(held, STREAMS)]
    *got, query_1, query = together(*got, query_1, query)
    held = together(*[jnp.concatenate([h, g]) for h, g in zip(held, got)])
    third = [send(h, **{st[2][0]: st[2][1]}) for h, st in zip(held, STREAMS)]
    query_2 = send_x(query, 2)
    held, third = zip(*[together(h, t) for h, t in zip(held, third)])
    fourth = [send(h, **{st[3][0]: st[3][1]}) for h, st in zip(held, STREAMS)]
    held, third = list(held), list(third)
    third, fourth = zip(*[together(t, f) for t, f in zip(third, fourth)])
    third, fourth = list(third), list(fourth)
    query_2, query, fourth[0] = together(query_2, query, fourth[0])
    queries = [query, query_1, query_2, send_x(query, 3)]
    fifth = [send(h, **{st[3][0]: st[3][1]}) for h, st in zip(third, STREAMS)]
    table = pack(held + third, (0, 4, 8, 12, 1, 5, 9, 13))
    table = pack(fourth + fifth, (2, 6, 10, 14, 3, 7, 11, 15), table)
    return table, queries


def place_of(flipped, first):
    return jnp.where(
        flipped == 0, 0, jnp.where(flipped == 2, 3, jnp.where(flipped == first, 1, 2))
    )


def local(query_emb, positive_emb, item_hidden, item_weight, neg_blocks, block_home, sample_counts):
    rank = lax.axis_index("tp")
    place = lax.axis_index("cat")
    core, my_z, my_y = place % 2, (place // 2) % NZ, place // (2 * NZ)
    qblocks = neg_blocks.shape[0]
    total_blocks = block_home.shape[0]

    core_id = core.reshape(1).astype(jnp.int32)
    rank_id = rank.reshape(1).astype(jnp.int32)
    hidden = item_hidden.reshape(NBD, TP, 2, ROWS, -1)
    keep = lax.dynamic_index_in_dim(hidden, core, 2, keepdims=False)
    give = lax.dynamic_index_in_dim(hidden, 1 - core, 2, keepdims=False)
    half = lax.dynamic_slice_in_dim(item_weight, core * (HID // TP // 2), HID // TP // 2, 0)
    swapped = send(give, c=1)
    mine_w = [half] + [send_x(half, d) for d in (1, 2, 3)]
    both = jnp.concatenate([keep, swapped])

    def piece(d):
        cut = lax.dynamic_index_in_dim(both, (rank + d) % TP, 1, keepdims=False)
        return cut.reshape(2 * NBD * ROWS, -1)

    hiddens = [piece(0)] + [send_x(piece(d), d) for d in (1, 2, 3)]
    theirs_w = send(together(jnp.stack(mine_w), hiddens[1], hiddens[3])[0], c=1)
    picks = jnp.concatenate([send(neg_blocks, c=1), neg_blocks])
    both_query = jnp.stack([send(query_emb, c=1), query_emb])
    items, late_query, picks = together(
        tower(core_id, rank_id, hiddens, mine_w, theirs_w), both_query, picks
    )
    table, queries = spread(items, late_query)
    pos_part = SCALE * jnp.sum(
        query_emb.astype(jnp.float32) * positive_emb.astype(jnp.float32), axis=1
    ).reshape(qblocks, 1, BLK)

    matches = picks[:, :, None] == jnp.arange(total_blocks, dtype=jnp.int32)[None, None, :]
    home = jnp.sum(jnp.where(matches, block_home[None, None, :], 0), axis=2)
    slot, owner = home % NBD, home // NBD
    flip_z = ((owner // 2) % NZ) ^ my_z
    flip_y = (owner // (2 * NZ)) ^ my_y
    late = slot // (NBD // 2)
    at_y = place_of(flip_y, jnp.where(late == 0, 1, 3))
    at_z = place_of(flip_z, jnp.where(late == 0, 1, 3))
    near = owner % 2 == core
    rows = jnp.where(near, at_z * 4 + at_y, 128 // 4 + at_y * 4 + at_z)
    rows = (rows * 4 + late * 64 + slot % 4).astype(jnp.int32)
    count_rows = sample_counts.reshape(2 * total_blocks, 128)[home.reshape(-1) * 2 + rank // 2]
    counts = lax.dynamic_slice_in_dim(count_rows, (rank % 2 * 2 + core) * ROWS, ROWS, 1)
    lq = (jnp.log(counts.astype(jnp.float32)) * LOG2E).reshape(2 * qblocks, COLS)

    rows = rows.reshape(-1)
    table, pos_part, rows, lq = together(table, pos_part, rows, lq)

    raw = (jax.ShapeDtypeStruct((PART, BLK + TAIL, E), jnp.bfloat16),)
    share = jax.ShapeDtypeStruct((PART, BLK + EXTRA, 128), jnp.bfloat16)
    others = []
    for start in (0, PART):
        made = attend(
            first_kernel,
            start,
            (rows,),
            (*queries, lq, table),
            raw,
            "attend_other",
        )
        others.append([send(one, c=1) for one in made])
    parts = []
    for start, other in zip((0, PART), others):
        shares = attend(
            second_kernel,
            start,
            (rows,),
            (*queries, lq, table, *other, pos_part),
            (share,) * TP,
            "attend_own",
        )
        parts += [shares[0]] + [send_x(shares[d], d) for d in (1, 2, 3)]
    loss, grad = last(parts, positive_emb)
    return loss.reshape(-1), grad


def solution(mesh):
    placed = (
        P("cat", "tp"),
        P("cat", "tp"),
        P("cat", "tp"),
        P("tp", None),
        P("cat", None),
        P(),
        P(),
    )
    return jax.shard_map(
        local, mesh=mesh, in_specs=placed, out_specs=(P("cat"), P("cat", "tp")), check_vma=False
    )
```

```python
import functools
import math

import jax
import jax.numpy as jnp
from jax import lax
from jax.experimental import pallas as pl
from jax.experimental.pallas import tpu as pltpu
from jax.sharding import PartitionSpec as P

BLK = 256
TP = 4
NY = 4
NZ = 4
E = 512
LOG2E = math.log2(math.e)
LN2 = math.log(2.0)
SCALE = 2.0 / math.sqrt(E)
LOW = -1e30
ROWS = BLK // TP // 2
NBD = 8
PICKS = 64
COLS = PICKS * ROWS
TILE = 512
HID = 1024
TAIL = 16
EXTRA = 32


def cat_perm(flip_y, flip_z, flip_c):
    def at(y, z, c):
        return (y * NZ + z) * 2 + c

    return [
        (at(y, z, c), at(y ^ flip_y, z ^ flip_z, c ^ flip_c))
        for y in range(NY)
        for z in range(NZ)
        for c in range(2)
    ]


def send(value, y=0, z=0, c=0):
    return lax.ppermute(value, "cat", cat_perm(y, z, c))


def send_x(value, d):
    return lax.ppermute(value, "tp", [(i, (i + d) % TP) for i in range(TP)])


def tower_kernel(core_ref, rank_ref, *refs):
    hidden = refs[0:4]
    mine, theirs = refs[4:8], refs[8]
    out_ref, quarters = refs[9:]
    core = core_ref[0]
    half = HID // TP // 2
    acc = jnp.zeros((NBD * 2 * ROWS, E), jnp.float32)
    for d in range(TP):
        low = jnp.where(core == 0, mine[d][...], theirs[d])
        high = jnp.where(core == 0, theirs[d], mine[d][...])
        acc += jnp.dot(hidden[d][:, :half], low, preferred_element_type=jnp.float32)
        acc += jnp.dot(hidden[d][:, half:], high, preferred_element_type=jnp.float32)
    for s in range(TP):
        quarters[s] = acc[:, s * 128 : (s + 1) * 128].astype(jnp.bfloat16).reshape(quarters.shape[1:])
    for d in range(TP):
        out_ref[:, :, d * 128 : (d + 1) * 128] = quarters[lax.rem(rank_ref[0] + TP - d, TP)]


def tower(core, rank, hidden, mine, theirs):
    return pl.pallas_call(
        tower_kernel,
        out_shape=jax.ShapeDtypeStruct((2 * NBD, ROWS, E), jnp.bfloat16),
        in_specs=[pl.BlockSpec(memory_space=pltpu.SMEM)] * 2
        + [pl.BlockSpec(memory_space=pltpu.VMEM)] * 9,
        scratch_shapes=[pltpu.VMEM((TP, 2 * NBD, ROWS, 128), jnp.bfloat16)],
        out_specs=pl.BlockSpec(memory_space=pltpu.VMEM),
        compiler_params=pltpu.CompilerParams(vmem_limit_bytes=40 << 20),
        cost_estimate=pl.CostEstimate(
            flops=2 * 512 * 1024 * 512, bytes_accessed=3 << 20, transcendentals=0
        ),
        name="tower",
    )(core, rank, *hidden, *mine, theirs)


PART = 2


def one_block(block, side, q_refs, lq_ref, row_ref, table, picked, scores):
    base = side * 2 * PART
    for j in range(PICKS):
        picked[pl.ds(j * ROWS, ROWS), :] = table[row_ref[(base + block) * PICKS + j]]
    here = pl.ds(block * BLK, BLK)
    query = jnp.concatenate([q_refs[d][side, here] for d in range(TP)], axis=1)
    top = jnp.full((BLK, 128), LOW, jnp.float32)
    for n in range(COLS // TILE):
        cols = pl.ds(n * TILE, TILE)
        part = lax.dot_general(
            query,
            picked[cols, :],
            (((1,), (1,)), ((), ())),
            preferred_element_type=jnp.float32,
        )
        part = part * (SCALE * LOG2E) - lq_ref[pl.ds(base + block, 1), cols]
        scores[:, cols] = part
        for g in range(TILE // 128):
            top = jnp.maximum(top, part[:, g * 128 : (g + 1) * 128])
    top = jnp.max(top, axis=1, keepdims=True)
    total = jnp.zeros((BLK, 128), jnp.float32)
    acc = jnp.zeros((BLK, E), jnp.float32)
    for n in range(COLS // TILE):
        cols = pl.ds(n * TILE, TILE)
        weight = jnp.exp2(scores[:, cols] - top)
        for g in range(TILE // 128):
            total += weight[:, g * 128 : (g + 1) * 128]
        acc += jnp.dot(
            weight.astype(jnp.bfloat16), picked[cols, :], preferred_element_type=jnp.float32
        )
    return top, jnp.sum(total, axis=1, keepdims=True), acc


def rows_of(top, total):
    lane = lax.broadcasted_iota(jnp.int32, (BLK, 128), 1)
    both = jnp.where(lane == 0, top, jnp.where(lane == 1, total, 0.0))
    return jnp.transpose(both)[:8]


def pack_kernel(places, *refs):
    count = len(places)
    pieces, table, sems = refs[:count], refs[-2], refs[-1]
    copies = [
        pltpu.make_async_copy(piece, table.at[pl.ds(place * 16, 16)], sems.at[n])
        for n, (piece, place) in enumerate(zip(pieces, places))
    ]
    for copy in copies:
        copy.start()
    for copy in copies:
        copy.wait()


def pack(pieces, places, table=None):
    given = () if table is None else (table,)
    vmem = pl.BlockSpec(memory_space=pltpu.VMEM)
    return pl.pallas_call(
        functools.partial(pack_kernel, places),
        out_shape=jax.ShapeDtypeStruct((256, ROWS, E), jnp.bfloat16),
        in_specs=[pl.BlockSpec(memory_space=pl.ANY)] * len(pieces) + [vmem] * len(given),
        out_specs=vmem,
        scratch_shapes=[pltpu.SemaphoreType.DMA((len(pieces),))],
        input_output_aliases={len(pieces): 0} if given else {},
        compiler_params=pltpu.CompilerParams(vmem_limit_bytes=20 << 20),
        cost_estimate=pl.CostEstimate(flops=0, bytes_accessed=8 << 20, transcendentals=0),
        name="pack",
    )(*pieces, *given)


def first_kernel(start, row_ref, *refs):
    q_refs, (lq_ref, table) = refs[:TP], refs[TP : TP + 2]
    out_ref, picked, scores = refs[TP + 2 :]

    for n in range(PART):
        top, total, acc = one_block(
            start + n, 0, q_refs, lq_ref, row_ref, table,
            picked.at[n], scores.at[n],
        )
        stat = rows_of(top, total)
        parts = parts_of(stat[0:1]) + parts_of(stat[1:2])
        rows = [jnp.concatenate(parts[at : at + 2], axis=1) for at in (0, 2, 4)]
        rows.append(jnp.zeros((TAIL - 3, E), jnp.float32))
        out_ref[n, :BLK] = acc.astype(jnp.bfloat16)
        out_ref[n, BLK:] = jnp.concatenate(rows, axis=0).astype(jnp.bfloat16)


def parts_of(row):
    out = []
    for _ in range(3):
        part = row.astype(jnp.bfloat16).astype(jnp.float32)
        out.append(part)
        row = row - part
    return out


def split_rows(row):
    return [part[:, at : at + 128] for part in parts_of(row) for at in (0, 128)]


def joined_row(rows):
    halves = [rows[n : n + 1] + (rows[n + 2 : n + 3] + rows[n + 4 : n + 5]) for n in range(2)]
    return jnp.concatenate(halves, axis=1)


def second_kernel(start, row_ref, *refs):
    q_refs, (lq_ref, table), refs = refs[:TP], refs[TP : TP + 2], refs[TP + 2 :]
    other_ref, pos_ref = refs[:2]
    outs = refs[2:6]
    picked, scores = refs[6:]

    for n in range(PART):
        top, total, acc = one_block(
            start + n, 1, q_refs, lq_ref, row_ref, table,
            picked.at[n], scores.at[n],
        )
        tail = other_ref[n, BLK:].astype(jnp.float32)
        left, right = tail[:, :BLK], tail[:, BLK:]
        row = lax.broadcasted_iota(jnp.int32, (128, BLK), 0)
        their_top = left[0:1] + (right[0:1] + left[1:2])
        their_total = right[1:2] + (left[2:3] + right[2:3])
        theirs = jnp.where(row == 0, their_top, jnp.where(row == 1, their_total, 0.0))
        theirs = jnp.transpose(theirs)
        their_top, their_total = theirs[:, 0:1], theirs[:, 1:2]
        joint = jnp.maximum(top, their_top)
        mine_by, theirs_by = jnp.exp2(top - joint), jnp.exp2(their_top - joint)
        acc = acc * mine_by + other_ref[n, :BLK].astype(jnp.float32) * theirs_by
        stat = rows_of(joint, total * mine_by + their_total * theirs_by)
        rows = split_rows(stat[0:1]) + split_rows(stat[1:2]) + split_rows(pos_ref[start + n])
        rows.append(jnp.zeros((EXTRA - len(rows), 128), jnp.float32))
        tail = jnp.concatenate(rows, axis=0).astype(jnp.bfloat16)
        for d in range(TP):
            at = (TP - d) % TP * 128
            outs[d][n, :BLK] = acc[:, at : at + 128].astype(jnp.bfloat16)
            outs[d][n, BLK:] = tail


def attend(body, start, scalars, inputs, outs, name):
    vmem = pl.BlockSpec(memory_space=pltpu.VMEM)
    return pl.pallas_call(
        functools.partial(body, start),
        in_specs=[pl.BlockSpec(memory_space=pltpu.SMEM)] * len(scalars) + [vmem] * len(inputs),
        out_specs=(vmem,) * len(outs),
        out_shape=outs,
        scratch_shapes=[
            pltpu.VMEM((PART, COLS, E), jnp.bfloat16),
            pltpu.VMEM((PART, BLK, COLS), jnp.float32),
        ],
        compiler_params=pltpu.CompilerParams(vmem_limit_bytes=32 << 20),
        cost_estimate=pl.CostEstimate(
            flops=PART * 4 * BLK * COLS * E,
            bytes_accessed=2 << 20,
            transcendentals=PART * BLK * COLS,
        ),
        name=name,
    )(*scalars, *inputs)


def last_kernel(*refs):
    positive_ref, loss_ref, grad_ref = refs[8:]
    for block in range(2 * PART):
        parts = refs[0:4] if block < PART else refs[4:8]
        finish(parts, block % PART, block, positive_ref, loss_ref, grad_ref)


def finish(parts, n, block, positive_ref, loss_ref, grad_ref):
    here = pl.ds(block * BLK, BLK)
    tails = [ref[n, BLK:].astype(jnp.float32) for ref in parts]
    tops = [joined_row(tail[0:6]) for tail in tails]
    totals = [joined_row(tail[6:12]) for tail in tails]
    shares = [joined_row(tail[12:18]) for tail in tails]
    pos = (shares[0] + shares[1] + shares[2] + shares[3]) * LOG2E
    joint = pos
    for top in tops:
        joint = jnp.maximum(joint, top)
    total = jnp.exp2(pos - joint)
    for top, one in zip(tops, totals):
        total += one * jnp.exp2(top - joint)
    log_total = joint + jnp.log(total) * LOG2E
    loss_ref[block] = (log_total - pos) * LN2
    factors = [jnp.exp2(top - log_total) * SCALE for top in tops]
    factors.append((jnp.exp2(pos - log_total) - 1.0) * SCALE)
    row = lax.broadcasted_iota(jnp.int32, (128, BLK), 0)
    packed = jnp.zeros((128, BLK), jnp.float32)
    for at, factor in enumerate(factors):
        packed = jnp.where(row == at, factor, packed)
    by = jnp.transpose(packed)
    grad = by[:, 4:5] * positive_ref[here].astype(jnp.float32)
    for s in range(4):
        grad += by[:, s : s + 1] * parts[s][n, :BLK].astype(jnp.float32)
    grad_ref[here] = grad.astype(jnp.bfloat16)


def last(parts, positive):
    vmem = pl.BlockSpec(memory_space=pltpu.VMEM)
    blocks = positive.shape[0] // BLK
    return pl.pallas_call(
        last_kernel,
        in_specs=[vmem] * 9,
        out_specs=(vmem, vmem),
        out_shape=(
            jax.ShapeDtypeStruct((blocks, 1, BLK), jnp.float32),
            jax.ShapeDtypeStruct((blocks * BLK, 128), jnp.bfloat16),
        ),
        compiler_params=pltpu.CompilerParams(vmem_limit_bytes=16 << 20),
        name="last",
    )(*parts, positive)


STREAMS = (
    (("y", 1), ("y", 3), ("z", 1), ("z", 3)),
    (("y", 3), ("y", 1), ("z", 3), ("z", 1)),
    (("z", 1), ("z", 3), ("y", 1), ("y", 3)),
    (("z", 3), ("z", 1), ("y", 3), ("y", 1)),
)


def together(*values):
    return list(lax.optimization_barrier(tuple(values)))


def spread(items, query):
    held = [items[n * 4 : n * 4 + 4] for n in range(4)]
    query_1 = send_x(query, 1)
    for step in range(2):
        got = [send(h, **{st[step][0]: st[step][1]}) for h, st in zip(held, STREAMS)]
        held = [jnp.concatenate(together(h, g)) for h, g in zip(held, got)]
    held[3], query_1, query = together(held[3], query_1, query)
    third = [send(h, **{st[2][0]: st[2][1]}) for h, st in zip(held, STREAMS)]
    query_2 = send_x(query, 2)
    held, third = zip(*[together(h, t) for h, t in zip(held, third)])
    fourth = [send(h, **{st[3][0]: st[3][1]}) for h, st in zip(held, STREAMS)]
    held, third = list(held), list(third)
    third, fourth = zip(*[together(t, f) for t, f in zip(third, fourth)])
    third, fourth = list(third), list(fourth)
    query_2, query, fourth[0] = together(query_2, query, fourth[0])
    queries = [query, query_1, query_2, send_x(query, 3)]
    fifth = [send(h, **{st[3][0]: st[3][1]}) for h, st in zip(third, STREAMS)]
    table = pack(held + third, (0, 4, 8, 12, 1, 5, 9, 13))
    table = pack(fourth + fifth, (2, 6, 10, 14, 3, 7, 11, 15), table)
    return table, queries


def place_of(flipped, first):
    return jnp.where(
        flipped == 0, 0, jnp.where(flipped == 2, 3, jnp.where(flipped == first, 1, 2))
    )


def local(query_emb, positive_emb, item_hidden, item_weight, neg_blocks, block_home, sample_counts):
    rank = lax.axis_index("tp")
    place = lax.axis_index("cat")
    core, my_z, my_y = place % 2, (place // 2) % NZ, place // (2 * NZ)
    qblocks = neg_blocks.shape[0]
    total_blocks = block_home.shape[0]

    core_id = core.reshape(1).astype(jnp.int32)
    rank_id = rank.reshape(1).astype(jnp.int32)
    hidden = item_hidden.reshape(NBD, TP, 2, ROWS, -1)
    keep = lax.dynamic_index_in_dim(hidden, core, 2, keepdims=False)
    give = lax.dynamic_index_in_dim(hidden, 1 - core, 2, keepdims=False)
    half = lax.dynamic_slice_in_dim(item_weight, core * (HID // TP // 2), HID // TP // 2, 0)
    swapped = send(give, c=1)
    mine_w = [half] + [send_x(half, d) for d in (1, 2, 3)]
    both = jnp.concatenate([keep, swapped])

    def piece(d):
        cut = lax.dynamic_index_in_dim(both, (rank + d) % TP, 1, keepdims=False)
        return cut.reshape(2 * NBD * ROWS, -1)

    hiddens = [piece(0)] + [send_x(piece(d), d) for d in (1, 2, 3)]
    theirs_w = send(together(jnp.stack(mine_w), hiddens[1], hiddens[3])[0], c=1)
    picks = jnp.concatenate([send(neg_blocks, c=1), neg_blocks])
    both_query = jnp.stack([send(query_emb, c=1), query_emb])
    items, late_query, picks = together(
        tower(core_id, rank_id, hiddens, mine_w, theirs_w), both_query, picks
    )
    table, queries = spread(items, late_query)
    pos_part = SCALE * jnp.sum(
        query_emb.astype(jnp.float32) * positive_emb.astype(jnp.float32), axis=1
    ).reshape(qblocks, 1, BLK)

    matches = picks[:, :, None] == jnp.arange(total_blocks, dtype=jnp.int32)[None, None, :]
    home = jnp.sum(jnp.where(matches, block_home[None, None, :], 0), axis=2)
    slot, owner = home % NBD, home // NBD
    flip_z = ((owner // 2) % NZ) ^ my_z
    flip_y = (owner // (2 * NZ)) ^ my_y
    late = slot // (NBD // 2)
    at_y = place_of(flip_y, jnp.where(late == 0, 1, 3))
    at_z = place_of(flip_z, jnp.where(late == 0, 1, 3))
    near = owner % 2 == core
    rows = jnp.where(near, at_z * 4 + at_y, 128 // 4 + at_y * 4 + at_z)
    rows = (rows * 4 + late * 64 + slot % 4).astype(jnp.int32)
    count_rows = sample_counts.reshape(2 * total_blocks, 128)[home.reshape(-1) * 2 + rank // 2]
    counts = lax.dynamic_slice_in_dim(count_rows, (rank % 2 * 2 + core) * ROWS, ROWS, 1)
    lq = (jnp.log(counts.astype(jnp.float32)) * LOG2E).reshape(2 * qblocks, COLS)

    rows = rows.reshape(-1)
    table, pos_part, rows, lq = together(table, pos_part, rows, lq)

    raw = (jax.ShapeDtypeStruct((PART, BLK + TAIL, E), jnp.bfloat16),)
    share = jax.ShapeDtypeStruct((PART, BLK + EXTRA, 128), jnp.bfloat16)
    others = []
    for start in (0, PART):
        made = attend(
            first_kernel,
            start,
            (rows,),
            (*queries, lq, table),
            raw,
            "attend_other",
        )
        others.append([send(one, c=1) for one in made])
    parts = []
    for start, other in zip((0, PART), others):
        shares = attend(
            second_kernel,
            start,
            (rows,),
            (*queries, lq, table, *other, pos_part),
            (share,) * TP,
            "attend_own",
        )
        parts += [shares[0]] + [send_x(shares[d], d) for d in (1, 2, 3)]
    loss, grad = last(parts, positive_emb)
    return loss.reshape(-1), grad


def solution(mesh):
    placed = (
        P("cat", "tp"),
        P("cat", "tp"),
        P("cat", "tp"),
        P("tp", None),
        P("cat", None),
        P(),
        P(),
    )
    return jax.shard_map(
        local, mesh=mesh, in_specs=placed, out_specs=(P("cat"), P("cat", "tp")), check_vma=False
    )
```

```python
import functools
import math

import jax
import jax.numpy as jnp
from jax import lax
from jax.experimental import pallas as pl
from jax.experimental.pallas import tpu as pltpu
from jax.sharding import PartitionSpec as P

BLK = 256
TP = 4
NY = 4
NZ = 4
E = 512
LOG2E = math.log2(math.e)
LN2 = math.log(2.0)
SCALE = 2.0 / math.sqrt(E)
LOW = -1e30
ROWS = BLK // TP // 2
NBD = 8
PICKS = 64
COLS = PICKS * ROWS
TILE = 512
HID = 1024
TAIL = 16
EXTRA = 32


def cat_perm(flip_y, flip_z, flip_c):
    def at(y, z, c):
        return (y * NZ + z) * 2 + c

    return [
        (at(y, z, c), at(y ^ flip_y, z ^ flip_z, c ^ flip_c))
        for y in range(NY)
        for z in range(NZ)
        for c in range(2)
    ]


def send(value, y=0, z=0, c=0):
    return lax.ppermute(value, "cat", cat_perm(y, z, c))


def send_x(value, d):
    return lax.ppermute(value, "tp", [(i, (i + d) % TP) for i in range(TP)])


def tower_kernel(core_ref, rank_ref, *refs):
    hidden = refs[0:4]
    mine, theirs = refs[4:8], refs[8]
    out_ref, quarters = refs[9:]
    core = core_ref[0]
    half = HID // TP // 2
    acc = jnp.zeros((NBD * 2 * ROWS, E), jnp.float32)
    for d in range(TP):
        low = jnp.where(core == 0, mine[d][...], theirs[d])
        high = jnp.where(core == 0, theirs[d], mine[d][...])
        acc += jnp.dot(hidden[d][:, :half], low, preferred_element_type=jnp.float32)
        acc += jnp.dot(hidden[d][:, half:], high, preferred_element_type=jnp.float32)
    for s in range(TP):
        quarters[s] = acc[:, s * 128 : (s + 1) * 128].astype(jnp.bfloat16).reshape(quarters.shape[1:])
    for d in range(TP):
        out_ref[:, :, d * 128 : (d + 1) * 128] = quarters[lax.rem(rank_ref[0] + TP - d, TP)]


def tower(core, rank, hidden, mine, theirs):
    return pl.pallas_call(
        tower_kernel,
        out_shape=jax.ShapeDtypeStruct((2 * NBD, ROWS, E), jnp.bfloat16),
        in_specs=[pl.BlockSpec(memory_space=pltpu.SMEM)] * 2
        + [pl.BlockSpec(memory_space=pltpu.VMEM)] * 9,
        scratch_shapes=[pltpu.VMEM((TP, 2 * NBD, ROWS, 128), jnp.bfloat16)],
        out_specs=pl.BlockSpec(memory_space=pltpu.VMEM),
        compiler_params=pltpu.CompilerParams(vmem_limit_bytes=40 << 20),
        cost_estimate=pl.CostEstimate(
            flops=2 * 512 * 1024 * 512, bytes_accessed=3 << 20, transcendentals=0
        ),
        name="tower",
    )(core, rank, *hidden, *mine, theirs)


PART = 2


def one_block(block, side, q_refs, lq_ref, row_ref, table, picked, scores):
    base = side * 2 * PART
    for j in range(PICKS):
        picked[pl.ds(j * ROWS, ROWS), :] = table[row_ref[(base + block) * PICKS + j]]
    here = pl.ds(block * BLK, BLK)
    query = jnp.concatenate([q_refs[d][side, here] for d in range(TP)], axis=1)
    top = jnp.full((BLK, 128), LOW, jnp.float32)
    for n in range(COLS // TILE):
        cols = pl.ds(n * TILE, TILE)
        part = lax.dot_general(
            query,
            picked[cols, :],
            (((1,), (1,)), ((), ())),
            preferred_element_type=jnp.float32,
        )
        part = part * (SCALE * LOG2E) - lq_ref[pl.ds(base + block, 1), cols]
        scores[:, cols] = part
        for g in range(TILE // 128):
            top = jnp.maximum(top, part[:, g * 128 : (g + 1) * 128])
    top = jnp.max(top, axis=1, keepdims=True)
    total = jnp.zeros((BLK, 128), jnp.float32)
    acc = jnp.zeros((BLK, E), jnp.float32)
    for n in range(COLS // TILE):
        cols = pl.ds(n * TILE, TILE)
        weight = jnp.exp2(scores[:, cols] - top)
        for g in range(TILE // 128):
            total += weight[:, g * 128 : (g + 1) * 128]
        acc += jnp.dot(
            weight.astype(jnp.bfloat16), picked[cols, :], preferred_element_type=jnp.float32
        )
    return top, jnp.sum(total, axis=1, keepdims=True), acc


def rows_of(top, total):
    lane = lax.broadcasted_iota(jnp.int32, (BLK, 128), 1)
    both = jnp.where(lane == 0, top, jnp.where(lane == 1, total, 0.0))
    return jnp.transpose(both)[:8]


def pack_kernel(places, *refs):
    count = len(places)
    pieces, table, sems = refs[:count], refs[-2], refs[-1]
    copies = [
        pltpu.make_async_copy(piece, table.at[pl.ds(place * 16, 16)], sems.at[n])
        for n, (piece, place) in enumerate(zip(pieces, places))
    ]
    for copy in copies:
        copy.start()
    for copy in copies:
        copy.wait()


def pack(pieces, places, table=None):
    given = () if table is None else (table,)
    vmem = pl.BlockSpec(memory_space=pltpu.VMEM)
    return pl.pallas_call(
        functools.partial(pack_kernel, places),
        out_shape=jax.ShapeDtypeStruct((256, ROWS, E), jnp.bfloat16),
        in_specs=[pl.BlockSpec(memory_space=pl.ANY)] * len(pieces) + [vmem] * len(given),
        out_specs=vmem,
        scratch_shapes=[pltpu.SemaphoreType.DMA((len(pieces),))],
        input_output_aliases={len(pieces): 0} if given else {},
        compiler_params=pltpu.CompilerParams(vmem_limit_bytes=20 << 20),
        cost_estimate=pl.CostEstimate(flops=0, bytes_accessed=8 << 20, transcendentals=0),
        name="pack",
    )(*pieces, *given)


def first_kernel(start, row_ref, *refs):
    q_refs, (lq_ref, table) = refs[:TP], refs[TP : TP + 2]
    out_ref, picked, scores = refs[TP + 2 :]

    for n in range(PART):
        top, total, acc = one_block(
            start + n, 0, q_refs, lq_ref, row_ref, table,
            picked.at[n], scores.at[n],
        )
        stat = rows_of(top, total)
        parts = parts_of(stat[0:1]) + parts_of(stat[1:2])
        rows = [jnp.concatenate(parts[at : at + 2], axis=1) for at in (0, 2, 4)]
        rows.append(jnp.zeros((TAIL - 3, E), jnp.float32))
        out_ref[n, :BLK] = acc.astype(jnp.bfloat16)
        out_ref[n, BLK:] = jnp.concatenate(rows, axis=0).astype(jnp.bfloat16)


def parts_of(row):
    out = []
    for _ in range(3):
        part = row.astype(jnp.bfloat16).astype(jnp.float32)
        out.append(part)
        row = row - part
    return out


def split_rows(row):
    return [part[:, at : at + 128] for part in parts_of(row) for at in (0, 128)]


def joined_row(rows):
    halves = [rows[n : n + 1] + (rows[n + 2 : n + 3] + rows[n + 4 : n + 5]) for n in range(2)]
    return jnp.concatenate(halves, axis=1)


def second_kernel(start, row_ref, *refs):
    q_refs, (lq_ref, table), refs = refs[:TP], refs[TP : TP + 2], refs[TP + 2 :]
    other_ref, pos_ref = refs[:2]
    outs = refs[2:6]
    picked, scores = refs[6:]

    for n in range(PART):
        top, total, acc = one_block(
            start + n, 1, q_refs, lq_ref, row_ref, table,
            picked.at[n], scores.at[n],
        )
        tail = other_ref[n, BLK:].astype(jnp.float32)
        left, right = tail[:, :BLK], tail[:, BLK:]
        row = lax.broadcasted_iota(jnp.int32, (128, BLK), 0)
        their_top = left[0:1] + (right[0:1] + left[1:2])
        their_total = right[1:2] + (left[2:3] + right[2:3])
        theirs = jnp.where(row == 0, their_top, jnp.where(row == 1, their_total, 0.0))
        theirs = jnp.transpose(theirs)
        their_top, their_total = theirs[:, 0:1], theirs[:, 1:2]
        joint = jnp.maximum(top, their_top)
        mine_by, theirs_by = jnp.exp2(top - joint), jnp.exp2(their_top - joint)
        acc = acc * mine_by + other_ref[n, :BLK].astype(jnp.float32) * theirs_by
        stat = rows_of(joint, total * mine_by + their_total * theirs_by)
        rows = split_rows(stat[0:1]) + split_rows(stat[1:2]) + split_rows(pos_ref[start + n])
        rows.append(jnp.zeros((EXTRA - len(rows), 128), jnp.float32))
        tail = jnp.concatenate(rows, axis=0).astype(jnp.bfloat16)
        for d in range(TP):
            at = (TP - d) % TP * 128
            outs[d][n, :BLK] = acc[:, at : at + 128].astype(jnp.bfloat16)
            outs[d][n, BLK:] = tail


def attend(body, start, scalars, inputs, outs, name):
    vmem = pl.BlockSpec(memory_space=pltpu.VMEM)
    return pl.pallas_call(
        functools.partial(body, start),
        in_specs=[pl.BlockSpec(memory_space=pltpu.SMEM)] * len(scalars) + [vmem] * len(inputs),
        out_specs=(vmem,) * len(outs),
        out_shape=outs,
        scratch_shapes=[
            pltpu.VMEM((PART, COLS, E), jnp.bfloat16),
            pltpu.VMEM((PART, BLK, COLS), jnp.float32),
        ],
        compiler_params=pltpu.CompilerParams(vmem_limit_bytes=32 << 20),
        cost_estimate=pl.CostEstimate(
            flops=PART * 4 * BLK * COLS * E,
            bytes_accessed=2 << 20,
            transcendentals=PART * BLK * COLS,
        ),
        name=name,
    )(*scalars, *inputs)


def last_kernel(*refs):
    positive_ref, loss_ref, grad_ref = refs[8:]
    for block in range(2 * PART):
        parts = refs[0:4] if block < PART else refs[4:8]
        finish(parts, block % PART, block, positive_ref, loss_ref, grad_ref)


def finish(parts, n, block, positive_ref, loss_ref, grad_ref):
    here = pl.ds(block * BLK, BLK)
    tails = [ref[n, BLK:].astype(jnp.float32) for ref in parts]
    tops = [joined_row(tail[0:6]) for tail in tails]
    totals = [joined_row(tail[6:12]) for tail in tails]
    shares = [joined_row(tail[12:18]) for tail in tails]
    pos = (shares[0] + shares[1] + shares[2] + shares[3]) * LOG2E
    joint = pos
    for top in tops:
        joint = jnp.maximum(joint, top)
    total = jnp.exp2(pos - joint)
    for top, one in zip(tops, totals):
        total += one * jnp.exp2(top - joint)
    log_total = joint + jnp.log(total) * LOG2E
    loss_ref[block] = (log_total - pos) * LN2
    factors = [jnp.exp2(top - log_total) * SCALE for top in tops]
    factors.append((jnp.exp2(pos - log_total) - 1.0) * SCALE)
    row = lax.broadcasted_iota(jnp.int32, (128, BLK), 0)
    packed = jnp.zeros((128, BLK), jnp.float32)
    for at, factor in enumerate(factors):
        packed = jnp.where(row == at, factor, packed)
    by = jnp.transpose(packed)
    grad = by[:, 4:5] * positive_ref[here].astype(jnp.float32)
    for s in range(4):
        grad += by[:, s : s + 1] * parts[s][n, :BLK].astype(jnp.float32)
    grad_ref[here] = grad.astype(jnp.bfloat16)


def last(parts, positive):
    vmem = pl.BlockSpec(memory_space=pltpu.VMEM)
    blocks = positive.shape[0] // BLK
    return pl.pallas_call(
        last_kernel,
        in_specs=[vmem] * 9,
        out_specs=(vmem, vmem),
        out_shape=(
            jax.ShapeDtypeStruct((blocks, 1, BLK), jnp.float32),
            jax.ShapeDtypeStruct((blocks * BLK, 128), jnp.bfloat16),
        ),
        compiler_params=pltpu.CompilerParams(vmem_limit_bytes=16 << 20),
        name="last",
    )(*parts, positive)


STREAMS = (
    (("y", 1), ("y", 3), ("z", 1), ("z", 3)),
    (("y", 3), ("y", 1), ("z", 3), ("z", 1)),
    (("z", 1), ("z", 3), ("y", 1), ("y", 3)),
    (("z", 3), ("z", 1), ("y", 3), ("y", 1)),
)


def together(*values):
    return list(lax.optimization_barrier(tuple(values)))


def spread(items, query):
    held = [items[n * 4 : n * 4 + 4] for n in range(4)]
    query_1 = send_x(query, 1)
    for step in range(2):
        got = [send(h, **{st[step][0]: st[step][1]}) for h, st in zip(held, STREAMS)]
        held = [jnp.concatenate(together(h, g)) for h, g in zip(held, got)]
    held[3], query_1, query = together(held[3], query_1, query)
    third = [send(h, **{st[2][0]: st[2][1]}) for h, st in zip(held, STREAMS)]
    query_2 = send_x(query, 2)
    held, third = zip(*[together(h, t) for h, t in zip(held, third)])
    fourth = [send(h, **{st[3][0]: st[3][1]}) for h, st in zip(held, STREAMS)]
    held, third = list(held), list(third)
    third, fourth = zip(*[together(t, f) for t, f in zip(third, fourth)])
    third, fourth = list(third), list(fourth)
    query_2, query, *fourth = together(query_2, query, *fourth)
    queries = [query, query_1, query_2, send_x(query, 3)]
    fifth = [send(h, **{st[3][0]: st[3][1]}) for h, st in zip(third, STREAMS)]
    table = pack(held + third, (0, 4, 8, 12, 1, 5, 9, 13))
    table = pack(fourth + fifth, (2, 6, 10, 14, 3, 7, 11, 15), table)
    return table, queries


def place_of(flipped, first):
    return jnp.where(
        flipped == 0, 0, jnp.where(flipped == 2, 3, jnp.where(flipped == first, 1, 2))
    )


def local(query_emb, positive_emb, item_hidden, item_weight, neg_blocks, block_home, sample_counts):
    rank = lax.axis_index("tp")
    place = lax.axis_index("cat")
    core, my_z, my_y = place % 2, (place // 2) % NZ, place // (2 * NZ)
    qblocks = neg_blocks.shape[0]
    total_blocks = block_home.shape[0]

    core_id = core.reshape(1).astype(jnp.int32)
    rank_id = rank.reshape(1).astype(jnp.int32)
    hidden = item_hidden.reshape(NBD, TP, 2, ROWS, -1)
    keep = lax.dynamic_index_in_dim(hidden, core, 2, keepdims=False)
    give = lax.dynamic_index_in_dim(hidden, 1 - core, 2, keepdims=False)
    half = lax.dynamic_slice_in_dim(item_weight, core * (HID // TP // 2), HID // TP // 2, 0)
    swapped = send(give, c=1)
    mine_w = [half] + [send_x(half, d) for d in (1, 2, 3)]
    both = jnp.concatenate([keep, swapped])

    def piece(d):
        cut = lax.dynamic_index_in_dim(both, (rank + d) % TP, 1, keepdims=False)
        return cut.reshape(2 * NBD * ROWS, -1)

    hiddens = [piece(0)] + [send_x(piece(d), d) for d in (1, 2, 3)]
    theirs_w = send(together(jnp.stack(mine_w), hiddens[1], hiddens[3])[0], c=1)
    picks = jnp.concatenate([send(neg_blocks, c=1), neg_blocks])
    both_query = jnp.stack([send(query_emb, c=1), query_emb])
    items, late_query, picks = together(
        tower(core_id, rank_id, hiddens, mine_w, theirs_w), both_query, picks
    )
    table, queries = spread(items, late_query)
    pos_part = SCALE * jnp.sum(
        query_emb.astype(jnp.float32) * positive_emb.astype(jnp.float32), axis=1
    ).reshape(qblocks, 1, BLK)

    matches = picks[:, :, None] == jnp.arange(total_blocks, dtype=jnp.int32)[None, None, :]
    home = jnp.sum(jnp.where(matches, block_home[None, None, :], 0), axis=2)
    slot, owner = home % NBD, home // NBD
    flip_z = ((owner // 2) % NZ) ^ my_z
    flip_y = (owner // (2 * NZ)) ^ my_y
    late = slot // (NBD // 2)
    at_y = place_of(flip_y, jnp.where(late == 0, 1, 3))
    at_z = place_of(flip_z, jnp.where(late == 0, 1, 3))
    near = owner % 2 == core
    rows = jnp.where(near, at_z * 4 + at_y, 128 // 4 + at_y * 4 + at_z)
    rows = (rows * 4 + late * 64 + slot % 4).astype(jnp.int32)
    count_rows = sample_counts.reshape(2 * total_blocks, 128)[home.reshape(-1) * 2 + rank // 2]
    counts = lax.dynamic_slice_in_dim(count_rows, (rank % 2 * 2 + core) * ROWS, ROWS, 1)
    lq = (jnp.log(counts.astype(jnp.float32)) * LOG2E).reshape(2 * qblocks, COLS)

    rows = rows.reshape(-1)
    table, pos_part, rows, lq = together(table, pos_part, rows, lq)

    raw = (jax.ShapeDtypeStruct((PART, BLK + TAIL, E), jnp.bfloat16),)
    share = jax.ShapeDtypeStruct((PART, BLK + EXTRA, 128), jnp.bfloat16)
    others = []
    for start in (0, PART):
        made = attend(
            first_kernel,
            start,
            (rows,),
            (*queries, lq, table),
            raw,
            "attend_other",
        )
        others.append([send(one, c=1) for one in made])
    parts = []
    for start, other in zip((0, PART), others):
        shares = attend(
            second_kernel,
            start,
            (rows,),
            (*queries, lq, table, *other, pos_part),
            (share,) * TP,
            "attend_own",
        )
        parts += [shares[0]] + [send_x(shares[d], d) for d in (1, 2, 3)]
    loss, grad = last(parts, positive_emb)
    return loss.reshape(-1), grad


def solution(mesh):
    placed = (
        P("cat", "tp"),
        P("cat", "tp"),
        P("cat", "tp"),
        P("tp", None),
        P("cat", None),
        P(),
        P(),
    )
    return jax.shard_map(
        local, mesh=mesh, in_specs=placed, out_specs=(P("cat"), P("cat", "tp")), check_vma=False
    )
```

```python
import functools
import math

import jax
import jax.numpy as jnp
from jax import lax
from jax.experimental import pallas as pl
from jax.experimental.pallas import tpu as pltpu
from jax.sharding import PartitionSpec as P

BLK = 256
TP = 4
NY = 4
NZ = 4
E = 512
LOG2E = math.log2(math.e)
LN2 = math.log(2.0)
SCALE = 2.0 / math.sqrt(E)
LOW = -1e30
ROWS = BLK // TP // 2
NBD = 8
PICKS = 64
COLS = PICKS * ROWS
TILE = 512
HID = 1024
TAIL = 16
EXTRA = 32


def cat_perm(flip_y, flip_z, flip_c):
    def at(y, z, c):
        return (y * NZ + z) * 2 + c

    return [
        (at(y, z, c), at(y ^ flip_y, z ^ flip_z, c ^ flip_c))
        for y in range(NY)
        for z in range(NZ)
        for c in range(2)
    ]


def send(value, y=0, z=0, c=0):
    return lax.ppermute(value, "cat", cat_perm(y, z, c))


def send_x(value, d):
    return lax.ppermute(value, "tp", [(i, (i + d) % TP) for i in range(TP)])


def tower_kernel(core_ref, rank_ref, *refs):
    hidden = refs[0:4]
    mine, theirs = refs[4:8], refs[8]
    out_ref, quarters = refs[9:]
    core = core_ref[0]
    half = HID // TP // 2
    acc = jnp.zeros((NBD * 2 * ROWS, E), jnp.float32)
    for d in range(TP):
        low = jnp.where(core == 0, mine[d][...], theirs[d])
        high = jnp.where(core == 0, theirs[d], mine[d][...])
        acc += jnp.dot(hidden[d][:, :half], low, preferred_element_type=jnp.float32)
        acc += jnp.dot(hidden[d][:, half:], high, preferred_element_type=jnp.float32)
    for s in range(TP):
        quarters[s] = acc[:, s * 128 : (s + 1) * 128].astype(jnp.bfloat16).reshape(quarters.shape[1:])
    for d in range(TP):
        out_ref[:, :, d * 128 : (d + 1) * 128] = quarters[lax.rem(rank_ref[0] + TP - d, TP)]


def tower(core, rank, hidden, mine, theirs):
    return pl.pallas_call(
        tower_kernel,
        out_shape=jax.ShapeDtypeStruct((2 * NBD, ROWS, E), jnp.bfloat16),
        in_specs=[pl.BlockSpec(memory_space=pltpu.SMEM)] * 2
        + [pl.BlockSpec(memory_space=pltpu.VMEM)] * 9,
        scratch_shapes=[pltpu.VMEM((TP, 2 * NBD, ROWS, 128), jnp.bfloat16)],
        out_specs=pl.BlockSpec(memory_space=pltpu.VMEM),
        compiler_params=pltpu.CompilerParams(vmem_limit_bytes=40 << 20),
        cost_estimate=pl.CostEstimate(
            flops=2 * 512 * 1024 * 512, bytes_accessed=3 << 20, transcendentals=0
        ),
        name="tower",
    )(core, rank, *hidden, *mine, theirs)


PART = 2


def one_block(block, side, q_refs, lq_ref, row_ref, table, picked, scores):
    base = side * 2 * PART
    for j in range(PICKS):
        picked[pl.ds(j * ROWS, ROWS), :] = table[row_ref[(base + block) * PICKS + j]]
    here = pl.ds(block * BLK, BLK)
    query = jnp.concatenate([q_refs[d][side, here] for d in range(TP)], axis=1)
    top = jnp.full((BLK, 128), LOW, jnp.float32)
    for n in range(COLS // TILE):
        cols = pl.ds(n * TILE, TILE)
        part = lax.dot_general(
            query,
            picked[cols, :],
            (((1,), (1,)), ((), ())),
            preferred_element_type=jnp.float32,
        )
        part = part * (SCALE * LOG2E) - lq_ref[pl.ds(base + block, 1), cols]
        scores[:, cols] = part
        for g in range(TILE // 128):
            top = jnp.maximum(top, part[:, g * 128 : (g + 1) * 128])
    top = jnp.max(top, axis=1, keepdims=True)
    total = jnp.zeros((BLK, 128), jnp.float32)
    acc = jnp.zeros((BLK, E), jnp.float32)
    for n in range(COLS // TILE):
        cols = pl.ds(n * TILE, TILE)
        weight = jnp.exp2(scores[:, cols] - top)
        for g in range(TILE // 128):
            total += weight[:, g * 128 : (g + 1) * 128]
        acc += jnp.dot(
            weight.astype(jnp.bfloat16), picked[cols, :], preferred_element_type=jnp.float32
        )
    return top, jnp.sum(total, axis=1, keepdims=True), acc


def rows_of(top, total):
    lane = lax.broadcasted_iota(jnp.int32, (BLK, 128), 1)
    both = jnp.where(lane == 0, top, jnp.where(lane == 1, total, 0.0))
    return jnp.transpose(both)[:8]


def pack_kernel(places, *refs):
    count = len(places)
    pieces, table, sems = refs[:count], refs[-2], refs[-1]
    copies = [
        pltpu.make_async_copy(piece, table.at[pl.ds(place * 16, 16)], sems.at[n])
        for n, (piece, place) in enumerate(zip(pieces, places))
    ]
    for copy in copies:
        copy.start()
    for copy in copies:
        copy.wait()


def pack(pieces, places, table=None):
    given = () if table is None else (table,)
    vmem = pl.BlockSpec(memory_space=pltpu.VMEM)
    return pl.pallas_call(
        functools.partial(pack_kernel, places),
        out_shape=jax.ShapeDtypeStruct((256, ROWS, E), jnp.bfloat16),
        in_specs=[pl.BlockSpec(memory_space=pl.ANY)] * len(pieces) + [vmem] * len(given),
        out_specs=vmem,
        scratch_shapes=[pltpu.SemaphoreType.DMA((len(pieces),))],
        input_output_aliases={len(pieces): 0} if given else {},
        compiler_params=pltpu.CompilerParams(vmem_limit_bytes=20 << 20),
        cost_estimate=pl.CostEstimate(flops=0, bytes_accessed=8 << 20, transcendentals=0),
        name="pack",
    )(*pieces, *given)


def first_kernel(start, row_ref, *refs):
    q_refs, (lq_ref, table) = refs[:TP], refs[TP : TP + 2]
    out_ref, picked, scores = refs[TP + 2 :]

    for n in range(PART):
        top, total, acc = one_block(
            start + n, 0, q_refs, lq_ref, row_ref, table,
            picked.at[n], scores.at[n],
        )
        stat = rows_of(top, total)
        parts = parts_of(stat[0:1]) + parts_of(stat[1:2])
        rows = [jnp.concatenate(parts[at : at + 2], axis=1) for at in (0, 2, 4)]
        rows.append(jnp.zeros((TAIL - 3, E), jnp.float32))
        out_ref[n, :BLK] = acc.astype(jnp.bfloat16)
        out_ref[n, BLK:] = jnp.concatenate(rows, axis=0).astype(jnp.bfloat16)


def parts_of(row):
    out = []
    for _ in range(3):
        part = row.astype(jnp.bfloat16).astype(jnp.float32)
        out.append(part)
        row = row - part
    return out


def split_rows(row):
    return [part[:, at : at + 128] for part in parts_of(row) for at in (0, 128)]


def joined_row(rows):
    halves = [rows[n : n + 1] + (rows[n + 2 : n + 3] + rows[n + 4 : n + 5]) for n in range(2)]
    return jnp.concatenate(halves, axis=1)


def second_kernel(start, row_ref, *refs):
    q_refs, (lq_ref, table), refs = refs[:TP], refs[TP : TP + 2], refs[TP + 2 :]
    other_ref, pos_ref = refs[:2]
    outs = refs[2:6]
    picked, scores = refs[6:]

    for n in range(PART):
        top, total, acc = one_block(
            start + n, 1, q_refs, lq_ref, row_ref, table,
            picked.at[n], scores.at[n],
        )
        tail = other_ref[n, BLK:].astype(jnp.float32)
        left, right = tail[:, :BLK], tail[:, BLK:]
        row = lax.broadcasted_iota(jnp.int32, (128, BLK), 0)
        their_top = left[0:1] + (right[0:1] + left[1:2])
        their_total = right[1:2] + (left[2:3] + right[2:3])
        theirs = jnp.where(row == 0, their_top, jnp.where(row == 1, their_total, 0.0))
        theirs = jnp.transpose(theirs)
        their_top, their_total = theirs[:, 0:1], theirs[:, 1:2]
        joint = jnp.maximum(top, their_top)
        mine_by, theirs_by = jnp.exp2(top - joint), jnp.exp2(their_top - joint)
        acc = acc * mine_by + other_ref[n, :BLK].astype(jnp.float32) * theirs_by
        stat = rows_of(joint, total * mine_by + their_total * theirs_by)
        rows = split_rows(stat[0:1]) + split_rows(stat[1:2]) + split_rows(pos_ref[start + n])
        rows.append(jnp.zeros((EXTRA - len(rows), 128), jnp.float32))
        tail = jnp.concatenate(rows, axis=0).astype(jnp.bfloat16)
        for d in range(TP):
            at = (TP - d) % TP * 128
            outs[d][n, :BLK] = acc[:, at : at + 128].astype(jnp.bfloat16)
            outs[d][n, BLK:] = tail


def attend(body, start, scalars, inputs, outs, name):
    vmem = pl.BlockSpec(memory_space=pltpu.VMEM)
    return pl.pallas_call(
        functools.partial(body, start),
        in_specs=[pl.BlockSpec(memory_space=pltpu.SMEM)] * len(scalars) + [vmem] * len(inputs),
        out_specs=(vmem,) * len(outs),
        out_shape=outs,
        scratch_shapes=[
            pltpu.VMEM((PART, COLS, E), jnp.bfloat16),
            pltpu.VMEM((PART, BLK, COLS), jnp.float32),
        ],
        compiler_params=pltpu.CompilerParams(vmem_limit_bytes=32 << 20),
        cost_estimate=pl.CostEstimate(
            flops=PART * 4 * BLK * COLS * E,
            bytes_accessed=2 << 20,
            transcendentals=PART * BLK * COLS,
        ),
        name=name,
    )(*scalars, *inputs)


def last_kernel(*refs):
    positive_ref, loss_ref, grad_ref = refs[8:]
    for block in range(2 * PART):
        parts = refs[0:4] if block < PART else refs[4:8]
        finish(parts, block % PART, block, positive_ref, loss_ref, grad_ref)


def finish(parts, n, block, positive_ref, loss_ref, grad_ref):
    here = pl.ds(block * BLK, BLK)
    tails = [ref[n, BLK:].astype(jnp.float32) for ref in parts]
    tops = [joined_row(tail[0:6]) for tail in tails]
    totals = [joined_row(tail[6:12]) for tail in tails]
    shares = [joined_row(tail[12:18]) for tail in tails]
    pos = (shares[0] + shares[1] + shares[2] + shares[3]) * LOG2E
    joint = pos
    for top in tops:
        joint = jnp.maximum(joint, top)
    total = jnp.exp2(pos - joint)
    for top, one in zip(tops, totals):
        total += one * jnp.exp2(top - joint)
    log_total = joint + jnp.log(total) * LOG2E
    loss_ref[block] = (log_total - pos) * LN2
    factors = [jnp.exp2(top - log_total) * SCALE for top in tops]
    factors.append((jnp.exp2(pos - log_total) - 1.0) * SCALE)
    row = lax.broadcasted_iota(jnp.int32, (128, BLK), 0)
    packed = jnp.zeros((128, BLK), jnp.float32)
    for at, factor in enumerate(factors):
        packed = jnp.where(row == at, factor, packed)
    by = jnp.transpose(packed)
    grad = by[:, 4:5] * positive_ref[here].astype(jnp.float32)
    for s in range(4):
        grad += by[:, s : s + 1] * parts[s][n, :BLK].astype(jnp.float32)
    grad_ref[here] = grad.astype(jnp.bfloat16)


def last(parts, positive):
    vmem = pl.BlockSpec(memory_space=pltpu.VMEM)
    blocks = positive.shape[0] // BLK
    return pl.pallas_call(
        last_kernel,
        in_specs=[vmem] * 9,
        out_specs=(vmem, vmem),
        out_shape=(
            jax.ShapeDtypeStruct((blocks, 1, BLK), jnp.float32),
            jax.ShapeDtypeStruct((blocks * BLK, 128), jnp.bfloat16),
        ),
        compiler_params=pltpu.CompilerParams(vmem_limit_bytes=16 << 20),
        name="last",
    )(*parts, positive)


STREAMS = (
    (("y", 1), ("y", 3), ("z", 1), ("z", 3)),
    (("y", 3), ("y", 1), ("z", 3), ("z", 1)),
    (("z", 1), ("z", 3), ("y", 1), ("y", 3)),
    (("z", 3), ("z", 1), ("y", 3), ("y", 1)),
)


def together(*values):
    return list(lax.optimization_barrier(tuple(values)))


def spread(items, query, lq):
    held = [items[n * 4 : n * 4 + 4] for n in range(4)]
    got = [send(h, **{st[0][0]: st[0][1]}) for h, st in zip(held, STREAMS)]
    query_1 = send_x(query, 1)
    got = together(*got)
    held = together(*[jnp.concatenate([h, g]) for h, g in zip(held, got)])
    got = [send(h, **{st[1][0]: st[1][1]}) for h, st in zip(held, STREAMS)]
    *got, query_1, query = together(*got, query_1, query)
    held = together(*[jnp.concatenate([h, g]) for h, g in zip(held, got)])
    third = [send(h, **{st[2][0]: st[2][1]}) for h, st in zip(held, STREAMS)]
    query_2 = send_x(query, 2)
    held, third = zip(*[together(h, t) for h, t in zip(held, third)])
    fourth = [send(h, **{st[3][0]: st[3][1]}) for h, st in zip(held, STREAMS)]
    held, third = list(held), list(third)
    third, fourth = zip(*[together(t, f) for t, f in zip(third, fourth)])
    third, fourth = list(third), list(fourth)
    query_2, query, fourth[0], lq = together(query_2, query, fourth[0], lq)
    queries = [query, query_1, query_2, send_x(query, 3)]
    fifth = [send(h, **{st[3][0]: st[3][1]}) for h, st in zip(third, STREAMS)]
    table = pack(held + third, (0, 4, 8, 12, 1, 5, 9, 13))
    table = pack(fourth + fifth, (2, 6, 10, 14, 3, 7, 11, 15), table)
    return table, queries, lq


def place_of(flipped, first):
    return jnp.where(
        flipped == 0, 0, jnp.where(flipped == 2, 3, jnp.where(flipped == first, 1, 2))
    )


def local(query_emb, positive_emb, item_hidden, item_weight, neg_blocks, block_home, sample_counts):
    rank = lax.axis_index("tp")
    place = lax.axis_index("cat")
    core, my_z, my_y = place % 2, (place // 2) % NZ, place // (2 * NZ)
    qblocks = neg_blocks.shape[0]
    total_blocks = block_home.shape[0]

    core_id = core.reshape(1).astype(jnp.int32)
    rank_id = rank.reshape(1).astype(jnp.int32)
    hidden = item_hidden.reshape(NBD, TP, 2, ROWS, -1)
    keep = lax.dynamic_index_in_dim(hidden, core, 2, keepdims=False)
    give = lax.dynamic_index_in_dim(hidden, 1 - core, 2, keepdims=False)
    half = lax.dynamic_slice_in_dim(item_weight, core * (HID // TP // 2), HID // TP // 2, 0)
    swapped = send(give, c=1)
    mine_w = [half] + [send_x(half, d) for d in (1, 2, 3)]
    both = jnp.concatenate([keep, swapped])

    def piece(d):
        cut = lax.dynamic_index_in_dim(both, (rank + d) % TP, 1, keepdims=False)
        return cut.reshape(2 * NBD * ROWS, -1)

    hiddens = [piece(0)] + [send_x(piece(d), d) for d in (1, 2, 3)]
    theirs_w = send(together(jnp.stack(mine_w), hiddens[1], hiddens[3])[0], c=1)
    picks = jnp.concatenate([send(neg_blocks, c=1), neg_blocks])
    both_query = jnp.stack([send(query_emb, c=1), query_emb])
    items, late_query, picks = together(
        tower(core_id, rank_id, hiddens, mine_w, theirs_w), both_query, picks
    )
    pos_part = SCALE * jnp.sum(
        query_emb.astype(jnp.float32) * positive_emb.astype(jnp.float32), axis=1
    ).reshape(qblocks, 1, BLK)

    matches = picks[:, :, None] == jnp.arange(total_blocks, dtype=jnp.int32)[None, None, :]
    home = jnp.sum(jnp.where(matches, block_home[None, None, :], 0), axis=2)
    slot, owner = home % NBD, home // NBD
    flip_z = ((owner // 2) % NZ) ^ my_z
    flip_y = (owner // (2 * NZ)) ^ my_y
    late = slot // (NBD // 2)
    at_y = place_of(flip_y, jnp.where(late == 0, 1, 3))
    at_z = place_of(flip_z, jnp.where(late == 0, 1, 3))
    near = owner % 2 == core
    rows = jnp.where(near, at_z * 4 + at_y, 128 // 4 + at_y * 4 + at_z)
    rows = (rows * 4 + late * 64 + slot % 4).astype(jnp.int32)
    count_rows = sample_counts.reshape(2 * total_blocks, 128)[home.reshape(-1) * 2 + rank // 2]
    counts = lax.dynamic_slice_in_dim(count_rows, (rank % 2 * 2 + core) * ROWS, ROWS, 1)
    lq = (jnp.log(counts.astype(jnp.float32)) * LOG2E).reshape(2 * qblocks, COLS)

    table, queries, lq = spread(items, late_query, lq)
    rows = rows.reshape(-1)
    table, pos_part, rows, lq = together(table, pos_part, rows, lq)

    raw = (jax.ShapeDtypeStruct((PART, BLK + TAIL, E), jnp.bfloat16),)
    share = jax.ShapeDtypeStruct((PART, BLK + EXTRA, 128), jnp.bfloat16)
    others = []
    for start in (0, PART):
        made = attend(
            first_kernel,
            start,
            (rows,),
            (*queries, lq, table),
            raw,
            "attend_other",
        )
        others.append([send(one, c=1) for one in made])
    parts = []
    for start, other in zip((0, PART), others):
        shares = attend(
            second_kernel,
            start,
            (rows,),
            (*queries, lq, table, *other, pos_part),
            (share,) * TP,
            "attend_own",
        )
        parts += [shares[0]] + [send_x(shares[d], d) for d in (1, 2, 3)]
    loss, grad = last(parts, positive_emb)
    return loss.reshape(-1), grad


def solution(mesh):
    placed = (
        P("cat", "tp"),
        P("cat", "tp"),
        P("cat", "tp"),
        P("tp", None),
        P("cat", None),
        P(),
        P(),
    )
    return jax.shard_map(
        local, mesh=mesh, in_specs=placed, out_specs=(P("cat"), P("cat", "tp")), check_vma=False
    )
```
